128 devices in a mesh: tensor: 8 (over z_lo, y), dp: 16 (over x, z_hi, core).
Axes of the slice: x: 4, y: 4, z: 4 (z_hi: 2, z_lo: 2; z = z_hi * 2 + z_lo), core: 2. Of those that a mesh axis runs over, the one named last changes fastest.
Arguments:
- tokens: bfloat16 [2048, 1024], P('dp'), may hold values from -6 to 6
- segment_ids: int32 [2048], replicated, may hold values from 0 to 2, as said below
- norm_gain: bfloat16 [2, 2, 1024], replicated, may hold values from 0.25 to 1.75
- norm_bias: bfloat16 [2, 2, 1024], replicated, may hold values from -1.5 to 1.5
- w_qkv: bfloat16 [2, 1024, 3, 1024], P(None, None, None, 'tensor'), may hold values from -0.1875 to 0.1875
- b_qv: bfloat16 [2, 2, 1024], P(None, None, 'tensor'), may hold values from -1.5 to 1.5
- w_out: bfloat16 [2, 1024, 1024], P(None, 'tensor'), may hold values from -2 to 2
- b_out: bfloat16 [2, 1024], replicated, may hold values from -1.5 to 1.5
- w_fc: bfloat16 [2, 1024, 4096], P(None, None, 'tensor'), may hold values from -0.1875 to 0.1875
- b_fc: bfloat16 [2, 4096], P(None, 'tensor'), may hold values from -2.5 to 2.5
- w_proj: bfloat16 [2, 4096, 1024], P(None, 'tensor'), may hold values from -0.09375 to 0.09375
- b_proj: bfloat16 [2, 1024], replicated, may hold values from -1.5 to 1.5
- cotangent: bfloat16 [2048, 1024], P('dp'), may hold values from -6 to 6
Outputs:
- out: float32 [2048, 1024], P('dp')
- grad_input: float32 [2048, 1024], P('dp')
- g_norm_gain: float32 [2, 2, 1024], replicated
- g_norm_bias: float32 [2, 2, 1024], replicated
- g_w_qkv: float32 [2, 1024, 3, 1024], P(None, None, None, 'tensor')
- g_b_qv: float32 [2, 2, 1024], P(None, None, 'tensor')
- g_w_out: float32 [2, 1024, 1024], P(None, 'tensor')
- g_b_out: float32 [2, 1024], replicated
- g_w_fc: float32 [2, 1024, 4096], P(None, None, 'tensor')
- g_b_fc: float32 [2, 4096], P(None, 'tensor')
- g_w_proj: float32 [2, 4096, 1024], P(None, 'tensor')
- g_b_proj: float32 [2, 1024], replicated
The draws below stay inside these ranges and needn't reach their ends.
Inputs may be any that keep to these rules, and one draw needn't show every extreme that they name: `segment_ids`: never falling along the tokens; segment 1 holds token 127 and token 1920; segments 0 and 2 each hold 1 to 127 tokens.
All inputs are finite; a program needn't handle non-finite values.
Results may differ from the reference program's by a relative error of at most 0.023.
Values may be sent and summed in bfloat16 or wider, within the bound.
No kernel may reach another device: no remote copies, remote signals or barrier semaphores. Data moves between devices by JAX's collectives and lax.ppermute only.
A program may use at most 128 MiB of HBM per device.

```python
import jax
import jax.numpy as jnp
from jax import lax

D = 1024
HEADS = 16
HD = 64
FF = 4096
LAYERS = 2
TOK_DEV = 128
TOKENS = 2048


def draw_segment_ids(key, part):
    key = jax.random.fold_in(key, 5)
    first_key, last_key = jax.random.split(key)
    first = jax.random.randint(first_key, (), 1, TOK_DEV)
    last = jax.random.randint(last_key, (), TOKENS - TOK_DEV + 1, TOKENS)
    spots = jnp.arange(TOKENS, dtype=jnp.int32)
    return (spots >= first).astype(jnp.int32) + (spots >= last).astype(jnp.int32)


def block_scale(rng, dims, shards, low, high):
    level, own = 1.0, jax.random.fold_in(rng, 6)
    for position, shards_of in shards:
        heights = jnp.exp(jax.random.uniform(jax.random.fold_in(own, position), (shards_of,), jnp.float32, low / len(shards), high / len(shards)))
        level = level * jnp.repeat(heights, dims[position] // shards_of).reshape([-1 if axis == position else 1 for axis in range(len(dims))])
    return level


def scatter_about(rng, shape, deviation, bound, shards=(), kind=jnp.bfloat16):
    drawn = deviation * jax.random.normal(rng, shape, jnp.float32)
    if shards:
        drawn = drawn * block_scale(rng, shape, shards, -0.22, 0.18)
    return jnp.clip(drawn, -bound, bound).astype(kind)


def setup_inputs(seed: int = 0) -> dict:
    splits = jax.random.split(jax.random.key(seed), 14)
    tokens = scatter_about(splits[0], (TOKENS, D), 1.0, 6.0, ((0, 16),))
    segment_ids = draw_segment_ids(jax.random.fold_in(splits[13], 71), 0)
    norm_gain = jnp.clip(1.0 + 0.15 * jax.random.normal(splits[2], (LAYERS, 2, D), jnp.float32), 0.25, 1.75).astype(jnp.bfloat16)
    norm_bias = scatter_about(splits[3], (LAYERS, 2, D), 0.3, 1.5)
    w_qkv = scatter_about(splits[4], (LAYERS, D, 3, D), D ** -0.5, 0.1875, ((3, 8),))
    b_qv = scatter_about(splits[5], (LAYERS, 2, D), 0.3, 1.5, ((2, 8),))
    w_out = scatter_about(splits[6], (LAYERS, D, D), (D * 16 // TOKENS) ** -0.5, 2.0, ((1, 8),))
    b_out = scatter_about(splits[7], (LAYERS, D), 0.3, 1.5)
    w_fc = scatter_about(splits[8], (LAYERS, D, FF), D ** -0.5, 0.1875, ((2, 8),))
    b_fc = scatter_about(splits[9], (LAYERS, FF), 0.5, 2.5, ((1, 8),))
    w_proj = scatter_about(splits[10], (LAYERS, FF, D), FF ** -0.5, 0.09375, ((1, 8),))
    b_proj = scatter_about(splits[11], (LAYERS, D), 0.3, 1.5)
    cotangent = scatter_about(splits[12], (TOKENS, D), 1.0, 6.0, ((0, 16),))
    return dict(tokens=tokens, segment_ids=segment_ids, norm_gain=norm_gain, norm_bias=norm_bias, w_qkv=w_qkv, b_qv=b_qv, w_out=w_out, b_out=b_out, w_fc=w_fc, b_fc=b_fc, w_proj=w_proj, b_proj=b_proj, cotangent=cotangent)


@jax.custom_vjp
def low(v):
    return lax.optimization_barrier(v.astype(jnp.bfloat16)).astype(jnp.float32)

@jax.custom_vjp
def low_back(v):
    return v

def low_keep(v):
    return (low(v), None)

def low_pass(kept, grad):
    return (grad,)

def back_keep(v):
    return (v, None)

def back_low(kept, grad):
    return (low(grad),)
low.defvjp(low_keep, low_pass)
low_back.defvjp(back_keep, back_low)

def multiply(spec, left, right):
    return jnp.einsum(spec, left, right, precision=lax.Precision.HIGHEST)

def layer_norm(value, gain, shift):
    mean = lax.optimization_barrier(jnp.mean(value, -1, keepdims=True))
    centered = value - mean
    spread = lax.optimization_barrier(jnp.mean(centered * centered, -1, keepdims=True))
    return centered * lax.rsqrt(spread + 1e-05) * gain + shift

def attend(queries, keys, values, segment_ids):
    count = queries.shape[0]
    width = min(512, count)
    key_spots = jnp.arange(count, dtype=jnp.int32)
    scale = HD ** (-0.5)

    def one_block(args):
        block, start = args
        spots = start + jnp.arange(width, dtype=jnp.int32)
        block_seg = lax.dynamic_slice_in_dim(segment_ids, start, width)
        allowed = (segment_ids[None, :] == block_seg[:, None]) & (key_spots[None, :] <= spots[:, None])
        raw = low_back(multiply('qhd,khd->hqk', block, keys) * scale)
        masked = jnp.where(allowed[None], raw, -1e+30)
        top = lax.optimization_barrier(jnp.max(masked, -1, keepdims=True))
        expd = jnp.exp(masked - top)
        probs = expd / lax.optimization_barrier(jnp.sum(expd, -1, keepdims=True))
        return multiply('hqk,khd->qhd', low(probs), values)
    blocks = queries.reshape(count // width, width, queries.shape[1], queries.shape[2])
    starts = jnp.arange(count // width, dtype=jnp.int32) * width
    return lax.map(jax.checkpoint(one_block), (blocks, starts)).reshape(queries.shape)

def reference(tokens, segment_ids, norm_gain, norm_bias, w_qkv, b_qv, w_out, b_out, w_fc, b_fc, w_proj, b_proj, cotangent):

    def forward(state, gains, shifts, wqkv, bqv, wout, bout, wfc, bfc, wproj, bproj):
        count = state.shape[0]
        for layer in range(LAYERS):
            a_low = low(layer_norm(state, gains[layer, 0], shifts[layer, 0]))
            mixed = multiply('td,dcn->tcn', a_low, wqkv[layer])
            queries = low(low_back(mixed[:, 0] + bqv[layer, 0]))
            keys = low(low_back(mixed[:, 1]))
            values = low(low_back(mixed[:, 2] + bqv[layer, 1]))
            attended = attend(queries.reshape(count, HEADS, HD), keys.reshape(count, HEADS, HD), values.reshape(count, HEADS, HD), segment_ids)
            o_low = low(low_back(attended.reshape(count, D)))
            middle = state + low_back(multiply('tn,nd->td', o_low, wout[layer]) + bout[layer])
            b_low = low(layer_norm(middle, gains[layer, 1], shifts[layer, 1]))
            hidden_pre = low_back(multiply('td,df->tf', b_low, wfc[layer]) + bfc[layer])
            h_low = low(jax.nn.gelu(hidden_pre, approximate=True))
            state = middle + low_back(multiply('tf,fd->td', h_low, wproj[layer]) + bproj[layer])
        return state
    params = (norm_gain.astype(jnp.float32), norm_bias.astype(jnp.float32), w_qkv.astype(jnp.float32), b_qv.astype(jnp.float32), w_out.astype(jnp.float32), b_out.astype(jnp.float32), w_fc.astype(jnp.float32), b_fc.astype(jnp.float32), w_proj.astype(jnp.float32), b_proj.astype(jnp.float32))
    out, pull = jax.vjp(forward, tokens.astype(jnp.float32), *params)
    grads = pull(cotangent.astype(jnp.float32))
    return (out, grads[0], grads[1], grads[2], grads[3], grads[4], grads[5], grads[6], grads[7], grads[8], grads[9], grads[10])
```

```python
import jax
import jax.numpy as jnp
from jax import lax
from jax.sharding import PartitionSpec as P

HD = 64
F32 = jnp.float32
BF16 = jnp.bfloat16


def norm_parts(value):
    mean = jnp.mean(value, -1, keepdims=True)
    centered = value - mean
    spread = jnp.mean(centered * centered, -1, keepdims=True)
    factor = lax.rsqrt(spread + 1e-05)
    return centered * factor, factor


def normalize_back(grad, normed, factor, gain):
    scaled = grad * gain
    back = factor * (
        scaled
        - jnp.mean(scaled, -1, keepdims=True)
        - normed * jnp.mean(scaled * normed, -1, keepdims=True)
    )
    return back, jnp.sum(grad * normed, 0), jnp.sum(grad, 0)


def gelu_tanh(value):
    return jax.nn.gelu(value, approximate=True)


def split_heads(value):
    return value.reshape(value.shape[0], value.shape[1] // HD, HD)


def dot(left, right):
    return jnp.dot(left, right, preferred_element_type=F32)


def column_sum(value):
    return jnp.sum(value.astype(F32), 0)


def gather(value, axis):
    count = lax.axis_size(axis)
    return lax.all_to_all(jnp.broadcast_to(value, (count,) + value.shape), axis, 0, 0)


def scatter_sum(value, axis):
    count = lax.axis_size(axis)
    parts = value.astype(BF16).reshape((count, value.shape[0] // count) + value.shape[1:])
    return jnp.sum(lax.all_to_all(parts, axis, 0, 0).astype(F32), 0)


def gather_rows(value, axis):
    whole = gather(value, axis)
    return whole.reshape((-1,) + whole.shape[2:])


def body(
    tokens,
    segment_ids,
    norm_gain,
    norm_bias,
    w_qkv,
    b_qv,
    w_out,
    b_out,
    w_fc,
    b_fc,
    w_proj,
    b_proj,
    cotangent,
):
    rows = tokens.shape[0]
    total = segment_ids.shape[0]
    layers = w_qkv.shape[0]
    width = w_qkv.shape[1]
    local = w_qkv.shape[3]
    scale = HD ** (-0.5)
    first = lax.axis_index("dp") * rows
    share = rows // lax.axis_size("tensor")
    own = lax.axis_index("tensor") * share
    query_pos = first + jnp.arange(rows, dtype=jnp.int32)
    key_pos = jnp.arange(total, dtype=jnp.int32)
    query_seg = lax.dynamic_slice_in_dim(segment_ids, first, rows)
    allowed = (segment_ids[None, :] == query_seg[:, None]) & (
        key_pos[None, :] <= query_pos[:, None]
    )
    gains = norm_gain.astype(F32)
    shifts = norm_bias.astype(F32)
    state = lax.dynamic_slice_in_dim(tokens, own, share).astype(F32)
    a_full = norm_parts(tokens.astype(F32))[0] * gains[0, 0] + shifts[0, 0]
    a_low = a_full.astype(BF16)
    saved = []
    for layer in range(layers):
        a_normed, a_factor = norm_parts(state)
        if layer:
            a_rows = a_normed * gains[layer, 0] + shifts[layer, 0]
            a_low = gather_rows(a_rows.astype(BF16), "tensor")
        bias_qv = b_qv[layer].astype(F32)
        q_low = (dot(a_low, w_qkv[layer, :, 0]) + bias_qv[0]).astype(BF16)
        k_low = dot(a_low, w_qkv[layer, :, 1]).astype(BF16)
        v_low = (dot(a_low, w_qkv[layer, :, 2]) + bias_qv[1]).astype(BF16)
        kv_all = gather_rows(jnp.concatenate((k_low, v_low), 1), "dp")
        k_all, v_all = kv_all[:, :local], kv_all[:, local:]
        raw = jnp.einsum(
            "qhd,khd->hqk", split_heads(q_low), split_heads(k_all), preferred_element_type=F32
        )
        scores = jnp.where(allowed[None], raw * scale, -1e30)
        top = jnp.max(scores, -1, keepdims=True)
        expd = jnp.exp(scores - top)
        denom = jnp.sum(expd, -1, keepdims=True)
        probs = expd / denom
        log_total = top + jnp.log(denom)
        attended = jnp.einsum(
            "hqk,khd->qhd", probs.astype(BF16), split_heads(v_all), preferred_element_type=F32
        )
        o_low = attended.reshape(rows, local).astype(BF16)
        attn = scatter_sum(dot(o_low, w_out[layer]), "tensor")
        middle = state + (attn + b_out[layer].astype(F32))
        b_normed, b_factor = norm_parts(middle)
        b_rows = b_normed * gains[layer, 1] + shifts[layer, 1]
        b_low = gather_rows(b_rows.astype(BF16), "tensor")
        hidden_pre = dot(b_low, w_fc[layer]) + b_fc[layer].astype(F32)
        h_low = gelu_tanh(hidden_pre).astype(BF16)
        mlp = scatter_sum(dot(h_low, w_proj[layer]), "tensor")
        saved.append(
            (
                a_normed,
                a_factor,
                a_low,
                q_low,
                k_all,
                v_all,
                log_total,
                o_low,
                b_normed,
                b_factor,
                b_low,
                hidden_pre,
                h_low,
            )
        )
        state = middle + (mlp + b_proj[layer].astype(F32))
    out_rows = state.astype(BF16)
    out = None
    g_m = cotangent
    grad = lax.dynamic_slice_in_dim(cotangent, own, share).astype(F32)
    done = [None] * layers
    hold = None
    for layer in reversed(range(layers)):
        (
            a_normed,
            a_factor,
            a_low,
            q_low,
            k_all,
            v_all,
            log_total,
            o_low,
            b_normed,
            b_factor,
            b_low,
            hidden_pre,
            h_low,
        ) = saved[layer]
        g_b_proj = column_sum(g_m)
        g_w_proj = jnp.einsum("tf,td->fd", h_low, g_m, preferred_element_type=F32)
        d_hidden = jnp.einsum("td,fd->tf", g_m, w_proj[layer], preferred_element_type=F32)
        d_pre = jax.vjp(gelu_tanh, hidden_pre)[1](d_hidden)[0]
        g_f = d_pre.astype(BF16)
        g_b_fc = column_sum(g_f)
        g_w_fc = jnp.einsum("td,tf->df", b_low, g_f, preferred_element_type=F32)
        d_b_part = jnp.einsum("tf,df->td", g_f, w_fc[layer], preferred_element_type=F32)
        d_b = scatter_sum(d_b_part, "tensor")
        back_b, gain_b, shift_b = normalize_back(d_b, b_normed, b_factor, gains[layer, 1])
        grad_mid = grad + back_b
        sent = [grad_mid.astype(BF16), jnp.stack((gain_b, shift_b)).astype(BF16)]
        if out is None:
            sent.append(out_rows)
        got = gather(jnp.concatenate(sent, 0), "tensor")
        g_y = got[:, :share].reshape(rows, width)
        gain_b, shift_b = jnp.sum(got[:, share : share + 2].astype(F32), 0)
        if out is None:
            out = got[:, share + 2 :].reshape(rows, width).astype(F32)
        g_b_out = column_sum(g_y)
        g_w_out = jnp.einsum("tn,td->nd", o_low, g_y, preferred_element_type=F32)
        g_o = jnp.einsum("td,nd->tn", g_y, w_out[layer], preferred_element_type=F32).astype(BF16)
        q_heads = split_heads(q_low)
        k_heads = split_heads(k_all)
        v_heads = split_heads(v_all)
        o_heads = split_heads(g_o)
        raw = jnp.einsum("qhd,khd->hqk", q_heads, k_heads, preferred_element_type=F32)
        scores = jnp.where(allowed[None], raw * scale, -1e30)
        probs = jnp.exp(scores - log_total)
        d_probs = jnp.einsum("qhd,khd->hqk", o_heads, v_heads, preferred_element_type=F32)
        delta = jnp.sum(probs * d_probs, -1, keepdims=True)
        g_s = (probs * (d_probs - delta)).astype(BF16)
        d_q = jnp.einsum("hqk,khd->qhd", g_s, k_heads, preferred_element_type=F32) * scale
        part_k = jnp.einsum("hqk,qhd->khd", g_s, q_heads, preferred_element_type=F32) * scale
        part_v = jnp.einsum(
            "hqk,qhd->khd", probs.astype(BF16), o_heads, preferred_element_type=F32
        )
        parts = jnp.concatenate((part_k.reshape(total, local), part_v.reshape(total, local)), 1)
        d_kv = scatter_sum(parts, "dp").astype(BF16)
        g_q = d_q.reshape(rows, local).astype(BF16)
        g_v = d_kv[:, local:]
        g_three = jnp.concatenate((g_q, d_kv), 1)
        w_three = w_qkv[layer].reshape(width, 3 * local)
        g_w_qkv = jnp.einsum("td,tn->dn", a_low, g_three, preferred_element_type=F32)
        d_a_part = jnp.einsum("tn,dn->td", g_three, w_three, preferred_element_type=F32)
        d_a = scatter_sum(d_a_part, "tensor")
        back_a, gain_a, shift_a = normalize_back(d_a, a_normed, a_factor, gains[layer, 0])
        grad = grad_mid + back_a
        sent = (grad.astype(BF16), jnp.stack((gain_a, shift_a)).astype(BF16))
        got = gather(jnp.concatenate(sent, 0), "tensor")
        g_m = got[:, :share].reshape(rows, width)
        gain_a, shift_a = jnp.sum(got[:, share : share + 2].astype(F32), 0)
        small = jnp.concatenate(
            (
                jnp.stack((gain_a, gain_b, shift_a, shift_b, g_b_out, g_b_proj)).reshape(-1),
                column_sum(g_q),
                column_sum(g_v),
                g_b_fc,
            )
        )
        big = ()
        for group in (((g_w_proj, g_w_fc, g_w_out, g_w_qkv),) if layer else ((g_w_proj, g_w_fc), (g_w_out, g_w_qkv))):
            group = tuple(part.astype(BF16) for part in group)
            if hold is not None:
                group = lax.optimization_barrier((group, hold))[0]
            hold = lax.psum(group, "dp")
            big = big + hold
        small = jnp.sum(gather(small.astype(BF16).reshape(1, -1), "dp").astype(F32), 0)[0]
        done[layer] = (small, big)
    grad_input = g_m.astype(F32)

    def both(pick):
        return jnp.stack([pick(*done[layer]) for layer in range(layers)]).astype(F32)

    edge = 6 * width
    return (
        out,
        grad_input,
        both(lambda small, big: small[: 2 * width].reshape(2, width)),
        both(lambda small, big: small[2 * width : 4 * width].reshape(2, width)),
        both(lambda small, big: big[3].reshape(width, 3, local)),
        both(lambda small, big: small[edge : edge + 2 * local].reshape(2, local)),
        both(lambda small, big: big[2]),
        both(lambda small, big: small[4 * width : 5 * width]),
        both(lambda small, big: big[1]),
        both(lambda small, big: small[edge + 2 * local :]),
        both(lambda small, big: big[0]),
        both(lambda small, big: small[5 * width : 6 * width]),
    )


def solution(mesh):
    in_specs = (
        P("dp", None),
        P(),
        P(),
        P(),
        P(None, None, None, "tensor"),
        P(None, None, "tensor"),
        P(None, "tensor", None),
        P(),
        P(None, None, "tensor"),
        P(None, "tensor"),
        P(None, "tensor", None),
        P(),
        P("dp", None),
    )
    out_specs = (
        P("dp", None),
        P("dp", None),
        P(),
        P(),
        P(None, None, None, "tensor"),
        P(None, None, "tensor"),
        P(None, "tensor", None),
        P(),
        P(None, None, "tensor"),
        P(None, "tensor"),
        P(None, "tensor", None),
        P(),
    )
    return jax.shard_map(body, mesh=mesh, in_specs=in_specs, out_specs=out_specs, check_vma=False)
```

```python
import jax
import jax.numpy as jnp
from jax import lax
from jax.sharding import PartitionSpec as P

HD = 64
F32 = jnp.float32
BF16 = jnp.bfloat16


def norm_parts(value):
    mean = jnp.mean(value, -1, keepdims=True)
    centered = value - mean
    spread = jnp.mean(centered * centered, -1, keepdims=True)
    factor = lax.rsqrt(spread + 1e-05)
    return centered * factor, factor


def normalize_back(grad, normed, factor, gain):
    scaled = grad * gain
    back = factor * (
        scaled
        - jnp.mean(scaled, -1, keepdims=True)
        - normed * jnp.mean(scaled * normed, -1, keepdims=True)
    )
    return back, jnp.sum(grad * normed, 0), jnp.sum(grad, 0)


def gelu_tanh(value):
    return jax.nn.gelu(value, approximate=True)


def split_heads(value):
    return value.reshape(value.shape[0], value.shape[1] // HD, HD)


def dot(left, right):
    return jnp.dot(left, right, preferred_element_type=F32)


def column_sum(value):
    return jnp.sum(value.astype(F32), 0)


def gather(value, axis):
    count = lax.axis_size(axis)
    return lax.all_to_all(jnp.broadcast_to(value, (count,) + value.shape), axis, 0, 0)


def scatter_sum(value, axis):
    count = lax.axis_size(axis)
    parts = value.astype(BF16).reshape((count, value.shape[0] // count) + value.shape[1:])
    return jnp.sum(lax.all_to_all(parts, axis, 0, 0).astype(F32), 0)


def sum_all(parts):
    mine = jnp.sum(lax.all_to_all(parts, "dp", 0, 0).astype(F32), 0)
    return gather(mine.astype(BF16), "dp")


def pair_sums(parts):
    place = lax.axis_index("dp")
    count = lax.axis_size("dp")
    x_low, x_high = (place // 4) % 2, place // 8
    steps = ((place % 2, 1), (x_low ^ x_high, 4), (x_high, 12), ((place // 2) % 2, 2))

    def swap(value, flip):
        return lax.ppermute(value, "dp", [(i, i ^ flip) for i in range(count)])

    for bit, flip in steps:
        halves = parts.reshape((2, -1) + parts.shape[1:])
        mine = lax.dynamic_index_in_dim(halves, bit, 0, keepdims=False)
        other = lax.dynamic_index_in_dim(halves, 1 - bit, 0, keepdims=False)
        parts = (mine.astype(F32) + swap(other, flip).astype(F32)).astype(BF16)
    for bit, flip in reversed(steps):
        got = swap(parts, flip)
        parts = jnp.concatenate((jnp.where(bit, got, parts), jnp.where(bit, parts, got)), 0)
    return parts


def gather_rows(value, axis):
    whole = gather(value, axis)
    return whole.reshape((-1,) + whole.shape[2:])


def body(
    tokens,
    segment_ids,
    norm_gain,
    norm_bias,
    w_qkv,
    b_qv,
    w_out,
    b_out,
    w_fc,
    b_fc,
    w_proj,
    b_proj,
    cotangent,
):
    rows = tokens.shape[0]
    total = segment_ids.shape[0]
    layers = w_qkv.shape[0]
    width = w_qkv.shape[1]
    local = w_qkv.shape[3]
    scale = HD ** (-0.5)
    first = lax.axis_index("dp") * rows
    share = rows // lax.axis_size("tensor")
    own = lax.axis_index("tensor") * share
    query_pos = first + jnp.arange(rows, dtype=jnp.int32)
    key_pos = jnp.arange(total, dtype=jnp.int32)
    query_seg = lax.dynamic_slice_in_dim(segment_ids, first, rows)
    allowed = (segment_ids[None, :] == query_seg[:, None]) & (
        key_pos[None, :] <= query_pos[:, None]
    )
    gains = norm_gain.astype(F32)
    shifts = norm_bias.astype(F32)
    state = lax.dynamic_slice_in_dim(tokens, own, share).astype(F32)
    a_full = norm_parts(tokens.astype(F32))[0] * gains[0, 0] + shifts[0, 0]
    a_low = a_full.astype(BF16)
    saved = []
    for layer in range(layers):
        a_normed, a_factor = norm_parts(state)
        if layer:
            a_rows = a_normed * gains[layer, 0] + shifts[layer, 0]
            a_low = gather_rows(a_rows.astype(BF16), "tensor")
        bias_qv = b_qv[layer].astype(F32)
        q_low = (dot(a_low, w_qkv[layer, :, 0]) + bias_qv[0]).astype(BF16)
        k_low = dot(a_low, w_qkv[layer, :, 1]).astype(BF16)
        v_low = (dot(a_low, w_qkv[layer, :, 2]) + bias_qv[1]).astype(BF16)
        kv_all = gather_rows(jnp.concatenate((k_low, v_low), 1), "dp")
        k_all, v_all = kv_all[:, :local], kv_all[:, local:]
        raw = jnp.einsum(
            "qhd,khd->hqk", split_heads(q_low), split_heads(k_all), preferred_element_type=F32
        )
        scores = jnp.where(allowed[None], raw * scale, -1e30)
        top = jnp.max(scores, -1, keepdims=True)
        expd = jnp.exp(scores - top)
        denom = jnp.sum(expd, -1, keepdims=True)
        probs = expd / denom
        log_total = top + jnp.log(denom)
        attended = jnp.einsum(
            "hqk,khd->qhd", probs.astype(BF16), split_heads(v_all), preferred_element_type=F32
        )
        o_low = attended.reshape(rows, local).astype(BF16)
        attn = scatter_sum(dot(o_low, w_out[layer]), "tensor")
        middle = state + (attn + b_out[layer].astype(F32))
        b_normed, b_factor = norm_parts(middle)
        b_rows = b_normed * gains[layer, 1] + shifts[layer, 1]
        b_low = gather_rows(b_rows.astype(BF16), "tensor")
        hidden_pre = dot(b_low, w_fc[layer]) + b_fc[layer].astype(F32)
        h_low = gelu_tanh(hidden_pre).astype(BF16)
        mlp = scatter_sum(dot(h_low, w_proj[layer]), "tensor")
        saved.append(
            (
                a_normed,
                a_factor,
                a_low,
                q_low,
                k_all,
                v_all,
                log_total,
                o_low,
                b_normed,
                b_factor,
                b_low,
                hidden_pre,
                h_low,
            )
        )
        state = middle + (mlp + b_proj[layer].astype(F32))
    out_rows = state.astype(BF16)
    out = None
    g_m = cotangent
    grad = lax.dynamic_slice_in_dim(cotangent, own, share).astype(F32)
    done = [None] * layers
    for layer in reversed(range(layers)):
        (
            a_normed,
            a_factor,
            a_low,
            q_low,
            k_all,
            v_all,
            log_total,
            o_low,
            b_normed,
            b_factor,
            b_low,
            hidden_pre,
            h_low,
        ) = saved[layer]
        g_b_proj = column_sum(g_m)
        g_w_proj = jnp.einsum("tf,td->fd", h_low, g_m, preferred_element_type=F32)
        d_hidden = jnp.einsum("td,fd->tf", g_m, w_proj[layer], preferred_element_type=F32)
        d_pre = jax.vjp(gelu_tanh, hidden_pre)[1](d_hidden)[0]
        g_f = d_pre.astype(BF16)
        g_b_fc = column_sum(g_f)
        g_w_fc = jnp.einsum("td,tf->df", b_low, g_f, preferred_element_type=F32)
        d_b_part = jnp.einsum("tf,df->td", g_f, w_fc[layer], preferred_element_type=F32)
        d_b = scatter_sum(d_b_part, "tensor")
        back_b, gain_b, shift_b = normalize_back(d_b, b_normed, b_factor, gains[layer, 1])
        grad_mid = grad + back_b
        sent = [grad_mid.astype(BF16), jnp.stack((gain_b, shift_b)).astype(BF16)]
        if out is None:
            sent.append(out_rows)
        got = gather(jnp.concatenate(sent, 0), "tensor")
        g_y = got[:, :share].reshape(rows, width)
        gain_b, shift_b = jnp.sum(got[:, share : share + 2].astype(F32), 0)
        if out is None:
            out = got[:, share + 2 :].reshape(rows, width).astype(F32)
        g_b_out = column_sum(g_y)
        g_w_out = jnp.einsum("tn,td->nd", o_low, g_y, preferred_element_type=F32)
        g_o = jnp.einsum("td,nd->tn", g_y, w_out[layer], preferred_element_type=F32).astype(BF16)
        q_heads = split_heads(q_low)
        k_heads = split_heads(k_all)
        v_heads = split_heads(v_all)
        o_heads = split_heads(g_o)
        raw = jnp.einsum("qhd,khd->hqk", q_heads, k_heads, preferred_element_type=F32)
        scores = jnp.where(allowed[None], raw * scale, -1e30)
        probs = jnp.exp(scores - log_total)
        d_probs = jnp.einsum("qhd,khd->hqk", o_heads, v_heads, preferred_element_type=F32)
        delta = jnp.sum(probs * d_probs, -1, keepdims=True)
        g_s = (probs * (d_probs - delta)).astype(BF16)
        d_q = jnp.einsum("hqk,khd->qhd", g_s, k_heads, preferred_element_type=F32) * scale
        part_k = jnp.einsum("hqk,qhd->khd", g_s, q_heads, preferred_element_type=F32) * scale
        part_v = jnp.einsum(
            "hqk,qhd->khd", probs.astype(BF16), o_heads, preferred_element_type=F32
        )
        parts = jnp.concatenate((part_k.reshape(total, local), part_v.reshape(total, local)), 1)
        d_kv = scatter_sum(parts, "dp").astype(BF16)
        g_q = d_q.reshape(rows, local).astype(BF16)
        g_v = d_kv[:, local:]
        g_three = jnp.concatenate((g_q, d_kv), 1)
        w_three = w_qkv[layer].reshape(width, 3 * local)
        g_w_qkv = jnp.einsum("td,tn->dn", a_low, g_three, preferred_element_type=F32)
        d_a_part = jnp.einsum("tn,dn->td", g_three, w_three, preferred_element_type=F32)
        d_a = scatter_sum(d_a_part, "tensor")
        back_a, gain_a, shift_a = normalize_back(d_a, a_normed, a_factor, gains[layer, 0])
        grad = grad_mid + back_a
        sent = (grad.astype(BF16), jnp.stack((gain_a, shift_a)).astype(BF16))
        got = gather(jnp.concatenate(sent, 0), "tensor")
        g_m = got[:, :share].reshape(rows, width)
        gain_a, shift_a = jnp.sum(got[:, share : share + 2].astype(F32), 0)
        small = jnp.concatenate(
            (
                jnp.stack((gain_a, gain_b, shift_a, shift_b, g_b_out, g_b_proj)).reshape(-1),
                column_sum(g_q),
                column_sum(g_v),
                g_b_fc,
            )
        )
        ranks = lax.axis_size("dp")
        small = small.reshape(ranks, 1, -1)
        edge = small.shape[2]
        small = jnp.pad(small, ((0, 0), (0, 7), (0, width - edge)))
        tail = jnp.concatenate((g_w_out.reshape(ranks, -1, width), small), 1).astype(BF16)
        early = (g_w_proj.astype(BF16), g_w_fc.astype(BF16))
        g_w_qkv = g_w_qkv.astype(BF16).reshape(ranks, -1, 3 * local)
        if layer:
            early = lax.psum(early, "dp")
            g_w_qkv = pair_sums(g_w_qkv)
            tail = pair_sums(tail)
        else:
            early = tuple(
                pair_sums(part.reshape(ranks, -1, part.shape[1])).reshape(part.shape) for part in early
            )
            g_w_qkv = sum_all(g_w_qkv)
            tail = sum_all(tail)
        done[layer] = (
            tail[:, -8, : edge].reshape(-1),
            early + (tail[:, :-8].reshape(g_w_out.shape), g_w_qkv),
        )
    grad_input = g_m.astype(F32)

    def both(pick):
        return jnp.stack([pick(*done[layer]) for layer in range(layers)]).astype(F32)

    edge = 6 * width
    return (
        out,
        grad_input,
        both(lambda small, big: small[: 2 * width].reshape(2, width)),
        both(lambda small, big: small[2 * width : 4 * width].reshape(2, width)),
        both(lambda small, big: big[3].reshape(width, 3, local)),
        both(lambda small, big: small[edge : edge + 2 * local].reshape(2, local)),
        both(lambda small, big: big[2]),
        both(lambda small, big: small[4 * width : 5 * width]),
        both(lambda small, big: big[1]),
        both(lambda small, big: small[edge + 2 * local :]),
        both(lambda small, big: big[0]),
        both(lambda small, big: small[5 * width : 6 * width]),
    )


def solution(mesh):
    in_specs = (
        P("dp", None),
        P(),
        P(),
        P(),
        P(None, None, None, "tensor"),
        P(None, None, "tensor"),
        P(None, "tensor", None),
        P(),
        P(None, None, "tensor"),
        P(None, "tensor"),
        P(None, "tensor", None),
        P(),
        P("dp", None),
    )
    out_specs = (
        P("dp", None),
        P("dp", None),
        P(),
        P(),
        P(None, None, None, "tensor"),
        P(None, None, "tensor"),
        P(None, "tensor", None),
        P(),
        P(None, None, "tensor"),
        P(None, "tensor"),
        P(None, "tensor", None),
        P(),
    )
    return jax.shard_map(body, mesh=mesh, in_specs=in_specs, out_specs=out_specs, check_vma=False)
```

```python
import jax
import jax.numpy as jnp
from jax import lax
from jax.sharding import PartitionSpec as P

HD = 64
F32 = jnp.float32
BF16 = jnp.bfloat16


def norm_parts(value):
    mean = jnp.mean(value, -1, keepdims=True)
    centered = value - mean
    spread = jnp.mean(centered * centered, -1, keepdims=True)
    factor = lax.rsqrt(spread + 1e-05)
    return centered * factor, factor


def normalize_back(grad, normed, factor, gain):
    scaled = grad * gain
    back = factor * (
        scaled
        - jnp.mean(scaled, -1, keepdims=True)
        - normed * jnp.mean(scaled * normed, -1, keepdims=True)
    )
    return back, jnp.sum(grad * normed, 0), jnp.sum(grad, 0)


def gelu_tanh(value):
    return jax.nn.gelu(value, approximate=True)


def split_heads(value):
    return value.reshape(value.shape[0], value.shape[1] // HD, HD)


def dot(left, right):
    return jnp.dot(left, right, preferred_element_type=F32)


def column_sum(value):
    return jnp.sum(value.astype(F32), 0)


def gather(value, axis):
    count = lax.axis_size(axis)
    return lax.all_to_all(jnp.broadcast_to(value, (count,) + value.shape), axis, 0, 0)


def scatter_sum(value, axis):
    count = lax.axis_size(axis)
    parts = value.astype(BF16).reshape((count, value.shape[0] // count) + value.shape[1:])
    return jnp.sum(lax.all_to_all(parts, axis, 0, 0).astype(F32), 0)


def sum_all(parts):
    mine = jnp.sum(lax.all_to_all(parts, "dp", 0, 0).astype(F32), 0)
    return gather(mine.astype(BF16), "dp")


def pair_sums(parts, turn, after):
    place = lax.axis_index("dp")
    count = lax.axis_size("dp")
    x_low, x_high = (place // 4) % 2, place // 8
    along_x = ((x_low ^ x_high, 4), (x_high, 12)) if turn else ((x_high, 12), (x_low ^ x_high, 4))
    steps = ((place % 2, 1),) + along_x + (((place // 2) % 2, 2),)

    def swap(value, flip):
        return lax.ppermute(value, "dp", [(i, i ^ flip) for i in range(count)])

    for bit, flip in steps:
        halves = parts.reshape((2, -1) + parts.shape[1:])
        mine = lax.dynamic_index_in_dim(halves, bit, 0, keepdims=False)
        other = lax.dynamic_index_in_dim(halves, 1 - bit, 0, keepdims=False)
        parts = (mine.astype(F32) + swap(other, flip).astype(F32)).astype(BF16)
    parts = lax.optimization_barrier((parts, after))[0]
    for bit, flip in reversed(steps):
        got = swap(parts, flip)
        parts = jnp.concatenate((jnp.where(bit, got, parts), jnp.where(bit, parts, got)), 0)
    return parts


def gather_rows(value, axis):
    whole = gather(value, axis)
    return whole.reshape((-1,) + whole.shape[2:])


def body(
    tokens,
    segment_ids,
    norm_gain,
    norm_bias,
    w_qkv,
    b_qv,
    w_out,
    b_out,
    w_fc,
    b_fc,
    w_proj,
    b_proj,
    cotangent,
):
    rows = tokens.shape[0]
    total = segment_ids.shape[0]
    layers = w_qkv.shape[0]
    width = w_qkv.shape[1]
    local = w_qkv.shape[3]
    scale = HD ** (-0.5)
    first = lax.axis_index("dp") * rows
    share = rows // lax.axis_size("tensor")
    own = lax.axis_index("tensor") * share
    query_pos = first + jnp.arange(rows, dtype=jnp.int32)
    key_pos = jnp.arange(total, dtype=jnp.int32)
    query_seg = lax.dynamic_slice_in_dim(segment_ids, first, rows)
    allowed = (segment_ids[None, :] == query_seg[:, None]) & (
        key_pos[None, :] <= query_pos[:, None]
    )
    gains = norm_gain.astype(F32)
    shifts = norm_bias.astype(F32)
    state = lax.dynamic_slice_in_dim(tokens, own, share).astype(F32)
    a_full = norm_parts(tokens.astype(F32))[0] * gains[0, 0] + shifts[0, 0]
    a_low = a_full.astype(BF16)
    saved = []
    for layer in range(layers):
        a_normed, a_factor = norm_parts(state)
        if layer:
            a_rows = a_normed * gains[layer, 0] + shifts[layer, 0]
            a_low = gather_rows(a_rows.astype(BF16), "tensor")
        bias_qv = b_qv[layer].astype(F32)
        q_low = (dot(a_low, w_qkv[layer, :, 0]) + bias_qv[0]).astype(BF16)
        k_low = dot(a_low, w_qkv[layer, :, 1]).astype(BF16)
        v_low = (dot(a_low, w_qkv[layer, :, 2]) + bias_qv[1]).astype(BF16)
        kv_all = gather_rows(jnp.concatenate((k_low, v_low), 1), "dp")
        k_all, v_all = kv_all[:, :local], kv_all[:, local:]
        raw = jnp.einsum(
            "qhd,khd->hqk", split_heads(q_low), split_heads(k_all), preferred_element_type=F32
        )
        scores = jnp.where(allowed[None], raw * scale, -1e30)
        top = jnp.max(scores, -1, keepdims=True)
        expd = jnp.exp(scores - top)
        denom = jnp.sum(expd, -1, keepdims=True)
        probs = expd / denom
        log_total = top + jnp.log(denom)
        attended = jnp.einsum(
            "hqk,khd->qhd", probs.astype(BF16), split_heads(v_all), preferred_element_type=F32
        )
        o_low = attended.reshape(rows, local).astype(BF16)
        attn = scatter_sum(dot(o_low, w_out[layer]), "tensor")
        middle = state + (attn + b_out[layer].astype(F32))
        b_normed, b_factor = norm_parts(middle)
        b_rows = b_normed * gains[layer, 1] + shifts[layer, 1]
        b_low = gather_rows(b_rows.astype(BF16), "tensor")
        hidden_pre = dot(b_low, w_fc[layer]) + b_fc[layer].astype(F32)
        h_low = gelu_tanh(hidden_pre).astype(BF16)
        mlp_part = dot(h_low, w_proj[layer])
        saved.append(
            (
                a_normed,
                a_factor,
                a_low,
                q_low,
                k_all,
                v_all,
                log_total,
                o_low,
                b_normed,
                b_factor,
                b_low,
                hidden_pre,
                h_low,
            )
        )
        if layer < layers - 1:
            state = middle + (scatter_sum(mlp_part, "tensor") + b_proj[layer].astype(F32))
    out = None
    g_m = cotangent
    grad = lax.dynamic_slice_in_dim(cotangent, own, share).astype(F32)
    done = [None] * layers
    smalls = []
    for layer in reversed(range(layers)):
        (
            a_normed,
            a_factor,
            a_low,
            q_low,
            k_all,
            v_all,
            log_total,
            o_low,
            b_normed,
            b_factor,
            b_low,
            hidden_pre,
            h_low,
        ) = saved[layer]
        g_b_proj = column_sum(g_m)
        g_w_proj = jnp.einsum("tf,td->fd", h_low, g_m, preferred_element_type=F32)
        d_hidden = jnp.einsum("td,fd->tf", g_m, w_proj[layer], preferred_element_type=F32)
        d_pre = jax.vjp(gelu_tanh, hidden_pre)[1](d_hidden)[0]
        g_f = d_pre.astype(BF16)
        g_b_fc = column_sum(g_f)
        g_w_fc = jnp.einsum("td,tf->df", b_low, g_f, preferred_element_type=F32)
        d_b_part = jnp.einsum("tf,df->td", g_f, w_fc[layer], preferred_element_type=F32)
        if out is None:
            both_parts = jnp.stack((mlp_part.reshape(-1, share, width), d_b_part.reshape(-1, share, width)), 1)
            both_sums = scatter_sum(both_parts.reshape(-1, width), "tensor")
            d_b = both_sums[share:]
            out_rows = (middle + (both_sums[:share] + b_proj[layer].astype(F32))).astype(BF16)
        else:
            d_b = scatter_sum(d_b_part, "tensor")
        back_b, gain_b, shift_b = normalize_back(d_b, b_normed, b_factor, gains[layer, 1])
        grad_mid = grad + back_b
        sent = [grad_mid.astype(BF16), jnp.stack((gain_b, shift_b)).astype(BF16)]
        if out is None:
            sent.append(out_rows)
        got = gather(jnp.concatenate(sent, 0), "tensor")
        g_y = got[:, :share].reshape(rows, width)
        gain_b, shift_b = jnp.sum(got[:, share : share + 2].astype(F32), 0)
        if out is None:
            out = got[:, share + 2 :].reshape(rows, width).astype(F32)
        g_b_out = column_sum(g_y)
        g_w_out = jnp.einsum("tn,td->nd", o_low, g_y, preferred_element_type=F32)
        g_o = jnp.einsum("td,nd->tn", g_y, w_out[layer], preferred_element_type=F32).astype(BF16)
        q_heads = split_heads(q_low)
        k_heads = split_heads(k_all)
        v_heads = split_heads(v_all)
        o_heads = split_heads(g_o)
        raw = jnp.einsum("qhd,khd->hqk", q_heads, k_heads, preferred_element_type=F32)
        scores = jnp.where(allowed[None], raw * scale, -1e30)
        probs = jnp.exp(scores - log_total)
        d_probs = jnp.einsum("qhd,khd->hqk", o_heads, v_heads, preferred_element_type=F32)
        delta = jnp.sum(probs * d_probs, -1, keepdims=True)
        g_s = (probs * (d_probs - delta)).astype(BF16)
        d_q = jnp.einsum("hqk,khd->qhd", g_s, k_heads, preferred_element_type=F32) * scale
        part_k = jnp.einsum("hqk,qhd->khd", g_s, q_heads, preferred_element_type=F32) * scale
        part_v = jnp.einsum(
            "hqk,qhd->khd", probs.astype(BF16), o_heads, preferred_element_type=F32
        )
        parts = jnp.concatenate((part_k.reshape(total, local), part_v.reshape(total, local)), 1)
        d_kv = scatter_sum(parts, "dp").astype(BF16)
        g_q = d_q.reshape(rows, local).astype(BF16)
        g_v = d_kv[:, local:]
        g_three = jnp.concatenate((g_q, d_kv), 1)
        w_three = w_qkv[layer].reshape(width, 3 * local)
        g_w_qkv = jnp.einsum("td,tn->dn", a_low, g_three, preferred_element_type=F32)
        d_a_part = jnp.einsum("tn,dn->td", g_three, w_three, preferred_element_type=F32)
        d_a = scatter_sum(d_a_part, "tensor")
        back_a, gain_a, shift_a = normalize_back(d_a, a_normed, a_factor, gains[layer, 0])
        grad = grad_mid + back_a
        sent = (grad.astype(BF16), jnp.stack((gain_a, shift_a)).astype(BF16))
        got = gather(jnp.concatenate(sent, 0), "tensor")
        g_m = got[:, :share].reshape(rows, width)
        gain_a, shift_a = jnp.sum(got[:, share : share + 2].astype(F32), 0)
        norms = jnp.stack((gain_b, shift_b, g_b_out, g_b_proj))
        smalls.append(jnp.concatenate((norms.reshape(-1), column_sum(g_q), column_sum(g_v), g_b_fc)))
        last = jnp.stack((gain_a, shift_a))
        big = tuple(part.astype(BF16) for part in (g_w_proj, g_w_fc, g_w_out, g_w_qkv))
        if layer:
            smalls.append(last.reshape(-1))
            done[layer] = lax.psum(big, "dp")
    ranks = lax.axis_size("dp")
    early = tuple(
        pair_sums(part.reshape(ranks, -1, part.shape[1]), turn, d_kv).reshape(part.shape)
        for turn, part in enumerate(big[:2])
    )
    small = jnp.concatenate(smalls)
    wide = 4 * width
    packed = jnp.concatenate(
        (
            big[2].reshape(ranks, 8, width),
            big[3].reshape(ranks, 8, 8, 3 * local).transpose(0, 2, 1, 3).reshape(ranks, 8, 3 * width),
            jnp.pad(small.astype(BF16).reshape(ranks, 8, -1), ((0, 0), (0, 0), (0, 128 - small.size // (8 * ranks)))),
        ),
        2,
    )
    mine = jnp.sum(lax.all_to_all(packed, "dp", 0, 0).astype(F32), 0)
    got = gather(jnp.concatenate((mine, last.reshape(8, -1)), 1).astype(BF16), "dp")
    late_out = got[:, :, :width].reshape(big[2].shape)
    late_qkv = got[:, :, width:wide].reshape(ranks, 8, 8, 3 * local).transpose(0, 2, 1, 3).reshape(big[3].shape)
    done[0] = early + (late_out, late_qkv)
    small = got[:, :, wide : wide + small.size // (8 * ranks)].reshape(-1)
    last = jnp.sum(got[:, :, wide + 128 :].astype(F32), 0).reshape(2, width)
    cut = 4 * width
    piece = cut + 2 * local + b_fc.shape[1]
    norm_grads, others = [], []
    for layer, base in enumerate((piece + 2 * width, 0)):
        norm_b = small[base : base + cut].reshape(4, width)
        norm_a = small[piece : piece + 2 * width].reshape(2, width) if layer else last
        norm_grads.append(jnp.stack((norm_a, norm_b[:2].astype(norm_a.dtype)), 1))
        others.append((norm_b, small[base + cut : base + piece]))
    grad_input = g_m.astype(F32)

    def both(index):
        return jnp.stack([done[layer][index] for layer in range(layers)]).astype(F32)

    def small_of(pick):
        return jnp.stack([pick(*others[layer]) for layer in range(layers)]).astype(F32)

    return (
        out,
        grad_input,
        jnp.stack([pair[0].astype(F32) for pair in norm_grads]),
        jnp.stack([pair[1].astype(F32) for pair in norm_grads]),
        both(3).reshape(layers, width, 3, local),
        small_of(lambda norm, rest: rest[: 2 * local].reshape(2, local)),
        both(2),
        small_of(lambda norm, rest: norm[2]),
        both(1),
        small_of(lambda norm, rest: rest[2 * local :]),
        both(0),
        small_of(lambda norm, rest: norm[3]),
    )


def solution(mesh):
    in_specs = (
        P("dp", None),
        P(),
        P(),
        P(),
        P(None, None, None, "tensor"),
        P(None, None, "tensor"),
        P(None, "tensor", None),
        P(),
        P(None, None, "tensor"),
        P(None, "tensor"),
        P(None, "tensor", None),
        P(),
        P("dp", None),
    )
    out_specs = (
        P("dp", None),
        P("dp", None),
        P(),
        P(),
        P(None, None, None, "tensor"),
        P(None, None, "tensor"),
        P(None, "tensor", None),
        P(),
        P(None, None, "tensor"),
        P(None, "tensor"),
        P(None, "tensor", None),
        P(),
    )
    return jax.shard_map(body, mesh=mesh, in_specs=in_specs, out_specs=out_specs, check_vma=False)
```

```python
import functools

import jax
import jax.numpy as jnp
from jax import lax
from jax.experimental import pallas as pl
from jax.experimental.pallas import tpu as pltpu
from jax.sharding import PartitionSpec as P

HD = 64
F32 = jnp.float32
BF16 = jnp.bfloat16
ROOT = 0.7978845608028654
CUBE = 0.044715


def dot(left, right):
    return jnp.dot(left, right, preferred_element_type=F32)


def dot_t(left, right):
    return lax.dot_general(left, right, (((1,), (1,)), ((), ())), preferred_element_type=F32)


def norm_parts(value):
    mean = jnp.mean(value, -1, keepdims=True)
    centered = value - mean
    spread = jnp.mean(centered * centered, -1, keepdims=True)
    factor = lax.rsqrt(spread + 1e-05)
    return centered * factor, factor


def tanh_part(value):
    return jnp.tanh(ROOT * (value + CUBE * value * value * value))


def gelu(value):
    return 0.5 * value * (1.0 + tanh_part(value))


def gelu_slope(value):
    bend = tanh_part(value)
    inner = ROOT * (1.0 + 3.0 * CUBE * value * value)
    return 0.5 * (1.0 + bend) + 0.5 * value * (1.0 - bend * bend) * inner


def call(kernel, outs, layered, *args):
    layer, wide = layered

    def spec(index, arg):
        if arg.dtype == jnp.int32 and arg.shape == (1,):
            return pl.BlockSpec(memory_space=pltpu.SMEM)
        if index in wide:
            rest = arg.shape[1:]
            return pl.BlockSpec((None,) + rest, lambda i: (layer,) + (0,) * len(rest))
        return pl.BlockSpec(arg.shape, lambda i: (0,) * arg.ndim)

    return pl.pallas_call(
        kernel,
        grid=(1,),
        in_specs=[spec(index, arg) for index, arg in enumerate(args)],
        out_specs=[pl.BlockSpec(out.shape, lambda i, n=len(out.shape): (0,) * n) for out in outs],
        out_shape=outs,
        compiler_params=pltpu.CompilerParams(vmem_limit_bytes=40 * 1024 * 1024),
    )(*args)


def shape(dims, kind):
    return jax.ShapeDtypeStruct(dims, kind)


def project(a_low, w_ref, bias_ref, q_ref, kv_ref, all_ref):
    q_ref[...] = (dot(a_low, w_ref[0]) + bias_ref[0:1].astype(F32)).astype(BF16)
    k_low = dot(a_low, w_ref[1]).astype(BF16)
    v_low = (dot(a_low, w_ref[2]) + bias_ref[1:2].astype(F32)).astype(BF16)
    local = k_low.shape[1]
    kv_ref[:, :local] = k_low
    kv_ref[:, local:] = v_low
    for index in range(all_ref.shape[0]):
        all_ref[index, :, :local] = k_low
        all_ref[index, :, local:] = v_low


def first_kernel(x_ref, gain_ref, shift_ref, w_ref, bias_ref, a_ref, q_ref, kv_ref, all_ref):
    normed, _ = norm_parts(x_ref[...].astype(F32))
    a_low = (normed * gain_ref[...] + shift_ref[...]).astype(BF16)
    a_ref[...] = a_low
    project(a_low, w_ref, bias_ref, q_ref, kv_ref, all_ref)


def project_kernel(a_ref, w_ref, bias_ref, q_ref, kv_ref, all_ref):
    project(a_ref[...], w_ref, bias_ref, q_ref, kv_ref, all_ref)


def head_masks(rows, local):
    column = lax.broadcasted_iota(jnp.int32, (rows, local), 1)
    return [column < HD, column >= HD]


def only(mask, value):
    return jnp.where(mask, value.astype(F32), 0.0).astype(BF16)


def allowed_of(start_ref, own_ref, all_ref, own_is_query):
    own_spot = start_ref[0] + lax.broadcasted_iota(jnp.int32, own_ref.shape, 0)
    spots = lax.broadcasted_iota(jnp.int32, all_ref.shape, 1)
    order = spots <= own_spot if own_is_query else spots >= own_spot
    return (all_ref[...] == own_ref[...]) & order


def attend_kernel(start_ref, own_ref, all_ref, q_ref, kv_ref, w_ref, o_ref, low_ref, log_ref, part_ref):
    rows, local = q_ref.shape
    total = all_ref.shape[1]
    keys = kv_ref[:, :, :local].reshape(total, local)
    values = kv_ref[:, :, local:].reshape(total, local)
    allowed = allowed_of(start_ref, own_ref, all_ref, True)
    queries = q_ref[...].astype(F32) * HD ** (-0.5)
    masks = head_masks(rows, local)
    outs, logs = [], []
    for mask in masks:
        scores = jnp.where(allowed, dot_t(only(mask, queries), keys), -1e30)
        top = jnp.max(scores, -1, keepdims=True)
        expd = jnp.exp(scores - top)
        denom = jnp.sum(expd, -1, keepdims=True)
        outs.append(dot((expd * (1.0 / denom)).astype(BF16), values))
        logs.append(top + jnp.log(denom))
    attended = jnp.where(masks[0], outs[0], outs[1])
    o_low = attended.astype(BF16)
    o_ref[...] = attended
    low_ref[...] = o_low
    log_ref[...] = jnp.where(masks[0], logs[0], logs[1])
    part_ref[...] = dot(o_low, w_ref[...]).astype(BF16).reshape(part_ref.shape)


def sum_parts(ref, start, rows):
    total = ref[0, start : start + rows].astype(F32)
    for index in range(1, ref.shape[0]):
        total = total + ref[index, start : start + rows].astype(F32)
    return total


def row_kernel(parts_ref, state_ref, bias_ref, gain_ref, shift_ref, state_out, normed_ref, factor_ref, sent_ref):
    state = state_ref[...] + (sum_parts(parts_ref, 0, state_ref.shape[0]) + bias_ref[...])
    normed, factor = norm_parts(state)
    low = (normed * gain_ref[...] + shift_ref[...]).astype(BF16)
    state_out[...] = state
    normed_ref[...] = normed
    factor_ref[...] = jnp.broadcast_to(factor, factor_ref.shape)
    for index in range(sent_ref.shape[0]):
        sent_ref[index] = low


def forward_kernel(b_ref, fc_ref, bias_ref, proj_ref, pre_ref, h_ref, part_ref):
    pre = dot(b_ref[...], fc_ref[...]) + bias_ref[...].astype(F32)
    h_low = gelu(pre).astype(BF16)
    pre_ref[...] = pre
    h_ref[...] = h_low
    part_ref[...] = dot(h_low, proj_ref[...]).astype(BF16).reshape(part_ref.shape)


def turn_kernel(b_ref, fc_ref, bias_ref, proj_ref, g_ref, h_ref, gf_ref, part_ref):
    share = part_ref.shape[1] // 2
    pre = dot(b_ref[...], fc_ref[...]) + bias_ref[...].astype(F32)
    h_low = gelu(pre).astype(BF16)
    h_ref[...] = h_low
    parts = dot(h_low, proj_ref[...]).astype(BF16)
    part_ref[:, :share] = parts.reshape(-1, share, parts.shape[1])
    g_f = (dot_t(g_ref[...], proj_ref[...]) * gelu_slope(pre)).astype(BF16)
    gf_ref[...] = g_f
    parts = dot_t(g_f, fc_ref[...]).astype(BF16)
    part_ref[:, share:] = parts.reshape(-1, share, parts.shape[1])


def backward_kernel(g_ref, pre_ref, fc_ref, proj_ref, gf_ref, part_ref):
    g_f = (dot_t(g_ref[...], proj_ref[...]) * gelu_slope(pre_ref[...])).astype(BF16)
    gf_ref[...] = g_f
    part_ref[...] = dot_t(g_f, fc_ref[...]).astype(BF16).reshape(part_ref.shape)


def norm_back(d_value, normed_ref, factor_ref, gain_ref, grad_ref, sums_ref):
    normed = normed_ref[...]
    scaled = d_value * gain_ref[...]
    back = factor_ref[:, 0:1] * (
        scaled
        - jnp.mean(scaled, -1, keepdims=True)
        - normed * jnp.mean(scaled * normed, -1, keepdims=True)
    )
    sums_ref[0:1] = jnp.sum(d_value * normed, 0, keepdims=True)
    sums_ref[1:2] = jnp.sum(d_value, 0, keepdims=True)
    return grad_ref[...] + back


def back_kernel(parts_ref, normed_ref, factor_ref, gain_ref, grad_ref, grad_out, sums_ref, sent_ref):
    share = normed_ref.shape[0]
    grad = norm_back(sum_parts(parts_ref, 0, share), normed_ref, factor_ref, gain_ref, grad_ref, sums_ref)
    grad_out[...] = grad
    low = grad.astype(BF16)
    for index in range(sent_ref.shape[0]):
        sent_ref[index] = low


def turn_back_kernel(
    parts_ref, state_ref, bias_ref, normed_ref, factor_ref, gain_ref, grad_ref, grad_out, sums_ref, sent_ref
):
    share = normed_ref.shape[0]
    out = (state_ref[...] + (sum_parts(parts_ref, 0, share) + bias_ref[...])).astype(BF16)
    grad = norm_back(sum_parts(parts_ref, share, share), normed_ref, factor_ref, gain_ref, grad_ref, sums_ref)
    grad_out[...] = grad
    low = grad.astype(BF16)
    for index in range(sent_ref.shape[0]):
        sent_ref[index, :share] = low
        sent_ref[index, share:] = out


def two_terms(value):
    high = value.astype(BF16).astype(F32)
    return high, value - high


def output_back_kernel(gy_ref, w_ref, o_ref, log_ref, go_ref, delta_ref, sent_ref):
    rows, local = o_ref.shape
    g_o = dot_t(gy_ref[...], w_ref[...]).astype(BF16)
    go_ref[...] = g_o
    masks = head_masks(rows, local)
    product = g_o.astype(F32) * o_ref[...]
    deltas = [jnp.sum(jnp.where(mask, product, 0.0), -1, keepdims=True) for mask in masks]
    delta = jnp.where(masks[0], deltas[0], deltas[1])
    delta_ref[...] = delta
    rows_of = []
    for value in (log_ref[...], delta):
        turned = value.T
        high, rest = two_terms(jnp.concatenate((turned[0:1], turned[HD : HD + 1]), 0))
        rows_of += [high, rest]
    rows_of.append(jnp.zeros((8, local), F32))
    extra = jnp.concatenate(rows_of, 0).astype(BF16)
    for index in range(sent_ref.shape[0]):
        sent_ref[index, :rows] = g_o
        sent_ref[index, rows:] = extra


def query_back_kernel(start_ref, own_ref, all_ref, q_ref, kv_ref, go_ref, log_ref, delta_ref, gq_ref):
    rows, local = q_ref.shape
    total = all_ref.shape[1]
    keys = kv_ref[:, :, :local].reshape(total, local)
    values = kv_ref[:, :, local:].reshape(total, local)
    allowed = allowed_of(start_ref, own_ref, all_ref, True)
    queries = q_ref[...].astype(F32) * HD ** (-0.5)
    masks = head_masks(rows, local)
    outs = []
    for head, mask in enumerate(masks):
        at = slice(head * HD, head * HD + 1)
        scores = jnp.where(allowed, dot_t(only(mask, queries), keys), -1e30)
        probs = jnp.exp(scores - log_ref[:, at])
        d_probs = dot_t(only(mask, go_ref[...]), values)
        g_s = (probs * (d_probs - delta_ref[:, at])).astype(BF16)
        outs.append(dot(g_s, keys))
    gq_ref[...] = (jnp.where(masks[0], outs[0], outs[1]) * HD ** (-0.5)).astype(BF16)


def key_back_kernel(start_ref, own_ref, all_ref, kv_ref, q_ref, got_ref, gq_ref, w_ref, gkv_ref, part_ref):
    rows, twice = kv_ref.shape
    local = twice // 2
    total = all_ref.shape[1]
    allowed = allowed_of(start_ref, own_ref, all_ref, False)
    queries = q_ref[...]
    g_o = got_ref[:, :rows].reshape(total, local)
    extra = got_ref[:, rows:].astype(F32)
    keys = kv_ref[:, :local].astype(F32) * HD ** (-0.5)
    values = kv_ref[:, local:]
    masks = head_masks(rows, local)
    d_keys, d_values = [], []
    for head, mask in enumerate(masks):

        def row_of(base):
            row = extra[:, base + head : base + head + 1] + extra[:, base + 2 + head : base + 3 + head]
            return jnp.concatenate([row[index] for index in range(row.shape[0])], 1)

        scores = jnp.where(allowed, dot_t(only(mask, keys), queries), -1e30)
        probs = jnp.exp(scores - row_of(0))
        d_probs = dot_t(only(mask, values), g_o)
        g_s = (probs * (d_probs - row_of(4))).astype(BF16)
        d_keys.append(dot(g_s, queries))
        d_values.append(dot(probs.astype(BF16), g_o))
    g_k = (jnp.where(masks[0], d_keys[0], d_keys[1]) * HD ** (-0.5)).astype(BF16)
    g_v = jnp.where(masks[0], d_values[0], d_values[1]).astype(BF16)
    gkv_ref[:, :local] = g_k
    gkv_ref[:, local:] = g_v
    part = dot_t(gq_ref[...], w_ref[0]) + dot_t(g_k, w_ref[1]) + dot_t(g_v, w_ref[2])
    part_ref[...] = part.astype(BF16).reshape(part_ref.shape)


def swap_all(value, axis):
    return lax.all_to_all(value, axis, 0, 0)


def column_sum(value):
    return jnp.sum(value.astype(F32), 0)


def cross(left, right):
    return lax.dot_general(left, right, (((0,), (0,)), ((), ())), preferred_element_type=F32)


def pair_sums(parts, turn, after):
    place = lax.axis_index("dp")
    count = lax.axis_size("dp")
    x_low, x_high = (place // 4) % 2, place // 8
    along_x = ((x_low ^ x_high, 4), (x_high, 12)) if turn else ((x_high, 12), (x_low ^ x_high, 4))
    steps = ((place % 2, 1),) + along_x + (((place // 2) % 2, 2),)

    def swap(value, flip):
        return lax.ppermute(value, "dp", [(i, i ^ flip) for i in range(count)])

    for bit, flip in steps:
        halves = parts.reshape((2, -1) + parts.shape[1:])
        mine = lax.dynamic_index_in_dim(halves, bit, 0, keepdims=False)
        other = lax.dynamic_index_in_dim(halves, 1 - bit, 0, keepdims=False)
        parts = (mine.astype(F32) + swap(other, flip).astype(F32)).astype(BF16)
    parts = lax.optimization_barrier((parts, after))[0]
    for bit, flip in reversed(steps):
        got = swap(parts, flip)
        parts = jnp.concatenate((jnp.where(bit, got, parts), jnp.where(bit, parts, got)), 0)
    return parts


def body(
    tokens,
    segment_ids,
    norm_gain,
    norm_bias,
    w_qkv,
    b_qv,
    w_out,
    b_out,
    w_fc,
    b_fc,
    w_proj,
    b_proj,
    cotangent,
):
    rows, width = tokens.shape
    total = segment_ids.shape[0]
    layers = w_qkv.shape[0]
    local = w_qkv.shape[3]
    hidden = w_fc.shape[2]
    ranks, slots = lax.axis_size("dp"), lax.axis_size("tensor")
    share = rows // slots
    first = (lax.axis_index("dp") * rows).astype(jnp.int32)
    own = lax.axis_index("tensor") * share
    start = first.reshape(1)
    seg_own = lax.dynamic_slice_in_dim(segment_ids, first, rows).reshape(rows, 1)
    seg_all = segment_ids.reshape(1, total)
    spots = (start, seg_own, seg_all)
    gains = norm_gain.astype(F32).reshape(layers, 2, 1, width)
    shifts = norm_bias.astype(F32).reshape(layers, 2, 1, width)
    out_bias = b_out.astype(F32).reshape(layers, 1, width)
    end_bias = b_proj.astype(F32).reshape(layers, 1, width)
    w_three = w_qkv.transpose(0, 2, 1, 3)
    fc_bias = b_fc.reshape(layers, 1, hidden)
    state = lax.dynamic_slice_in_dim(tokens, own, share).astype(F32)
    a_normed, a_factor = norm_parts(state)
    a_factor = jnp.broadcast_to(a_factor, (share, 128))
    row_block = shape((share, width), F32)
    row_stat = shape((share, 128), F32)
    exchange = shape((slots, share, width), BF16)
    saved = []
    qkv_shapes = [
        shape((rows, local), BF16),
        shape((rows, 2 * local), BF16),
        shape((ranks, rows, 2 * local), BF16),
    ]
    a_low = None
    for layer in range(layers):
        if layer:
            q_low, kv_own, kv_sent = call(project_kernel, qkv_shapes, (layer, (1, 2)), a_low, w_three, b_qv)
        else:
            a_low, q_low, kv_own, kv_sent = call(
                first_kernel,
                [shape((rows, width), BF16)] + qkv_shapes,
                (layer, (3, 4)),
                tokens,
                gains[0, 0],
                shifts[0, 0],
                w_three,
                b_qv,
            )
        kv_all = swap_all(kv_sent, "dp")
        o_full, o_low, logs, attn_parts = call(
            attend_kernel,
            [shape((rows, local), F32), shape((rows, local), BF16), shape((rows, local), F32), exchange],
            (layer, (5,)),
            *spots,
            q_low,
            kv_all,
            w_out,
        )
        middle, b_normed, b_factor, b_sent = call(
            row_kernel,
            [row_block, row_block, row_stat, exchange],
            (layer, ()),
            swap_all(attn_parts, "tensor"),
            state,
            out_bias[layer],
            gains[layer, 1],
            shifts[layer, 1],
        )
        b_low = swap_all(b_sent, "tensor").reshape(rows, width)
        kept = [a_normed, a_factor, a_low, q_low, kv_own, kv_all, o_full, o_low, logs, b_normed, b_factor, b_low]
        if layer < layers - 1:
            pre, h_low, parts = call(
                forward_kernel,
                [shape((rows, hidden), F32), shape((rows, hidden), BF16), exchange],
                (layer, (1, 2, 3)),
                b_low,
                w_fc,
                fc_bias,
                w_proj,
            )
            state, a_normed, a_factor, a_sent = call(
                row_kernel,
                [row_block, row_block, row_stat, exchange],
                (layer, ()),
                swap_all(parts, "tensor"),
                middle,
                end_bias[layer],
                gains[layer + 1, 0],
                shifts[layer + 1, 0],
            )
            a_low = swap_all(a_sent, "tensor").reshape(rows, width)
            kept += [pre, h_low]
        saved.append(kept)
    q_every = lax.all_gather(jnp.concatenate([kept[3] for kept in saved], 1), "dp", axis=0, tiled=True)
    g_m = cotangent
    grad = lax.dynamic_slice_in_dim(cotangent, own, share).astype(F32)
    done = [None] * layers
    smalls, sums = [], []
    two_rows = shape((2, width), F32)
    out = None
    for layer in reversed(range(layers)):
        a_normed, a_factor, a_low, q_low, kv_own, kv_all, o_full, o_low, logs, b_normed, b_factor, b_low = (
            saved[layer][:12]
        )
        if layer == layers - 1:
            double = shape((slots, 2 * share, width), BF16)
            h_low, g_f, parts = call(
                turn_kernel,
                [shape((rows, hidden), BF16), shape((rows, hidden), BF16), double],
                (layer, (1, 2, 3)),
                b_low,
                w_fc,
                fc_bias,
                w_proj,
                g_m,
            )
            grad, sums_b, sent = call(
                turn_back_kernel,
                [row_block, two_rows, double],
                (layer, ()),
                swap_all(parts, "tensor"),
                middle,
                end_bias[layer],
                b_normed,
                b_factor,
                gains[layer, 1],
                grad,
            )
            got = swap_all(sent, "tensor")
            g_y = got[:, :share].reshape(rows, width)
            out = got[:, share:].reshape(rows, width).astype(F32)
        else:
            pre, h_low = saved[layer][12:]
            g_f, parts = call(
                backward_kernel,
                [shape((rows, hidden), BF16), exchange],
                (layer, (2, 3)),
                g_m,
                pre,
                w_fc,
                w_proj,
            )
            grad, sums_b, sent = call(
                back_kernel,
                [row_block, two_rows, exchange],
                (layer, ()),
                swap_all(parts, "tensor"),
                b_normed,
                b_factor,
                gains[layer, 1],
                grad,
            )
            g_y = swap_all(sent, "tensor").reshape(rows, width)
        g_o, delta, sent = call(
            output_back_kernel,
            [shape((rows, local), BF16), shape((rows, local), F32), shape((ranks, rows + 16, local), BF16)],
            (layer, (1,)),
            g_y,
            w_out,
            o_full,
            logs,
        )
        go_all = swap_all(sent, "dp")
        (g_q,) = call(
            query_back_kernel,
            [shape((rows, local), BF16)],
            (layer, ()),
            *spots,
            q_low,
            kv_all,
            g_o,
            logs,
            delta,
        )
        g_kv, parts = call(
            key_back_kernel,
            [shape((rows, 2 * local), BF16), exchange],
            (layer, (7,)),
            *spots,
            kv_own,
            q_every[:, layer * local : (layer + 1) * local],
            go_all,
            g_q,
            w_three,
        )
        grad, sums_a, sent = call(
            back_kernel,
            [row_block, two_rows, exchange],
            (layer, ()),
            swap_all(parts, "tensor"),
            a_normed,
            a_factor,
            gains[layer, 0],
            grad,
        )
        sums = [sums_a, sums_b] + sums
        smalls = [
            column_sum(g_y),
            column_sum(g_m),
            column_sum(g_q),
            column_sum(g_kv[:, local:]),
            column_sum(g_f),
        ] + smalls
        g_w_qkv = cross(a_low, jnp.concatenate((g_q, g_kv), 1))
        big = tuple(
            part.astype(BF16) for part in (cross(h_low, g_m), cross(b_low, g_f), cross(o_low, g_y), g_w_qkv)
        )
        if layer:
            g_m = swap_all(sent, "tensor").reshape(rows, width)
            done[layer] = lax.psum(big, "dp")
    early = tuple(
        pair_sums(part.reshape(ranks, -1, part.shape[1]), turn, g_kv).reshape(part.shape)
        for turn, part in enumerate(big[:2])
    )
    tail = jnp.concatenate([sent, jnp.broadcast_to(jnp.concatenate(sums, 0).astype(BF16), (slots, 8, width))], 1)
    got = swap_all(tail, "tensor")
    grad_input = got[:, :share].reshape(rows, width).astype(F32)
    norm_sums = jnp.sum(got[:, share:].astype(F32), 0)
    small = jnp.concatenate([norm_sums.reshape(-1)] + smalls)
    each = small.size // (8 * ranks)
    wide = 4 * width
    packed = jnp.concatenate(
        (
            big[2].reshape(ranks, 8, width),
            big[3].reshape(ranks, 8, 8, 3 * local).transpose(0, 2, 1, 3).reshape(ranks, 8, 3 * width),
            jnp.pad(small.astype(BF16).reshape(ranks, 8, each), ((0, 0), (0, 0), (0, 128 - each))),
        ),
        2,
    )
    mine = jnp.sum(swap_all(packed, "dp").astype(F32), 0).astype(BF16)
    got = swap_all(jnp.broadcast_to(mine, (ranks,) + mine.shape), "dp")
    late_out = got[:, :, :width].reshape(big[2].shape)
    late_qkv = got[:, :, width:wide].reshape(ranks, 8, 8, 3 * local).transpose(0, 2, 1, 3).reshape(big[3].shape)
    done[0] = early + (late_out, late_qkv)
    small = got[:, :, wide : wide + each].reshape(-1).astype(F32)
    norm_grads = small[: 8 * width].reshape(layers, 2, 2, width)
    per_layer = small[8 * width :].reshape(layers, -1)
    cut = 2 * width

    def both(index):
        return jnp.stack([done[layer][index] for layer in range(layers)]).astype(F32)

    return (
        out,
        grad_input,
        norm_grads[:, :, 0],
        norm_grads[:, :, 1],
        both(3).reshape(layers, width, 3, local),
        per_layer[:, cut : cut + 2 * local].reshape(layers, 2, local),
        both(2),
        per_layer[:, :width],
        both(1),
        per_layer[:, cut + 2 * local :],
        both(0),
        per_layer[:, width:cut],
    )


def solution(mesh):
    in_specs = (
        P("dp", None),
        P(),
        P(),
        P(),
        P(None, None, None, "tensor"),
        P(None, None, "tensor"),
        P(None, "tensor", None),
        P(),
        P(None, None, "tensor"),
        P(None, "tensor"),
        P(None, "tensor", None),
        P(),
        P("dp", None),
    )
    out_specs = (
        P("dp", None),
        P("dp", None),
        P(),
        P(),
        P(None, None, None, "tensor"),
        P(None, None, "tensor"),
        P(None, "tensor", None),
        P(),
        P(None, None, "tensor"),
        P(None, "tensor"),
        P(None, "tensor", None),
        P(),
    )
    return jax.shard_map(body, mesh=mesh, in_specs=in_specs, out_specs=out_specs, check_vma=False)
```

```python
import functools

import jax
import jax.numpy as jnp
from jax import lax
from jax.experimental import pallas as pl
from jax.experimental.pallas import tpu as pltpu
from jax.sharding import PartitionSpec as P

HD = 64
F32 = jnp.float32
BF16 = jnp.bfloat16
ROOT = 0.7978845608028654
CUBE = 0.044715


def dot(left, right):
    return jnp.dot(left, right, preferred_element_type=F32)


def dot_t(left, right):
    return lax.dot_general(left, right, (((1,), (1,)), ((), ())), preferred_element_type=F32)


def norm_parts(value):
    mean = jnp.mean(value, -1, keepdims=True)
    centered = value - mean
    spread = jnp.mean(centered * centered, -1, keepdims=True)
    factor = lax.rsqrt(spread + 1e-05)
    return centered * factor, factor


def tanh_part(value):
    return jnp.tanh(ROOT * (value + CUBE * value * value * value))


def gelu(value):
    return 0.5 * value * (1.0 + tanh_part(value))


def gelu_slope(value):
    bend = tanh_part(value)
    inner = ROOT * (1.0 + 3.0 * CUBE * value * value)
    return 0.5 * (1.0 + bend) + 0.5 * value * (1.0 - bend * bend) * inner


def call(kernel, outs, layered, *args, room=12, blocks={}):
    layer, wide = layered
    near = NEAR.get(kernel, ())
    args = [
        arg if index in near or arg.shape == (1,) else pltpu.with_memory_space_constraint(arg, pltpu.HBM)
        for index, arg in enumerate(args)
    ]

    def spec(index, arg):
        if arg.dtype == jnp.int32 and arg.shape == (1,):
            return pl.BlockSpec(memory_space=pltpu.SMEM)
        if index in blocks:
            return pl.BlockSpec(*blocks[index])
        if index in wide:
            rest = arg.shape[1:]
            return pl.BlockSpec((None,) + rest, lambda i: (layer,) + (0,) * len(rest))
        return pl.BlockSpec(arg.shape, lambda i: (0,) * arg.ndim)

    return pl.pallas_call(
        kernel,
        grid=(1,),
        in_specs=[spec(index, arg) for index, arg in enumerate(args)],
        out_specs=[pl.BlockSpec(out.shape, lambda i, n=len(out.shape): (0,) * n) for out in outs],
        out_shape=[pltpu.HBM(out.shape, out.dtype) for out in outs],
        cost_estimate=pl.CostEstimate(flops=1000, bytes_accessed=1000, transcendentals=0),
        compiler_params=pltpu.CompilerParams(vmem_limit_bytes=room * 1024 * 1024),
    )(*args)


def shape(dims, kind):
    return jax.ShapeDtypeStruct(dims, kind)


def project(a_low, w_ref, bias_ref, q_ref, kv_ref, all_ref):
    q_ref[...] = (dot(a_low, w_ref[0]) + bias_ref[0:1].astype(F32)).astype(BF16)
    k_low = dot(a_low, w_ref[1]).astype(BF16)
    v_low = (dot(a_low, w_ref[2]) + bias_ref[1:2].astype(F32)).astype(BF16)
    local = k_low.shape[1]
    kv_ref[:, :local] = k_low
    kv_ref[:, local:] = v_low
    for index in range(all_ref.shape[0]):
        all_ref[index, :, :local] = k_low
        all_ref[index, :, local:] = v_low


def first_kernel(x_ref, gain_ref, shift_ref, w_ref, bias_ref, a_ref, q_ref, kv_ref, all_ref):
    normed, _ = norm_parts(x_ref[...].astype(F32))
    a_low = (normed * gain_ref[...] + shift_ref[...]).astype(BF16)
    a_ref[...] = a_low
    project(a_low, w_ref, bias_ref, q_ref, kv_ref, all_ref)


def project_kernel(a_ref, w_ref, bias_ref, q_ref, kv_ref, all_ref):
    project(a_ref[...], w_ref, bias_ref, q_ref, kv_ref, all_ref)


def head_masks(rows, local):
    column = lax.broadcasted_iota(jnp.int32, (rows, local), 1)
    return [column < HD, column >= HD]


def only(mask, value):
    return jnp.where(mask, value.astype(F32), 0.0).astype(BF16)


def allowed_of(start_ref, own_ref, all_ref, own_is_query):
    own_spot = start_ref[0] + lax.broadcasted_iota(jnp.int32, own_ref.shape, 0)
    spots = lax.broadcasted_iota(jnp.int32, all_ref.shape, 1)
    order = spots <= own_spot if own_is_query else spots >= own_spot
    return (all_ref[...] == own_ref[...]) & order


def attend_kernel(start_ref, own_ref, all_ref, q_ref, kv_ref, w_ref, o_ref, low_ref, log_ref, part_ref):
    rows, local = q_ref.shape
    total = all_ref.shape[1]
    keys = kv_ref[:, :, :local].reshape(total, local)
    values = kv_ref[:, :, local:].reshape(total, local)
    allowed = allowed_of(start_ref, own_ref, all_ref, True)
    queries = q_ref[...].astype(F32) * HD ** (-0.5)
    masks = head_masks(rows, local)
    outs, logs = [], []
    for mask in masks:
        scores = jnp.where(allowed, dot_t(only(mask, queries), keys), -1e30)
        top = jnp.max(scores, -1, keepdims=True)
        expd = jnp.exp(scores - top)
        denom = jnp.sum(expd, -1, keepdims=True)
        outs.append(dot((expd * (1.0 / denom)).astype(BF16), values))
        logs.append(top + jnp.log(denom))
    attended = jnp.where(masks[0], outs[0], outs[1])
    o_low = attended.astype(BF16)
    o_ref[...] = attended
    low_ref[...] = o_low
    log_ref[...] = jnp.where(masks[0], logs[0], logs[1])
    part_ref[...] = dot(o_low, w_ref[...]).astype(BF16).reshape(part_ref.shape)


def sum_parts(ref, start, rows):
    total = ref[0, start : start + rows].astype(F32)
    for index in range(1, ref.shape[0]):
        total = total + ref[index, start : start + rows].astype(F32)
    return total


def row_kernel(parts_ref, state_ref, bias_ref, gain_ref, shift_ref, state_out, normed_ref, factor_ref, sent_ref):
    state = state_ref[...] + (sum_parts(parts_ref, 0, state_ref.shape[0]) + bias_ref[...])
    normed, factor = norm_parts(state)
    low = (normed * gain_ref[...] + shift_ref[...]).astype(BF16)
    state_out[...] = state
    normed_ref[...] = normed
    factor_ref[...] = jnp.broadcast_to(factor, factor_ref.shape)
    for index in range(sent_ref.shape[0]):
        sent_ref[index] = low


def forward_kernel(b_ref, fc_ref, bias_ref, proj_ref, pre_ref, h_ref, part_ref):
    pre = dot(b_ref[...], fc_ref[...]) + bias_ref[...].astype(F32)
    h_low = gelu(pre).astype(BF16)
    pre_ref[...] = pre
    h_ref[...] = h_low
    part_ref[...] = dot(h_low, proj_ref[...]).astype(BF16).reshape(part_ref.shape)


def turn_kernel(b_ref, fc_ref, bias_ref, proj_ref, g_ref, h_ref, gf_ref, part_ref):
    share = part_ref.shape[1] // 2
    pre = dot(b_ref[...], fc_ref[...]) + bias_ref[...].astype(F32)
    h_low = gelu(pre).astype(BF16)
    h_ref[...] = h_low
    parts = dot(h_low, proj_ref[...]).astype(BF16)
    part_ref[:, :share] = parts.reshape(-1, share, parts.shape[1])
    g_f = (dot_t(g_ref[...], proj_ref[...]) * gelu_slope(pre)).astype(BF16)
    gf_ref[...] = g_f
    parts = dot_t(g_f, fc_ref[...]).astype(BF16)
    part_ref[:, share:] = parts.reshape(-1, share, parts.shape[1])


def backward_kernel(g_ref, pre_ref, fc_ref, proj_ref, gf_ref, part_ref):
    g_f = (dot_t(g_ref[...], proj_ref[...]) * gelu_slope(pre_ref[...])).astype(BF16)
    gf_ref[...] = g_f
    part_ref[...] = dot_t(g_f, fc_ref[...]).astype(BF16).reshape(part_ref.shape)


def norm_back(d_value, normed_ref, factor_ref, gain_ref, grad_ref, sums_ref):
    normed = normed_ref[...]
    scaled = d_value * gain_ref[...]
    back = factor_ref[:, 0:1] * (
        scaled
        - jnp.mean(scaled, -1, keepdims=True)
        - normed * jnp.mean(scaled * normed, -1, keepdims=True)
    )
    sums_ref[0:1] = jnp.sum(d_value * normed, 0, keepdims=True)
    sums_ref[1:2] = jnp.sum(d_value, 0, keepdims=True)
    return grad_ref[...] + back


def back_kernel(parts_ref, normed_ref, factor_ref, gain_ref, grad_ref, grad_out, sums_ref, sent_ref):
    share = normed_ref.shape[0]
    grad = norm_back(sum_parts(parts_ref, 0, share), normed_ref, factor_ref, gain_ref, grad_ref, sums_ref)
    grad_out[...] = grad
    low = grad.astype(BF16)
    for index in range(sent_ref.shape[0]):
        sent_ref[index] = low


def turn_back_kernel(
    parts_ref, state_ref, bias_ref, normed_ref, factor_ref, gain_ref, grad_ref, grad_out, sums_ref, sent_ref
):
    share = normed_ref.shape[0]
    out = (state_ref[...] + (sum_parts(parts_ref, 0, share) + bias_ref[...])).astype(BF16)
    grad = norm_back(sum_parts(parts_ref, share, share), normed_ref, factor_ref, gain_ref, grad_ref, sums_ref)
    grad_out[...] = grad
    low = grad.astype(BF16)
    for index in range(sent_ref.shape[0]):
        sent_ref[index, :share] = low
        sent_ref[index, share:] = out


def two_terms(value):
    high = value.astype(BF16).astype(F32)
    return high, value - high


def output_back_kernel(gy_ref, w_ref, o_ref, log_ref, go_ref, delta_ref, sent_ref):
    rows, local = o_ref.shape
    g_o = dot_t(gy_ref[...].reshape(rows, -1), w_ref[...]).astype(BF16)
    go_ref[...] = g_o
    masks = head_masks(rows, local)
    product = g_o.astype(F32) * o_ref[...]
    deltas = [jnp.sum(jnp.where(mask, product, 0.0), -1, keepdims=True) for mask in masks]
    delta = jnp.where(masks[0], deltas[0], deltas[1])
    delta_ref[...] = delta
    rows_of = []
    for value in (log_ref[...], delta):
        turned = value.T
        high, rest = two_terms(jnp.concatenate((turned[0:1], turned[HD : HD + 1]), 0))
        rows_of += [high, rest]
    rows_of.append(jnp.zeros((8, local), F32))
    extra = jnp.concatenate(rows_of, 0).astype(BF16)
    for index in range(sent_ref.shape[0]):
        sent_ref[index, :rows] = g_o
        sent_ref[index, rows:] = extra


def query_back_kernel(start_ref, own_ref, all_ref, q_ref, kv_ref, go_ref, log_ref, delta_ref, gq_ref):
    rows, local = q_ref.shape
    total = all_ref.shape[1]
    keys = kv_ref[:, :, :local].reshape(total, local)
    values = kv_ref[:, :, local:].reshape(total, local)
    allowed = allowed_of(start_ref, own_ref, all_ref, True)
    queries = q_ref[...].astype(F32) * HD ** (-0.5)
    masks = head_masks(rows, local)
    outs = []
    for head, mask in enumerate(masks):
        at = slice(head * HD, head * HD + 1)
        scores = jnp.where(allowed, dot_t(only(mask, queries), keys), -1e30)
        probs = jnp.exp(scores - log_ref[:, at])
        d_probs = dot_t(only(mask, go_ref[...]), values)
        g_s = (probs * (d_probs - delta_ref[:, at])).astype(BF16)
        outs.append(dot(g_s, keys))
    gq_ref[...] = (jnp.where(masks[0], outs[0], outs[1]) * HD ** (-0.5)).astype(BF16)


def key_back_kernel(start_ref, own_ref, all_ref, kv_ref, q_ref, got_ref, gq_ref, w_ref, gkv_ref, part_ref):
    rows, twice = kv_ref.shape
    local = twice // 2
    total = all_ref.shape[1]
    allowed = allowed_of(start_ref, own_ref, all_ref, False)
    queries = q_ref[...]
    g_o = got_ref[:, :rows].reshape(total, local)
    extra = got_ref[:, rows:].astype(F32)
    keys = kv_ref[:, :local].astype(F32) * HD ** (-0.5)
    values = kv_ref[:, local:]
    masks = head_masks(rows, local)
    d_keys, d_values = [], []
    for head, mask in enumerate(masks):

        def row_of(base):
            row = extra[:, base + head : base + head + 1] + extra[:, base + 2 + head : base + 3 + head]
            return jnp.concatenate([row[index] for index in range(row.shape[0])], 1)

        scores = jnp.where(allowed, dot_t(only(mask, keys), queries), -1e30)
        probs = jnp.exp(scores - row_of(0))
        d_probs = dot_t(only(mask, values), g_o)
        g_s = (probs * (d_probs - row_of(4))).astype(BF16)
        d_keys.append(dot(g_s, queries))
        d_values.append(dot(probs.astype(BF16), g_o))
    g_k = (jnp.where(masks[0], d_keys[0], d_keys[1]) * HD ** (-0.5)).astype(BF16)
    g_v = jnp.where(masks[0], d_values[0], d_values[1]).astype(BF16)
    gkv_ref[:, :local] = g_k
    gkv_ref[:, local:] = g_v
    part = dot_t(gq_ref[...], w_ref[0]) + dot_t(g_k, w_ref[1]) + dot_t(g_v, w_ref[2])
    part_ref[...] = part.astype(BF16).reshape(part_ref.shape)


def end_grads_kernel(h_ref, gm_ref, b_ref, gf_ref, proj_ref, fc_ref, gm_sum, gf_sum):
    g_m = gm_ref[...].reshape(-1, gm_ref.shape[-1])
    g_f = gf_ref[...]
    proj_ref[...] = cross(h_ref[...], g_m).astype(BF16)
    fc_ref[...] = cross(b_ref[...], g_f).astype(BF16)
    gm_sum[...] = jnp.sum(g_m.astype(F32), 0, keepdims=True)
    gf_sum[...] = jnp.sum(g_f.astype(F32), 0, keepdims=True)


def attend_grads_kernel(o_ref, gy_ref, a_ref, gq_ref, gkv_ref, out_ref, qkv_ref, gy_sum, gq_sum, gv_sum):
    local = gq_ref.shape[1]
    g_y = gy_ref[...].reshape(-1, gy_ref.shape[-1])
    a_low = a_ref[...]
    g_q, g_v = gq_ref[...], gkv_ref[:, local:]
    out_ref[...] = cross(o_ref[...], g_y).astype(BF16)
    qkv_ref[0] = cross(a_low, g_q).astype(BF16)
    qkv_ref[1] = cross(a_low, gkv_ref[:, :local]).astype(BF16)
    qkv_ref[2] = cross(a_low, g_v).astype(BF16)
    gy_sum[...] = jnp.sum(g_y.astype(F32), 0, keepdims=True)
    gq_sum[...] = jnp.sum(g_q.astype(F32), 0, keepdims=True)
    gv_sum[...] = jnp.sum(g_v.astype(F32), 0, keepdims=True)


NEAR = {
    project_kernel: (0,),
    attend_kernel: (4,),
    row_kernel: (0,),
    forward_kernel: (0,),
    turn_kernel: (0,),
    turn_back_kernel: (0,),
    back_kernel: (0,),
    backward_kernel: (0,),
    output_back_kernel: (0,),
    query_back_kernel: (4,),
    key_back_kernel: (5,),
    end_grads_kernel: (1, 2),
    attend_grads_kernel: (1, 2),
}


def swap_all(value, axis):
    return lax.all_to_all(value, axis, 0, 0)


def cross(left, right):
    return lax.dot_general(left, right, (((0,), (0,)), ((), ())), preferred_element_type=F32)


def pair_sums(parts, turn, events):
    place = lax.axis_index("dp")
    count = lax.axis_size("dp")
    x_low, x_high = (place // 4) % 2, place // 8
    along_x = ((x_low ^ x_high, 4), (x_high, 12)) if turn else ((x_high, 12), (x_low ^ x_high, 4))
    steps = ((place % 2, 1),) + along_x + (((place // 2) % 2, 2),)
    y_here, keys_done, rows_done, tail_done = events
    waits = (y_here, keys_done, rows_done, tail_done, None, None, None, None)

    def swap(value, flip, wait):
        got = lax.ppermute(value, "dp", [(i, i ^ flip) for i in range(count)])
        return got if wait is None else lax.optimization_barrier((got, wait))[0]

    for (bit, flip), wait in zip(steps, waits):
        halves = parts.reshape((2, -1) + parts.shape[1:])
        mine = lax.dynamic_index_in_dim(halves, bit, 0, keepdims=False)
        other = lax.dynamic_index_in_dim(halves, 1 - bit, 0, keepdims=False)
        parts = (mine.astype(F32) + swap(other, flip, wait).astype(F32)).astype(BF16)
    for (bit, flip), wait in zip(reversed(steps), waits[4:]):
        got = swap(parts, flip, wait)
        parts = jnp.concatenate((jnp.where(bit, got, parts), jnp.where(bit, parts, got)), 0)
    return parts


def body(
    tokens,
    segment_ids,
    norm_gain,
    norm_bias,
    w_qkv,
    b_qv,
    w_out,
    b_out,
    w_fc,
    b_fc,
    w_proj,
    b_proj,
    cotangent,
):
    rows, width = tokens.shape
    total = segment_ids.shape[0]
    layers = w_qkv.shape[0]
    local = w_qkv.shape[3]
    hidden = w_fc.shape[2]
    ranks, slots = lax.axis_size("dp"), lax.axis_size("tensor")
    share = rows // slots
    first = (lax.axis_index("dp") * rows).astype(jnp.int32)
    own = lax.axis_index("tensor") * share
    start = first.reshape(1)
    seg_own = lax.dynamic_slice_in_dim(segment_ids, first, rows).reshape(rows, 1)
    seg_all = segment_ids.reshape(1, total)
    spots = (start, seg_own, seg_all)
    gains = norm_gain.astype(F32).reshape(layers, 2, 1, width)
    shifts = norm_bias.astype(F32).reshape(layers, 2, 1, width)
    out_bias = b_out.astype(F32).reshape(layers, 1, width)
    end_bias = b_proj.astype(F32).reshape(layers, 1, width)
    w_three = w_qkv.transpose(0, 2, 1, 3)
    fc_bias = b_fc.reshape(layers, 1, hidden)
    state = lax.dynamic_slice_in_dim(tokens, own, share).astype(F32)
    a_normed, a_factor = norm_parts(state)
    a_factor = jnp.broadcast_to(a_factor, (share, 128))
    row_block = shape((share, width), F32)
    row_stat = shape((share, 128), F32)
    exchange = shape((slots, share, width), BF16)
    saved = []
    qkv_shapes = [
        shape((rows, local), BF16),
        shape((rows, 2 * local), BF16),
        shape((ranks, rows, 2 * local), BF16),
    ]
    a_low = None
    for layer in range(layers):
        if layer:
            q_low, kv_own, kv_sent = call(project_kernel, qkv_shapes, (layer, (1, 2)), a_low, w_three, b_qv)
        else:
            a_low, q_low, kv_own, kv_sent = call(
                first_kernel,
                [shape((rows, width), BF16)] + qkv_shapes,
                (layer, (3, 4)),
                tokens,
                gains[0, 0],
                shifts[0, 0],
                w_three,
                b_qv,
            )
        kv_all = swap_all(kv_sent, "dp")
        o_full, o_low, logs, attn_parts = call(
            attend_kernel,
            [shape((rows, local), F32), shape((rows, local), BF16), shape((rows, local), F32), exchange],
            (layer, (5,)),
            *spots,
            q_low,
            kv_all,
            w_out,
            room=24,
        )
        middle, b_normed, b_factor, b_sent = call(
            row_kernel,
            [row_block, row_block, row_stat, exchange],
            (layer, ()),
            swap_all(attn_parts, "tensor"),
            state,
            out_bias[layer],
            gains[layer, 1],
            shifts[layer, 1],
        )
        b_low = swap_all(b_sent, "tensor").reshape(rows, width)
        kept = [a_normed, a_factor, a_low, q_low, kv_own, kv_all, o_full, o_low, logs, b_normed, b_factor, b_low]
        if layer < layers - 1:
            pre, h_low, parts = call(
                forward_kernel,
                [shape((rows, hidden), F32), shape((rows, hidden), BF16), exchange],
                (layer, (1, 2, 3)),
                b_low,
                w_fc,
                fc_bias,
                w_proj,
            )
            state, a_normed, a_factor, a_sent = call(
                row_kernel,
                [row_block, row_block, row_stat, exchange],
                (layer, ()),
                swap_all(parts, "tensor"),
                middle,
                end_bias[layer],
                gains[layer + 1, 0],
                shifts[layer + 1, 0],
            )
            a_low = swap_all(a_sent, "tensor").reshape(rows, width)
            kept += [pre, h_low]
        saved.append(kept)
    q_every = lax.all_gather(jnp.concatenate([kept[3] for kept in saved], 1), "dp", axis=0, tiled=True)
    g_m = cotangent
    grad = lax.dynamic_slice_in_dim(cotangent, own, share).astype(F32)
    done = [None] * layers
    smalls, sums = [], []
    two_rows = shape((2, width), F32)
    out = None
    events = []

    def end_grads(layer, h_low, g_m, b_low, g_f):
        return call(
            end_grads_kernel,
            [
                shape((hidden, width), BF16),
                shape((width, hidden), BF16),
                shape((1, width), F32),
                shape((1, hidden), F32),
            ],
            (layer, ()),
            h_low,
            g_m,
            b_low,
            g_f,
            room=16,
        )

    for layer in reversed(range(layers)):
        a_normed, a_factor, a_low, q_low, kv_own, kv_all, o_full, o_low, logs, b_normed, b_factor, b_low = (
            saved[layer][:12]
        )
        if layer == layers - 1:
            double = shape((slots, 2 * share, width), BF16)
            h_low, g_f, parts = call(
                turn_kernel,
                [shape((rows, hidden), BF16), shape((rows, hidden), BF16), double],
                (layer, (1, 2, 3)),
                b_low,
                w_fc,
                fc_bias,
                w_proj,
                g_m,
            )
            grad, sums_b, sent = call(
                turn_back_kernel,
                [row_block, two_rows, double],
                (layer, ()),
                swap_all(parts, "tensor"),
                middle,
                end_bias[layer],
                b_normed,
                b_factor,
                gains[layer, 1],
                grad,
            )
            got = swap_all(sent, "tensor")
            g_y = got
            out = got[:, share:].reshape(rows, width).astype(F32)
        else:
            pre, h_low = saved[layer][12:]
            g_f, parts = call(
                backward_kernel,
                [shape((rows, hidden), BF16), exchange],
                (layer, (2, 3)),
                g_m,
                pre,
                w_fc,
                w_proj,
            )
            g_w_proj, g_w_fc, gm_sum, gf_sum = end_grads(layer, h_low, g_m, b_low, g_f)
            grad, sums_b, sent = call(
                back_kernel,
                [row_block, two_rows, exchange],
                (layer, ()),
                swap_all(parts, "tensor"),
                b_normed,
                b_factor,
                gains[layer, 1],
                grad,
            )
            g_y = swap_all(sent, "tensor")
            events.append(g_y)
        g_o, delta, sent = call(
            output_back_kernel,
            [shape((rows, local), BF16), shape((rows, local), F32), shape((ranks, rows + 16, local), BF16)],
            (layer, (1,)),
            g_y,
            w_out,
            o_full,
            logs,
            blocks={0: ((slots, share, width), lambda i: (0, 0, 0))},
        )
        go_all = swap_all(sent, "dp")
        (g_q,) = call(
            query_back_kernel,
            [shape((rows, local), BF16)],
            (layer, ()),
            *spots,
            q_low,
            kv_all,
            g_o,
            logs,
            delta,
            room=24,
        )
        g_kv, parts = call(
            key_back_kernel,
            [shape((rows, 2 * local), BF16), exchange],
            (layer, (7,)),
            *spots,
            kv_own,
            q_every,
            go_all,
            g_q,
            w_three,
            room=24,
            blocks={4: ((total, local), lambda i: (0, layer))},
        )
        grad, sums_a, sent = call(
            back_kernel,
            [row_block, two_rows, exchange],
            (layer, ()),
            swap_all(parts, "tensor"),
            a_normed,
            a_factor,
            gains[layer, 0],
            grad,
        )
        sums = [sums_a, sums_b] + sums
        if layer:
            g_w_proj, g_w_fc, gm_sum, gf_sum = end_grads(layer, h_low, g_m, b_low, g_f)
        g_w_out, g_w_qkv, gy_sum, gq_sum, gv_sum = call(
            attend_grads_kernel,
            [
                shape((local, width), BF16),
                shape((3, width, local), BF16),
                shape((1, width), F32),
                shape((1, local), F32),
                shape((1, local), F32),
            ],
            (layer, ()),
            o_low,
            g_y,
            a_low,
            g_q,
            g_kv,
            room=16,
            blocks={1: ((slots, share, width), lambda i: (0, 0, 0))},
        )
        smalls = [gy_sum, gm_sum, gq_sum, gv_sum, gf_sum] + smalls
        if layer:
            big = (g_w_proj, g_w_fc, g_w_out, g_w_qkv)
            g_m, big = lax.optimization_barrier((swap_all(sent, "tensor").reshape(rows, width), big))
            done[layer] = lax.psum(big, "dp")
    tail = jnp.concatenate([sent, jnp.broadcast_to(jnp.concatenate(sums, 0).astype(BF16), (slots, 8, width))], 1)
    tail_got = got = swap_all(tail, "tensor")
    grad_input = got[:, :share].reshape(rows, width).astype(F32)
    norm_sums = jnp.sum(got[:, share:].astype(F32), 0)
    small = jnp.concatenate([norm_sums.reshape(-1)] + [part.reshape(-1) for part in smalls])
    each = small.size // (8 * ranks)
    wide = 4 * width
    packed = jnp.concatenate(
        (
            g_w_out.reshape(ranks, 8, width),
            g_w_qkv.reshape(3, ranks, 8, 8, local).transpose(1, 3, 0, 2, 4).reshape(ranks, 8, 3 * width),
            jnp.pad(small.astype(BF16).reshape(ranks, 8, each), ((0, 0), (0, 0), (0, 128 - each))),
        ),
        2,
    )
    arrived = swap_all(packed, "dp")
    events += [g_kv, grad, tail_got]
    early = tuple(
        pair_sums(part.reshape(ranks, -1, part.shape[1]), turn, events).reshape(part.shape)
        for turn, part in enumerate((g_w_proj, g_w_fc))
    )
    mine = jnp.sum(arrived.astype(F32), 0).astype(BF16)
    got = swap_all(jnp.broadcast_to(mine, (ranks,) + mine.shape), "dp")
    late_out = got[:, :, :width].reshape(g_w_out.shape)
    late_qkv = got[:, :, width:wide].reshape(ranks, 8, 3, 8, local).transpose(2, 0, 3, 1, 4).reshape(g_w_qkv.shape)
    done[0] = early + (late_out, late_qkv)
    small = got[:, :, wide : wide + each].reshape(-1).astype(F32)
    norm_grads = small[: 8 * width].reshape(layers, 2, 2, width)
    per_layer = small[8 * width :].reshape(layers, -1)
    cut = 2 * width

    def both(index):
        return jnp.stack([done[layer][index] for layer in range(layers)]).astype(F32)

    return (
        out,
        grad_input,
        norm_grads[:, :, 0],
        norm_grads[:, :, 1],
        both(3).transpose(0, 2, 1, 3),
        per_layer[:, cut : cut + 2 * local].reshape(layers, 2, local),
        both(2),
        per_layer[:, :width],
        both(1),
        per_layer[:, cut + 2 * local :],
        both(0),
        per_layer[:, width:cut],
    )


def solution(mesh):
    in_specs = (
        P("dp", None),
        P(),
        P(),
        P(),
        P(None, None, None, "tensor"),
        P(None, None, "tensor"),
        P(None, "tensor", None),
        P(),
        P(None, None, "tensor"),
        P(None, "tensor"),
        P(None, "tensor", None),
        P(),
        P("dp", None),
    )
    out_specs = (
        P("dp", None),
        P("dp", None),
        P(),
        P(),
        P(None, None, None, "tensor"),
        P(None, None, "tensor"),
        P(None, "tensor", None),
        P(),
        P(None, None, "tensor"),
        P(None, "tensor"),
        P(None, "tensor", None),
        P(),
    )
    return jax.shard_map(body, mesh=mesh, in_specs=in_specs, out_specs=out_specs, check_vma=False)
```

```python
import functools

import jax
import jax.numpy as jnp
from jax import lax
from jax.experimental import pallas as pl
from jax.experimental.pallas import tpu as pltpu
from jax.sharding import PartitionSpec as P

HD = 64
F32 = jnp.float32
BF16 = jnp.bfloat16
ROOT = 0.7978845608028654
CUBE = 0.044715


def dot(left, right):
    return jnp.dot(left, right, preferred_element_type=F32)


def dot_t(left, right):
    return lax.dot_general(left, right, (((1,), (1,)), ((), ())), preferred_element_type=F32)


def norm_parts(value):
    mean = jnp.mean(value, -1, keepdims=True)
    centered = value - mean
    spread = jnp.mean(centered * centered, -1, keepdims=True)
    factor = lax.rsqrt(spread + 1e-05)
    return centered * factor, factor


def tanh_part(value):
    return jnp.tanh(ROOT * (value + CUBE * value * value * value))


def gelu(value):
    return 0.5 * value * (1.0 + tanh_part(value))


def gelu_slope(value):
    bend = tanh_part(value)
    inner = ROOT * (1.0 + 3.0 * CUBE * value * value)
    return 0.5 * (1.0 + bend) + 0.5 * value * (1.0 - bend * bend) * inner


def call(kernel, outs, layered, *args, room=12, blocks={}):
    layer, wide = layered
    near = NEAR.get(kernel, ())
    args = [
        arg if index in near or arg.shape == (1,) else pltpu.with_memory_space_constraint(arg, pltpu.HBM)
        for index, arg in enumerate(args)
    ]

    def spec(index, arg):
        if arg.dtype == jnp.int32 and arg.shape == (1,):
            return pl.BlockSpec(memory_space=pltpu.SMEM)
        if index in blocks:
            return pl.BlockSpec(*blocks[index])
        if index in wide:
            rest = arg.shape[1:]
            return pl.BlockSpec((None,) + rest, lambda i: (layer,) + (0,) * len(rest))
        return pl.BlockSpec(arg.shape, lambda i: (0,) * arg.ndim)

    return pl.pallas_call(
        kernel,
        grid=(1,),
        in_specs=[spec(index, arg) for index, arg in enumerate(args)],
        out_specs=[pl.BlockSpec(out.shape, lambda i, n=len(out.shape): (0,) * n) for out in outs],
        out_shape=[pltpu.HBM(out.shape, out.dtype) for out in outs],
        cost_estimate=pl.CostEstimate(flops=1000, bytes_accessed=1000, transcendentals=0),
        compiler_params=pltpu.CompilerParams(vmem_limit_bytes=room * 1024 * 1024),
    )(*args)


def shape(dims, kind):
    return jax.ShapeDtypeStruct(dims, kind)


def project(a_low, w_ref, bias_ref, q_ref, kv_ref, all_ref):
    q_ref[...] = (dot(a_low, w_ref[0]) + bias_ref[0:1].astype(F32)).astype(BF16)
    k_low = dot(a_low, w_ref[1]).astype(BF16)
    v_low = (dot(a_low, w_ref[2]) + bias_ref[1:2].astype(F32)).astype(BF16)
    local = k_low.shape[1]
    kv_ref[:, :local] = k_low
    kv_ref[:, local:] = v_low
    for index in range(all_ref.shape[0]):
        all_ref[index, :, :local] = k_low
        all_ref[index, :, local:] = v_low


def first_kernel(x_ref, gain_ref, shift_ref, w_ref, bias_ref, a_ref, q_ref, kv_ref, all_ref):
    normed, _ = norm_parts(x_ref[...].astype(F32))
    a_low = (normed * gain_ref[...] + shift_ref[...]).astype(BF16)
    a_ref[...] = a_low
    project(a_low, w_ref, bias_ref, q_ref, kv_ref, all_ref)


def project_kernel(a_ref, w_ref, bias_ref, q_ref, kv_ref, all_ref):
    project(a_ref[...], w_ref, bias_ref, q_ref, kv_ref, all_ref)


def head_masks(rows, local):
    column = lax.broadcasted_iota(jnp.int32, (rows, local), 1)
    return [column < HD, column >= HD]


def only(mask, value):
    return jnp.where(mask, value.astype(F32), 0.0).astype(BF16)


def allowed_of(start_ref, own_ref, all_ref, own_is_query):
    own_spot = start_ref[0] + lax.broadcasted_iota(jnp.int32, own_ref.shape, 0)
    spots = lax.broadcasted_iota(jnp.int32, all_ref.shape, 1)
    order = spots <= own_spot if own_is_query else spots >= own_spot
    return (all_ref[...] == own_ref[...]) & order


def attend_kernel(start_ref, own_ref, all_ref, q_ref, kv_ref, w_ref, o_ref, low_ref, log_ref, part_ref):
    rows, local = q_ref.shape
    total = all_ref.shape[1]
    keys = kv_ref[:, :, :local].reshape(total, local)
    values = kv_ref[:, :, local:].reshape(total, local)
    allowed = allowed_of(start_ref, own_ref, all_ref, True)
    queries = q_ref[...].astype(F32) * HD ** (-0.5)
    masks = head_masks(rows, local)
    outs, logs = [], []
    for mask in masks:
        scores = jnp.where(allowed, dot_t(only(mask, queries), keys), -1e30)
        top = jnp.max(scores, -1, keepdims=True)
        expd = jnp.exp(scores - top)
        denom = jnp.sum(expd, -1, keepdims=True)
        outs.append(dot((expd * (1.0 / denom)).astype(BF16), values))
        logs.append(top + jnp.log(denom))
    attended = jnp.where(masks[0], outs[0], outs[1])
    o_low = attended.astype(BF16)
    o_ref[...] = attended
    low_ref[...] = o_low
    log_ref[...] = jnp.where(masks[0], logs[0], logs[1])
    part_ref[...] = dot(o_low, w_ref[...]).astype(BF16).reshape(part_ref.shape)


def sum_parts(ref, start, rows):
    total = ref[0, start : start + rows].astype(F32)
    for index in range(1, ref.shape[0]):
        total = total + ref[index, start : start + rows].astype(F32)
    return total


def row_kernel(parts_ref, state_ref, bias_ref, gain_ref, shift_ref, state_out, normed_ref, factor_ref, sent_ref):
    state = state_ref[...] + (sum_parts(parts_ref, 0, state_ref.shape[0]) + bias_ref[...])
    normed, factor = norm_parts(state)
    low = (normed * gain_ref[...] + shift_ref[...]).astype(BF16)
    state_out[...] = state
    normed_ref[...] = normed
    factor_ref[...] = jnp.broadcast_to(factor, factor_ref.shape)
    for index in range(sent_ref.shape[0]):
        sent_ref[index] = low


def forward_kernel(b_ref, fc_ref, bias_ref, proj_ref, pre_ref, h_ref, part_ref):
    pre = dot(b_ref[...], fc_ref[...]) + bias_ref[...].astype(F32)
    h_low = gelu(pre).astype(BF16)
    pre_ref[...] = pre
    h_ref[...] = h_low
    part_ref[...] = dot(h_low, proj_ref[...]).astype(BF16).reshape(part_ref.shape)


def turn_kernel(b_ref, fc_ref, bias_ref, proj_ref, g_ref, h_ref, gf_ref, part_ref):
    share = part_ref.shape[1] // 2
    pre = dot(b_ref[...], fc_ref[...]) + bias_ref[...].astype(F32)
    h_low = gelu(pre).astype(BF16)
    h_ref[...] = h_low
    parts = dot(h_low, proj_ref[...]).astype(BF16)
    part_ref[:, :share] = parts.reshape(-1, share, parts.shape[1])
    g_f = (dot_t(g_ref[...], proj_ref[...]) * gelu_slope(pre)).astype(BF16)
    gf_ref[...] = g_f
    parts = dot_t(g_f, fc_ref[...]).astype(BF16)
    part_ref[:, share:] = parts.reshape(-1, share, parts.shape[1])


def backward_kernel(g_ref, pre_ref, fc_ref, proj_ref, gf_ref, part_ref):
    g_f = (dot_t(g_ref[...], proj_ref[...]) * gelu_slope(pre_ref[...])).astype(BF16)
    gf_ref[...] = g_f
    part_ref[...] = dot_t(g_f, fc_ref[...]).astype(BF16).reshape(part_ref.shape)


def norm_back(d_value, normed_ref, factor_ref, gain_ref, grad_ref, sums_ref):
    normed = normed_ref[...]
    scaled = d_value * gain_ref[...]
    back = factor_ref[:, 0:1] * (
        scaled
        - jnp.mean(scaled, -1, keepdims=True)
        - normed * jnp.mean(scaled * normed, -1, keepdims=True)
    )
    sums_ref[0:1] = jnp.sum(d_value * normed, 0, keepdims=True)
    sums_ref[1:2] = jnp.sum(d_value, 0, keepdims=True)
    return grad_ref[...] + back


def back_kernel(parts_ref, normed_ref, factor_ref, gain_ref, grad_ref, grad_out, sums_ref, sent_ref):
    share = normed_ref.shape[0]
    grad = norm_back(sum_parts(parts_ref, 0, share), normed_ref, factor_ref, gain_ref, grad_ref, sums_ref)
    grad_out[...] = grad
    low = grad.astype(BF16)
    for index in range(sent_ref.shape[0]):
        sent_ref[index] = low


def turn_back_kernel(
    parts_ref, state_ref, bias_ref, normed_ref, factor_ref, gain_ref, grad_ref, grad_out, sums_ref, sent_ref
):
    share = normed_ref.shape[0]
    out = (state_ref[...] + (sum_parts(parts_ref, 0, share) + bias_ref[...])).astype(BF16)
    grad = norm_back(sum_parts(parts_ref, share, share), normed_ref, factor_ref, gain_ref, grad_ref, sums_ref)
    grad_out[...] = grad
    low = grad.astype(BF16)
    for index in range(sent_ref.shape[0]):
        sent_ref[index, :share] = low
        sent_ref[index, share:] = out


def two_terms(value):
    high = value.astype(BF16).astype(F32)
    return high, value - high


def output_back_kernel(gy_ref, w_ref, o_ref, log_ref, go_ref, delta_ref, sent_ref):
    rows, local = o_ref.shape
    g_o = dot_t(gy_ref[...].reshape(rows, -1), w_ref[...]).astype(BF16)
    go_ref[...] = g_o
    masks = head_masks(rows, local)
    product = g_o.astype(F32) * o_ref[...]
    deltas = [jnp.sum(jnp.where(mask, product, 0.0), -1, keepdims=True) for mask in masks]
    delta = jnp.where(masks[0], deltas[0], deltas[1])
    delta_ref[...] = delta
    rows_of = []
    for value in (log_ref[...], delta):
        turned = value.T
        high, rest = two_terms(jnp.concatenate((turned[0:1], turned[HD : HD + 1]), 0))
        rows_of += [high, rest]
    rows_of.append(jnp.zeros((8, local), F32))
    extra = jnp.concatenate(rows_of, 0).astype(BF16)
    for index in range(sent_ref.shape[0]):
        sent_ref[index, :rows] = g_o
        sent_ref[index, rows:] = extra


def query_back_kernel(start_ref, own_ref, all_ref, q_ref, kv_ref, go_ref, log_ref, delta_ref, gq_ref):
    rows, local = q_ref.shape
    total = all_ref.shape[1]
    keys = kv_ref[:, :, :local].reshape(total, local)
    values = kv_ref[:, :, local:].reshape(total, local)
    allowed = allowed_of(start_ref, own_ref, all_ref, True)
    queries = q_ref[...].astype(F32) * HD ** (-0.5)
    masks = head_masks(rows, local)
    outs = []
    for head, mask in enumerate(masks):
        at = slice(head * HD, head * HD + 1)
        scores = jnp.where(allowed, dot_t(only(mask, queries), keys), -1e30)
        probs = jnp.exp(scores - log_ref[:, at])
        d_probs = dot_t(only(mask, go_ref[...]), values)
        g_s = (probs * (d_probs - delta_ref[:, at])).astype(BF16)
        outs.append(dot(g_s, keys))
    gq_ref[...] = (jnp.where(masks[0], outs[0], outs[1]) * HD ** (-0.5)).astype(BF16)


def key_back_kernel(start_ref, own_ref, all_ref, kv_ref, q_ref, got_ref, gq_ref, w_ref, gkv_ref, part_ref):
    rows, twice = kv_ref.shape
    local = twice // 2
    total = all_ref.shape[1]
    allowed = allowed_of(start_ref, own_ref, all_ref, False)
    queries = q_ref[...]
    g_o = got_ref[:, :rows].reshape(total, local)
    extra = got_ref[:, rows:].astype(F32)
    keys = kv_ref[:, :local].astype(F32) * HD ** (-0.5)
    values = kv_ref[:, local:]
    masks = head_masks(rows, local)
    d_keys, d_values = [], []
    for head, mask in enumerate(masks):

        def row_of(base):
            row = extra[:, base + head : base + head + 1] + extra[:, base + 2 + head : base + 3 + head]
            return jnp.concatenate([row[index] for index in range(row.shape[0])], 1)

        scores = jnp.where(allowed, dot_t(only(mask, keys), queries), -1e30)
        probs = jnp.exp(scores - row_of(0))
        d_probs = dot_t(only(mask, values), g_o)
        g_s = (probs * (d_probs - row_of(4))).astype(BF16)
        d_keys.append(dot(g_s, queries))
        d_values.append(dot(probs.astype(BF16), g_o))
    g_k = (jnp.where(masks[0], d_keys[0], d_keys[1]) * HD ** (-0.5)).astype(BF16)
    g_v = jnp.where(masks[0], d_values[0], d_values[1]).astype(BF16)
    gkv_ref[:, :local] = g_k
    gkv_ref[:, local:] = g_v
    part = dot_t(gq_ref[...], w_ref[0]) + dot_t(g_k, w_ref[1]) + dot_t(g_v, w_ref[2])
    part_ref[...] = part.astype(BF16).reshape(part_ref.shape)


def end_grads_kernel(h_ref, gm_ref, b_ref, gf_ref, pack_ref, gm_sum, gf_sum):
    g_m, g_f = gm_ref[...], gf_ref[...]
    hidden = g_f.shape[1]
    pack_ref[:hidden] = cross(h_ref[...], g_m).astype(BF16)
    g_w_fc = cross(b_ref[...], g_f).astype(BF16)
    for block in range(g_w_fc.shape[0] // hidden):
        at = slice(block * hidden, (block + 1) * hidden)
        pack_ref[hidden:, at] = g_w_fc[at]
    gm_sum[...] = jnp.sum(g_m.astype(F32), 0, keepdims=True)
    gf_sum[...] = jnp.sum(g_f.astype(F32), 0, keepdims=True)


def attend_grads_kernel(o_ref, gy_ref, a_ref, gq_ref, gkv_ref, pack_ref, gy_sum, gq_sum, gv_sum):
    local = gq_ref.shape[1]
    g_y = gy_ref[...].reshape(-1, gy_ref.shape[-1])
    a_low = a_ref[...]
    g_q, g_k, g_v = gq_ref[...], gkv_ref[:, :local], gkv_ref[:, local:]
    pack_ref[:local] = cross(o_ref[...], g_y).astype(BF16)
    for index, grad in enumerate((g_q, g_k, g_v)):
        product = cross(a_low, grad).astype(BF16)
        for block in range(product.shape[0] // local):
            at = slice(block * local, (block + 1) * local)
            pack_ref[(index + 1) * local : (index + 2) * local, at] = product[at]
    gy_sum[...] = jnp.sum(g_y.astype(F32), 0, keepdims=True)
    gq_sum[...] = jnp.sum(g_q.astype(F32), 0, keepdims=True)
    gv_sum[...] = jnp.sum(g_v.astype(F32), 0, keepdims=True)


NEAR = {
    project_kernel: (0,),
    attend_kernel: (4,),
    row_kernel: (0,),
    forward_kernel: (0,),
    turn_kernel: (0,),
    turn_back_kernel: (0,),
    back_kernel: (0,),
    backward_kernel: (0,),
    output_back_kernel: (0,),
    query_back_kernel: (4,),
    key_back_kernel: (5,),
    end_grads_kernel: (1, 2),
    attend_grads_kernel: (1, 2),
}


def swap_all(value, axis):
    return lax.all_to_all(value, axis, 0, 0)


def cross(left, right):
    return lax.dot_general(left, right, (((0,), (0,)), ((), ())), preferred_element_type=F32)


CORE, DEPTH = 1, 2


def side_of(flip):
    return (lax.axis_index("dp") // flip) % 2


def swap(value, flip):
    return lax.ppermute(value, "dp", [(i, i ^ flip) for i in range(lax.axis_size("dp"))])


def after(value, event):
    return lax.optimization_barrier((value, event))[0]


def halve(value, flip, event=None, side=None):
    halves = value.reshape((2, value.shape[0] // 2) + value.shape[1:])
    side = side_of(flip) if side is None else side
    mine = lax.dynamic_index_in_dim(halves, side, 0, keepdims=False)
    got = swap(lax.dynamic_index_in_dim(halves, 1 - side, 0, keepdims=False), flip)
    got = got if event is None else after(got, event)
    return (mine.astype(F32) + got.astype(F32)).astype(BF16)


def rejoin(value, flip, side=None):
    got = swap(value, flip)
    side = side_of(flip) if side is None else side
    return jnp.concatenate((jnp.where(side, got, value), jnp.where(side, value, got)), 0)


def pair_sums(value, turn, events):
    place = lax.axis_index("dp")
    x_low, x_high = (place // 4) % 2, place // 8
    along_x = ((4, x_low ^ x_high), (12, x_high)) if turn else ((12, x_high), (4, x_low ^ x_high))
    steps = ((CORE, place % 2),) + along_x + ((DEPTH, (place // 2) % 2),)
    for (flip, side), event in zip(steps, events):
        value = halve(value, flip, event, side)
    for flip, side in steps[:0:-1]:
        value = rejoin(value, flip, side)
    return rejoin(after(value, events[-1]), *steps[0])


def sum_over_x(values):
    groups = [[4 * x + rest for x in range(lax.axis_size("dp") // 4)] for rest in range(4)]
    return lax.psum(values, "dp", axis_index_groups=groups)


def swap_chips(value):
    groups = [[2 * chip + core for chip in range(lax.axis_size("dp") // 2)] for core in range(2)]
    return lax.all_to_all(value, "dp", 0, 0, axis_index_groups=groups)


def body(
    tokens,
    segment_ids,
    norm_gain,
    norm_bias,
    w_qkv,
    b_qv,
    w_out,
    b_out,
    w_fc,
    b_fc,
    w_proj,
    b_proj,
    cotangent,
):
    rows, width = tokens.shape
    total = segment_ids.shape[0]
    layers = w_qkv.shape[0]
    local = w_qkv.shape[3]
    hidden = w_fc.shape[2]
    ranks, slots = lax.axis_size("dp"), lax.axis_size("tensor")
    share = rows // slots
    first = (lax.axis_index("dp") * rows).astype(jnp.int32)
    own = lax.axis_index("tensor") * share
    start = first.reshape(1)
    seg_own = lax.dynamic_slice_in_dim(segment_ids, first, rows).reshape(rows, 1)
    seg_all = segment_ids.reshape(1, total)
    spots = (start, seg_own, seg_all)
    gains = norm_gain.astype(F32).reshape(layers, 2, 1, width)
    shifts = norm_bias.astype(F32).reshape(layers, 2, 1, width)
    out_bias = b_out.astype(F32).reshape(layers, 1, width)
    end_bias = b_proj.astype(F32).reshape(layers, 1, width)
    w_three = w_qkv.transpose(0, 2, 1, 3)
    fc_bias = b_fc.reshape(layers, 1, hidden)
    state = lax.dynamic_slice_in_dim(tokens, own, share).astype(F32)
    a_normed, a_factor = norm_parts(state)
    a_factor = jnp.broadcast_to(a_factor, (share, 128))
    row_block = shape((share, width), F32)
    row_stat = shape((share, 128), F32)
    exchange = shape((slots, share, width), BF16)
    saved = []
    qkv_shapes = [
        shape((rows, local), BF16),
        shape((rows, 2 * local), BF16),
        shape((ranks, rows, 2 * local), BF16),
    ]
    a_low = None
    for layer in range(layers):
        if layer:
            q_low, kv_own, kv_sent = call(project_kernel, qkv_shapes, (layer, (1, 2)), a_low, w_three, b_qv)
        else:
            a_low, q_low, kv_own, kv_sent = call(
                first_kernel,
                [shape((rows, width), BF16)] + qkv_shapes,
                (layer, (3, 4)),
                tokens,
                gains[0, 0],
                shifts[0, 0],
                w_three,
                b_qv,
            )
        kv_all = swap_all(kv_sent, "dp")
        o_full, o_low, logs, attn_parts = call(
            attend_kernel,
            [shape((rows, local), F32), shape((rows, local), BF16), shape((rows, local), F32), exchange],
            (layer, (5,)),
            *spots,
            q_low,
            kv_all,
            w_out,
            room=24,
        )
        middle, b_normed, b_factor, b_sent = call(
            row_kernel,
            [row_block, row_block, row_stat, exchange],
            (layer, ()),
            swap_all(attn_parts, "tensor"),
            state,
            out_bias[layer],
            gains[layer, 1],
            shifts[layer, 1],
        )
        b_low = swap_all(b_sent, "tensor").reshape(rows, width)
        kept = [a_normed, a_factor, a_low, q_low, kv_own, kv_all, o_full, o_low, logs, b_normed, b_factor, b_low]
        if layer < layers - 1:
            pre, h_low, parts = call(
                forward_kernel,
                [shape((rows, hidden), F32), shape((rows, hidden), BF16), exchange],
                (layer, (1, 2, 3)),
                b_low,
                w_fc,
                fc_bias,
                w_proj,
            )
            state, a_normed, a_factor, a_sent = call(
                row_kernel,
                [row_block, row_block, row_stat, exchange],
                (layer, ()),
                swap_all(parts, "tensor"),
                middle,
                end_bias[layer],
                gains[layer + 1, 0],
                shifts[layer + 1, 0],
            )
            a_low = swap_all(a_sent, "tensor").reshape(rows, width)
            kept += [pre, h_low]
        saved.append(kept)
    q_every = lax.all_gather(jnp.concatenate([kept[3] for kept in saved], 1), "dp", axis=0, tiled=True)
    g_m = cotangent
    grad = lax.dynamic_slice_in_dim(cotangent, own, share).astype(F32)
    done = [None] * layers
    smalls, sums = [], []
    two_rows = shape((2, width), F32)
    out = None
    def end_grads(layer, h_low, g_m, b_low, g_f):
        return call(
            end_grads_kernel,
            [shape((2 * hidden, width), BF16), shape((1, width), F32), shape((1, hidden), F32)],
            (layer, ()),
            h_low,
            g_m,
            b_low,
            g_f,
            room=16,
        )

    for layer in reversed(range(layers)):
        a_normed, a_factor, a_low, q_low, kv_own, kv_all, o_full, o_low, logs, b_normed, b_factor, b_low = (
            saved[layer][:12]
        )
        if layer == layers - 1:
            double = shape((slots, 2 * share, width), BF16)
            h_low, g_f, parts = call(
                turn_kernel,
                [shape((rows, hidden), BF16), shape((rows, hidden), BF16), double],
                (layer, (1, 2, 3)),
                b_low,
                w_fc,
                fc_bias,
                w_proj,
                g_m,
            )
            grad, sums_b, sent = call(
                turn_back_kernel,
                [row_block, two_rows, double],
                (layer, ()),
                swap_all(parts, "tensor"),
                middle,
                end_bias[layer],
                b_normed,
                b_factor,
                gains[layer, 1],
                grad,
            )
            got = swap_all(sent, "tensor")
            g_y = got
            out = got[:, share:].reshape(rows, width).astype(F32)
        else:
            pre, h_low = saved[layer][12:]
            g_f, parts = call(
                backward_kernel,
                [shape((rows, hidden), BF16), exchange],
                (layer, (2, 3)),
                g_m,
                pre,
                w_fc,
                w_proj,
            )
            end_pack, gm_sum, gf_sum = end_grads(layer, h_low, g_m, b_low, g_f)
            grad, sums_b, sent = call(
                back_kernel,
                [row_block, two_rows, exchange],
                (layer, ()),
                swap_all(parts, "tensor"),
                b_normed,
                b_factor,
                gains[layer, 1],
                grad,
            )
            g_y = swap_all(sent, "tensor")
        g_o, delta, sent = call(
            output_back_kernel,
            [shape((rows, local), BF16), shape((rows, local), F32), shape((ranks, rows + 16, local), BF16)],
            (layer, (1,)),
            g_y,
            w_out,
            o_full,
            logs,
            blocks={0: ((slots, share, width), lambda i: (0, 0, 0))},
        )
        go_all = swap_all(sent, "dp")
        (g_q,) = call(
            query_back_kernel,
            [shape((rows, local), BF16)],
            (layer, ()),
            *spots,
            q_low,
            kv_all,
            g_o,
            logs,
            delta,
            room=24,
        )
        g_kv, parts = call(
            key_back_kernel,
            [shape((rows, 2 * local), BF16), exchange],
            (layer, (7,)),
            *spots,
            kv_own,
            q_every,
            go_all,
            g_q,
            w_three,
            room=24,
            blocks={4: ((total, local), lambda i: (0, layer))},
        )
        grad, sums_a, sent = call(
            back_kernel,
            [row_block, two_rows, exchange],
            (layer, ()),
            swap_all(parts, "tensor"),
            a_normed,
            a_factor,
            gains[layer, 0],
            grad,
        )
        sums = [sums_a, sums_b] + sums
        if layer:
            end_pack, gm_sum, gf_sum = end_grads(layer, h_low, g_m, b_low, g_f)
        attend_pack, gy_sum, gq_sum, gv_sum = call(
            attend_grads_kernel,
            [
                shape((4 * local, width), BF16),
                shape((1, width), F32),
                shape((1, local), F32),
                shape((1, local), F32),
            ],
            (layer, ()),
            o_low,
            g_y,
            a_low,
            g_q,
            g_kv,
            room=16,
            blocks={1: ((slots, share, width), lambda i: (0, 0, 0))},
        )
        smalls = [gy_sum, gm_sum, gq_sum, gv_sum, gf_sum] + smalls
        if layer:
            g_m = swap_all(sent, "tensor").reshape(rows, width)
            end_part = halve(halve(end_pack, CORE, go_all), DEPTH, grad)
            attend_part = halve(halve(attend_pack, CORE), DEPTH, g_m)
            done[layer] = sum_over_x((end_part, attend_part))
    tail = jnp.concatenate([sent, jnp.broadcast_to(jnp.concatenate(sums, 0).astype(BF16), (slots, 8, width))], 1)
    tail_got = got = swap_all(tail, "tensor")
    grad_input = got[:, :share].reshape(rows, width).astype(F32)
    norm_sums = jnp.sum(got[:, share:].astype(F32), 0)
    small = jnp.concatenate([norm_sums.reshape(-1)] + [part.reshape(-1) for part in smalls])
    each = small.size // (8 * ranks)
    wide = 4 * width
    packed = jnp.concatenate(
        (
            attend_pack.reshape(ranks, 4, 8, width).transpose(0, 2, 1, 3).reshape(ranks, 8, wide),
            jnp.pad(small.astype(BF16).reshape(ranks, 8, each), ((0, 0), (0, 0), (0, 128 - each))),
        ),
        2,
    )
    half = halve(packed, CORE)
    arrived = swap_chips(half)
    mine = jnp.sum(arrived.astype(F32), 0).astype(BF16)
    got = rejoin(swap_chips(jnp.broadcast_to(mine, (ranks // 2,) + mine.shape)), CORE)
    attend_pack = got[:, :, :wide].reshape(ranks, 8, 4, width).transpose(0, 2, 1, 3).reshape(attend_pack.shape)
    events = (g_y, g_kv, grad, half, arrived)
    end_pack = jnp.concatenate(
        [pair_sums(part, turn, events) for turn, part in enumerate((end_pack[:hidden], end_pack[hidden:]))], 0
    )
    ends, attends = [
        [mine, rejoin(after(rejoin(after(part, half), DEPTH), arrived), CORE)]
        for mine, part in zip((end_pack, attend_pack), done[1])
    ]

    small = got[:, :, wide : wide + each].reshape(-1).astype(F32)
    norm_grads = small[: 8 * width].reshape(layers, 2, 2, width)
    per_layer = small[8 * width :].reshape(layers, -1)
    cut = 2 * width

    def spread(pack):
        blocks = width // (pack.shape[-2])
        return pack.reshape(pack.shape[:-1] + (blocks, -1)).swapaxes(-3, -2).reshape(pack.shape[:-2] + (width, -1))

    g_w_proj = jnp.stack([pack[:hidden] for pack in ends]).astype(F32)
    g_w_fc = jnp.stack([spread(pack[hidden:]) for pack in ends]).astype(F32)
    g_w_out = jnp.stack([pack[:local] for pack in attends]).astype(F32)
    g_w_qkv = jnp.stack([spread(pack[local:].reshape(3, local, width)) for pack in attends]).astype(F32)

    return (
        out,
        grad_input,
        norm_grads[:, :, 0],
        norm_grads[:, :, 1],
        g_w_qkv.transpose(0, 2, 1, 3),
        per_layer[:, cut : cut + 2 * local].reshape(layers, 2, local),
        g_w_out,
        per_layer[:, :width],
        g_w_fc,
        per_layer[:, cut + 2 * local :],
        g_w_proj,
        per_layer[:, width:cut],
    )


def solution(mesh):
    in_specs = (
        P("dp", None),
        P(),
        P(),
        P(),
        P(None, None, None, "tensor"),
        P(None, None, "tensor"),
        P(None, "tensor", None),
        P(),
        P(None, None, "tensor"),
        P(None, "tensor"),
        P(None, "tensor", None),
        P(),
        P("dp", None),
    )
    out_specs = (
        P("dp", None),
        P("dp", None),
        P(),
        P(),
        P(None, None, None, "tensor"),
        P(None, None, "tensor"),
        P(None, "tensor", None),
        P(),
        P(None, None, "tensor"),
        P(None, "tensor"),
        P(None, "tensor", None),
        P(),
    )
    return jax.shard_map(body, mesh=mesh, in_specs=in_specs, out_specs=out_specs, check_vma=False)
```

```python
import functools

import jax
import jax.numpy as jnp
from jax import lax
from jax.experimental import pallas as pl
from jax.experimental.pallas import tpu as pltpu
from jax.sharding import PartitionSpec as P

HD = 64
F32 = jnp.float32
BF16 = jnp.bfloat16
ROOT = 0.7978845608028654
CUBE = 0.044715


def dot(left, right):
    return jnp.dot(left, right, preferred_element_type=F32)


def dot_t(left, right):
    return lax.dot_general(left, right, (((1,), (1,)), ((), ())), preferred_element_type=F32)


def norm_parts(value):
    mean = jnp.mean(value, -1, keepdims=True)
    centered = value - mean
    spread = jnp.mean(centered * centered, -1, keepdims=True)
    factor = lax.rsqrt(spread + 1e-05)
    return centered * factor, factor


def tanh_part(value):
    return jnp.tanh(ROOT * (value + CUBE * value * value * value))


def gelu(value):
    return 0.5 * value * (1.0 + tanh_part(value))


def gelu_slope(value):
    bend = tanh_part(value)
    inner = ROOT * (1.0 + 3.0 * CUBE * value * value)
    return 0.5 * (1.0 + bend) + 0.5 * value * (1.0 - bend * bend) * inner


def call(kernel, outs, layered, *args, room=12, blocks={}):
    layer, wide = layered
    near = NEAR.get(kernel, ())
    args = [
        arg if index in near or arg.shape == (1,) else pltpu.with_memory_space_constraint(arg, pltpu.HBM)
        for index, arg in enumerate(args)
    ]

    def spec(index, arg):
        if arg.dtype == jnp.int32 and arg.shape == (1,):
            return pl.BlockSpec(memory_space=pltpu.SMEM)
        if index in blocks:
            return pl.BlockSpec(*blocks[index])
        if index in wide:
            rest = arg.shape[1:]
            return pl.BlockSpec((None,) + rest, lambda i: (layer,) + (0,) * len(rest))
        return pl.BlockSpec(arg.shape, lambda i: (0,) * arg.ndim)

    return pl.pallas_call(
        kernel,
        grid=(1,),
        in_specs=[spec(index, arg) for index, arg in enumerate(args)],
        out_specs=[pl.BlockSpec(out.shape, lambda i, n=len(out.shape): (0,) * n) for out in outs],
        out_shape=[pltpu.HBM(out.shape, out.dtype) for out in outs],
        cost_estimate=pl.CostEstimate(flops=1000, bytes_accessed=1000, transcendentals=0),
        compiler_params=pltpu.CompilerParams(vmem_limit_bytes=room * 1024 * 1024),
    )(*args)


def shape(dims, kind):
    return jax.ShapeDtypeStruct(dims, kind)


def project(a_low, w_ref, bias_ref, q_ref, kv_ref, all_ref):
    q_ref[...] = (dot(a_low, w_ref[0]) + bias_ref[0:1].astype(F32)).astype(BF16)
    k_low = dot(a_low, w_ref[1]).astype(BF16)
    v_low = (dot(a_low, w_ref[2]) + bias_ref[1:2].astype(F32)).astype(BF16)
    local = k_low.shape[1]
    kv_ref[:, :local] = k_low
    kv_ref[:, local:] = v_low
    for index in range(all_ref.shape[0]):
        all_ref[index, :, :local] = k_low
        all_ref[index, :, local:] = v_low


def first_kernel(x_ref, gain_ref, shift_ref, w_ref, bias_ref, a_ref, q_ref, kv_ref, all_ref):
    normed, _ = norm_parts(x_ref[...].astype(F32))
    a_low = (normed * gain_ref[...] + shift_ref[...]).astype(BF16)
    a_ref[...] = a_low
    project(a_low, w_ref, bias_ref, q_ref, kv_ref, all_ref)


def project_kernel(a_ref, w_ref, bias_ref, q_ref, kv_ref, all_ref):
    project(a_ref[...], w_ref, bias_ref, q_ref, kv_ref, all_ref)


def head_masks(rows, local):
    column = lax.broadcasted_iota(jnp.int32, (rows, local), 1)
    return [column < HD, column >= HD]


def only(mask, value):
    return jnp.where(mask, value.astype(F32), 0.0).astype(BF16)


def allowed_of(start_ref, own_ref, all_ref, own_is_query):
    own_spot = start_ref[0] + lax.broadcasted_iota(jnp.int32, own_ref.shape, 0)
    spots = lax.broadcasted_iota(jnp.int32, all_ref.shape, 1)
    order = spots <= own_spot if own_is_query else spots >= own_spot
    return (all_ref[...] == own_ref[...]) & order


def attend_kernel(start_ref, own_ref, all_ref, q_ref, kv_ref, w_ref, o_ref, low_ref, log_ref, part_ref):
    rows, local = q_ref.shape
    total = all_ref.shape[1]
    keys = kv_ref[:, :, :local].reshape(total, local)
    values = kv_ref[:, :, local:].reshape(total, local)
    allowed = allowed_of(start_ref, own_ref, all_ref, True)
    queries = q_ref[...].astype(F32) * HD ** (-0.5)
    masks = head_masks(rows, local)
    outs, logs = [], []
    for mask in masks:
        scores = jnp.where(allowed, dot_t(only(mask, queries), keys), -1e30)
        top = jnp.max(scores, -1, keepdims=True)
        expd = jnp.exp(scores - top)
        denom = jnp.sum(expd, -1, keepdims=True)
        outs.append(dot((expd * (1.0 / denom)).astype(BF16), values))
        logs.append(top + jnp.log(denom))
    attended = jnp.where(masks[0], outs[0], outs[1])
    o_low = attended.astype(BF16)
    o_ref[...] = attended
    low_ref[...] = o_low
    log_ref[...] = jnp.where(masks[0], logs[0], logs[1])
    part_ref[...] = dot(o_low, w_ref[...]).astype(BF16).reshape(part_ref.shape)


def sum_parts(ref, start, rows):
    total = ref[0, start : start + rows].astype(F32)
    for index in range(1, ref.shape[0]):
        total = total + ref[index, start : start + rows].astype(F32)
    return total


def row_kernel(parts_ref, state_ref, bias_ref, gain_ref, shift_ref, state_out, normed_ref, factor_ref, sent_ref):
    state = state_ref[...] + (sum_parts(parts_ref, 0, state_ref.shape[0]) + bias_ref[...])
    normed, factor = norm_parts(state)
    low = (normed * gain_ref[...] + shift_ref[...]).astype(BF16)
    state_out[...] = state
    normed_ref[...] = normed
    factor_ref[...] = jnp.broadcast_to(factor, factor_ref.shape)
    for index in range(sent_ref.shape[0]):
        sent_ref[index] = low


def forward_kernel(b_ref, fc_ref, bias_ref, proj_ref, pre_ref, h_ref, part_ref):
    pre = dot(b_ref[...], fc_ref[...]) + bias_ref[...].astype(F32)
    h_low = gelu(pre).astype(BF16)
    pre_ref[...] = pre
    h_ref[...] = h_low
    part_ref[...] = dot(h_low, proj_ref[...]).astype(BF16).reshape(part_ref.shape)


def turn_kernel(b_ref, fc_ref, bias_ref, proj_ref, g_ref, h_ref, gf_ref, part_ref):
    share = part_ref.shape[1] // 2
    pre = dot(b_ref[...], fc_ref[...]) + bias_ref[...].astype(F32)
    h_low = gelu(pre).astype(BF16)
    h_ref[...] = h_low
    parts = dot(h_low, proj_ref[...]).astype(BF16)
    part_ref[:, :share] = parts.reshape(-1, share, parts.shape[1])
    g_f = (dot_t(g_ref[...], proj_ref[...]) * gelu_slope(pre)).astype(BF16)
    gf_ref[...] = g_f
    parts = dot_t(g_f, fc_ref[...]).astype(BF16)
    part_ref[:, share:] = parts.reshape(-1, share, parts.shape[1])


def backward_kernel(g_ref, pre_ref, fc_ref, proj_ref, gf_ref, part_ref):
    g_f = (dot_t(g_ref[...], proj_ref[...]) * gelu_slope(pre_ref[...])).astype(BF16)
    gf_ref[...] = g_f
    part_ref[...] = dot_t(g_f, fc_ref[...]).astype(BF16).reshape(part_ref.shape)


def norm_back(d_value, normed_ref, factor_ref, gain_ref, grad_ref, sums_ref):
    normed = normed_ref[...]
    scaled = d_value * gain_ref[...]
    back = factor_ref[:, 0:1] * (
        scaled
        - jnp.mean(scaled, -1, keepdims=True)
        - normed * jnp.mean(scaled * normed, -1, keepdims=True)
    )
    sums_ref[0:1] = jnp.sum(d_value * normed, 0, keepdims=True)
    sums_ref[1:2] = jnp.sum(d_value, 0, keepdims=True)
    return grad_ref[...] + back


def back_kernel(parts_ref, normed_ref, factor_ref, gain_ref, grad_ref, grad_out, sums_ref, sent_ref):
    share = normed_ref.shape[0]
    grad = norm_back(sum_parts(parts_ref, 0, share), normed_ref, factor_ref, gain_ref, grad_ref, sums_ref)
    grad_out[...] = grad
    low = grad.astype(BF16)
    for index in range(sent_ref.shape[0]):
        sent_ref[index] = low


def turn_back_kernel(
    parts_ref, state_ref, bias_ref, normed_ref, factor_ref, gain_ref, grad_ref, grad_out, sums_ref, sent_ref
):
    share = normed_ref.shape[0]
    out = (state_ref[...] + (sum_parts(parts_ref, 0, share) + bias_ref[...])).astype(BF16)
    grad = norm_back(sum_parts(parts_ref, share, share), normed_ref, factor_ref, gain_ref, grad_ref, sums_ref)
    grad_out[...] = grad
    low = grad.astype(BF16)
    for index in range(sent_ref.shape[0]):
        sent_ref[index, :share] = low
        sent_ref[index, share:] = out


def two_terms(value):
    high = value.astype(BF16).astype(F32)
    return high, value - high


def output_back_kernel(gy_ref, w_ref, o_ref, log_ref, go_ref, delta_ref, sent_ref):
    rows, local = o_ref.shape
    g_o = dot_t(gy_ref[...].reshape(rows, -1), w_ref[...]).astype(BF16)
    go_ref[...] = g_o
    masks = head_masks(rows, local)
    product = g_o.astype(F32) * o_ref[...]
    deltas = [jnp.sum(jnp.where(mask, product, 0.0), -1, keepdims=True) for mask in masks]
    delta = jnp.where(masks[0], deltas[0], deltas[1])
    delta_ref[...] = delta
    rows_of = []
    for value in (log_ref[...], delta):
        turned = value.T
        high, rest = two_terms(jnp.concatenate((turned[0:1], turned[HD : HD + 1]), 0))
        rows_of += [high, rest]
    rows_of.append(jnp.zeros((8, local), F32))
    extra = jnp.concatenate(rows_of, 0).astype(BF16)
    for index in range(sent_ref.shape[0]):
        sent_ref[index, :rows] = g_o
        sent_ref[index, rows:] = extra


def query_back_kernel(start_ref, own_ref, all_ref, q_ref, kv_ref, go_ref, log_ref, delta_ref, gq_ref):
    rows, local = q_ref.shape
    total = all_ref.shape[1]
    keys = kv_ref[:, :, :local].reshape(total, local)
    values = kv_ref[:, :, local:].reshape(total, local)
    allowed = allowed_of(start_ref, own_ref, all_ref, True)
    queries = q_ref[...].astype(F32) * HD ** (-0.5)
    masks = head_masks(rows, local)
    outs = []
    for head, mask in enumerate(masks):
        at = slice(head * HD, head * HD + 1)
        scores = jnp.where(allowed, dot_t(only(mask, queries), keys), -1e30)
        probs = jnp.exp(scores - log_ref[:, at])
        d_probs = dot_t(only(mask, go_ref[...]), values)
        g_s = (probs * (d_probs - delta_ref[:, at])).astype(BF16)
        outs.append(dot(g_s, keys))
    gq_ref[...] = (jnp.where(masks[0], outs[0], outs[1]) * HD ** (-0.5)).astype(BF16)


def key_back_kernel(start_ref, own_ref, all_ref, kv_ref, q_ref, got_ref, gq_ref, w_ref, gkv_ref, part_ref):
    rows, twice = kv_ref.shape
    local = twice // 2
    total = all_ref.shape[1]
    allowed = allowed_of(start_ref, own_ref, all_ref, False)
    queries = q_ref[...]
    g_o = got_ref[:, :rows].reshape(total, local)
    extra = got_ref[:, rows:].astype(F32)
    keys = kv_ref[:, :local].astype(F32) * HD ** (-0.5)
    values = kv_ref[:, local:]
    masks = head_masks(rows, local)
    d_keys, d_values = [], []
    for head, mask in enumerate(masks):

        def row_of(base):
            row = extra[:, base + head : base + head + 1] + extra[:, base + 2 + head : base + 3 + head]
            return jnp.concatenate([row[index] for index in range(row.shape[0])], 1)

        scores = jnp.where(allowed, dot_t(only(mask, keys), queries), -1e30)
        probs = jnp.exp(scores - row_of(0))
        d_probs = dot_t(only(mask, values), g_o)
        g_s = (probs * (d_probs - row_of(4))).astype(BF16)
        d_keys.append(dot(g_s, queries))
        d_values.append(dot(probs.astype(BF16), g_o))
    g_k = (jnp.where(masks[0], d_keys[0], d_keys[1]) * HD ** (-0.5)).astype(BF16)
    g_v = jnp.where(masks[0], d_values[0], d_values[1]).astype(BF16)
    gkv_ref[:, :local] = g_k
    gkv_ref[:, local:] = g_v
    part = dot_t(gq_ref[...], w_ref[0]) + dot_t(g_k, w_ref[1]) + dot_t(g_v, w_ref[2])
    part_ref[...] = part.astype(BF16).reshape(part_ref.shape)


def end_grads_kernel(h_ref, gm_ref, b_ref, gf_ref, pack_ref, gm_sum, gf_sum):
    g_m, g_f = gm_ref[...], gf_ref[...]
    hidden = g_f.shape[1]
    pack_ref[:hidden] = cross(h_ref[...], g_m).astype(BF16)
    g_w_fc = cross(b_ref[...], g_f).astype(BF16)
    for block in range(g_w_fc.shape[0] // hidden):
        at = slice(block * hidden, (block + 1) * hidden)
        pack_ref[hidden:, at] = g_w_fc[at]
    gm_sum[...] = jnp.sum(g_m.astype(F32), 0, keepdims=True)
    gf_sum[...] = jnp.sum(g_f.astype(F32), 0, keepdims=True)


def attend_grads_kernel(o_ref, gy_ref, a_ref, gq_ref, gkv_ref, pack_ref, gy_sum, gq_sum, gv_sum):
    local = gq_ref.shape[1]
    g_y = gy_ref[...].reshape(-1, gy_ref.shape[-1])
    a_low = a_ref[...]
    g_q, g_k, g_v = gq_ref[...], gkv_ref[:, :local], gkv_ref[:, local:]
    pack_ref[:local] = cross(o_ref[...], g_y).astype(BF16)
    for index, grad in enumerate((g_q, g_k, g_v)):
        product = cross(a_low, grad).astype(BF16)
        for block in range(product.shape[0] // local):
            at = slice(block * local, (block + 1) * local)
            pack_ref[(index + 1) * local : (index + 2) * local, at] = product[at]
    gy_sum[...] = jnp.sum(g_y.astype(F32), 0, keepdims=True)
    gq_sum[...] = jnp.sum(g_q.astype(F32), 0, keepdims=True)
    gv_sum[...] = jnp.sum(g_v.astype(F32), 0, keepdims=True)


NEAR = {
    project_kernel: (0,),
    attend_kernel: (4,),
    row_kernel: (0,),
    forward_kernel: (0,),
    turn_kernel: (0,),
    turn_back_kernel: (0,),
    back_kernel: (0,),
    backward_kernel: (0,),
    output_back_kernel: (0,),
    query_back_kernel: (4,),
    key_back_kernel: (5,),
    end_grads_kernel: (1, 2),
    attend_grads_kernel: (1, 2),
}


def swap_all(value, axis):
    return lax.all_to_all(value, axis, 0, 0)


def cross(left, right):
    return lax.dot_general(left, right, (((0,), (0,)), ((), ())), preferred_element_type=F32)


CORE, DEPTH = 1, 2


def side_of(flip):
    return (lax.axis_index("dp") // flip) % 2


def swap(value, flip):
    return lax.ppermute(value, "dp", [(i, i ^ flip) for i in range(lax.axis_size("dp"))])


def after(value, event):
    return lax.optimization_barrier((value, event))[0]


def halve(value, flip, event=None, side=None):
    halves = value.reshape((2, value.shape[0] // 2) + value.shape[1:])
    side = side_of(flip) if side is None else side
    mine = lax.dynamic_index_in_dim(halves, side, 0, keepdims=False)
    got = swap(lax.dynamic_index_in_dim(halves, 1 - side, 0, keepdims=False), flip)
    got = got if event is None else after(got, event)
    return (mine.astype(F32) + got.astype(F32)).astype(BF16)


def rejoin(value, flip, side=None, event=None):
    got = swap(value, flip)
    got = got if event is None else after(got, event)
    side = side_of(flip) if side is None else side
    return jnp.concatenate((jnp.where(side, got, value), jnp.where(side, value, got)), 0)


def pair_sums(value, turn, events):
    place = lax.axis_index("dp")
    x_low, x_high = (place // 4) % 2, place // 8
    along_x = ((4, x_low ^ x_high), (12, x_high)) if turn else ((12, x_high), (4, x_low ^ x_high))
    steps = ((CORE, place % 2), (DEPTH, (place // 2) % 2)) + along_x
    for (flip, side), event in zip(steps, events):
        value = halve(value, flip, event, side)
    for flip, side in steps[:1:-1]:
        value = rejoin(value, flip, side)
    value = after(value, events[-1])
    for flip, side in steps[1::-1]:
        value = rejoin(value, flip, side)
    return value


def sum_over_x(values):
    groups = [[4 * x + rest for x in range(lax.axis_size("dp") // 4)] for rest in range(4)]
    return lax.psum(values, "dp", axis_index_groups=groups)


def swap_chips(value):
    groups = [[2 * chip + core for chip in range(lax.axis_size("dp") // 2)] for core in range(2)]
    return lax.all_to_all(value, "dp", 0, 0, axis_index_groups=groups)


def body(
    tokens,
    segment_ids,
    norm_gain,
    norm_bias,
    w_qkv,
    b_qv,
    w_out,
    b_out,
    w_fc,
    b_fc,
    w_proj,
    b_proj,
    cotangent,
):
    rows, width = tokens.shape
    total = segment_ids.shape[0]
    layers = w_qkv.shape[0]
    local = w_qkv.shape[3]
    hidden = w_fc.shape[2]
    ranks, slots = lax.axis_size("dp"), lax.axis_size("tensor")
    share = rows // slots
    first = (lax.axis_index("dp") * rows).astype(jnp.int32)
    own = lax.axis_index("tensor") * share
    start = first.reshape(1)
    seg_own = lax.dynamic_slice_in_dim(segment_ids, first, rows).reshape(rows, 1)
    seg_all = segment_ids.reshape(1, total)
    spots = (start, seg_own, seg_all)
    gains = norm_gain.astype(F32).reshape(layers, 2, 1, width)
    shifts = norm_bias.astype(F32).reshape(layers, 2, 1, width)
    out_bias = b_out.astype(F32).reshape(layers, 1, width)
    end_bias = b_proj.astype(F32).reshape(layers, 1, width)
    w_three = w_qkv.transpose(0, 2, 1, 3)
    fc_bias = b_fc.reshape(layers, 1, hidden)
    state = lax.dynamic_slice_in_dim(tokens, own, share).astype(F32)
    a_normed, a_factor = norm_parts(state)
    a_factor = jnp.broadcast_to(a_factor, (share, 128))
    row_block = shape((share, width), F32)
    row_stat = shape((share, 128), F32)
    exchange = shape((slots, share, width), BF16)
    saved = []
    qkv_shapes = [
        shape((rows, local), BF16),
        shape((rows, 2 * local), BF16),
        shape((ranks, rows, 2 * local), BF16),
    ]
    a_low = None
    for layer in range(layers):
        if layer:
            q_low, kv_own, kv_sent = call(project_kernel, qkv_shapes, (layer, (1, 2)), a_low, w_three, b_qv)
        else:
            a_low, q_low, kv_own, kv_sent = call(
                first_kernel,
                [shape((rows, width), BF16)] + qkv_shapes,
                (layer, (3, 4)),
                tokens,
                gains[0, 0],
                shifts[0, 0],
                w_three,
                b_qv,
            )
        kv_all = swap_all(kv_sent, "dp")
        o_full, o_low, logs, attn_parts = call(
            attend_kernel,
            [shape((rows, local), F32), shape((rows, local), BF16), shape((rows, local), F32), exchange],
            (layer, (5,)),
            *spots,
            q_low,
            kv_all,
            w_out,
            room=24,
        )
        middle, b_normed, b_factor, b_sent = call(
            row_kernel,
            [row_block, row_block, row_stat, exchange],
            (layer, ()),
            swap_all(attn_parts, "tensor"),
            state,
            out_bias[layer],
            gains[layer, 1],
            shifts[layer, 1],
        )
        b_low = swap_all(b_sent, "tensor").reshape(rows, width)
        kept = [a_normed, a_factor, a_low, q_low, kv_own, kv_all, o_full, o_low, logs, b_normed, b_factor, b_low]
        if layer < layers - 1:
            pre, h_low, parts = call(
                forward_kernel,
                [shape((rows, hidden), F32), shape((rows, hidden), BF16), exchange],
                (layer, (1, 2, 3)),
                b_low,
                w_fc,
                fc_bias,
                w_proj,
            )
            state, a_normed, a_factor, a_sent = call(
                row_kernel,
                [row_block, row_block, row_stat, exchange],
                (layer, ()),
                swap_all(parts, "tensor"),
                middle,
                end_bias[layer],
                gains[layer + 1, 0],
                shifts[layer + 1, 0],
            )
            a_low = swap_all(a_sent, "tensor").reshape(rows, width)
            kept += [pre, h_low]
        saved.append(kept)
    q_every = lax.all_gather(jnp.concatenate([kept[3] for kept in saved], 1), "dp", axis=0, tiled=True)
    g_m = cotangent
    grad = lax.dynamic_slice_in_dim(cotangent, own, share).astype(F32)
    done = [None] * layers
    smalls, sums = [], []
    two_rows = shape((2, width), F32)
    out = None
    def end_grads(layer, h_low, g_m, b_low, g_f):
        return call(
            end_grads_kernel,
            [shape((2 * hidden, width), BF16), shape((1, width), F32), shape((1, hidden), F32)],
            (layer, ()),
            h_low,
            g_m,
            b_low,
            g_f,
            room=16,
        )

    for layer in reversed(range(layers)):
        a_normed, a_factor, a_low, q_low, kv_own, kv_all, o_full, o_low, logs, b_normed, b_factor, b_low = (
            saved[layer][:12]
        )
        if layer == layers - 1:
            double = shape((slots, 2 * share, width), BF16)
            h_low, g_f, parts = call(
                turn_kernel,
                [shape((rows, hidden), BF16), shape((rows, hidden), BF16), double],
                (layer, (1, 2, 3)),
                b_low,
                w_fc,
                fc_bias,
                w_proj,
                g_m,
            )
            grad, sums_b, sent = call(
                turn_back_kernel,
                [row_block, two_rows, double],
                (layer, ()),
                swap_all(parts, "tensor"),
                middle,
                end_bias[layer],
                b_normed,
                b_factor,
                gains[layer, 1],
                grad,
            )
            got = swap_all(sent, "tensor")
            g_y = got
            out = got[:, share:].reshape(rows, width).astype(F32)
        else:
            pre, h_low = saved[layer][12:]
            g_f, parts = call(
                backward_kernel,
                [shape((rows, hidden), BF16), exchange],
                (layer, (2, 3)),
                g_m,
                pre,
                w_fc,
                w_proj,
            )
            end_pack, gm_sum, gf_sum = end_grads(layer, h_low, g_m, b_low, g_f)
            grad, sums_b, sent = call(
                back_kernel,
                [row_block, two_rows, exchange],
                (layer, ()),
                swap_all(parts, "tensor"),
                b_normed,
                b_factor,
                gains[layer, 1],
                grad,
            )
            g_y = swap_all(sent, "tensor")
        grad_b = grad
        g_o, delta, sent = call(
            output_back_kernel,
            [shape((rows, local), BF16), shape((rows, local), F32), shape((ranks, rows + 16, local), BF16)],
            (layer, (1,)),
            g_y,
            w_out,
            o_full,
            logs,
            blocks={0: ((slots, share, width), lambda i: (0, 0, 0))},
        )
        go_all = swap_all(sent, "dp")
        (g_q,) = call(
            query_back_kernel,
            [shape((rows, local), BF16)],
            (layer, ()),
            *spots,
            q_low,
            kv_all,
            g_o,
            logs,
            delta,
            room=24,
        )
        g_kv, parts = call(
            key_back_kernel,
            [shape((rows, 2 * local), BF16), exchange],
            (layer, (7,)),
            *spots,
            kv_own,
            q_every,
            go_all,
            g_q,
            w_three,
            room=24,
            blocks={4: ((total, local), lambda i: (0, layer))},
        )
        grad, sums_a, sent = call(
            back_kernel,
            [row_block, two_rows, exchange],
            (layer, ()),
            swap_all(parts, "tensor"),
            a_normed,
            a_factor,
            gains[layer, 0],
            grad,
        )
        sums = [sums_a, sums_b] + sums
        if layer:
            end_pack, gm_sum, gf_sum = end_grads(layer, h_low, g_m, b_low, g_f)
        attend_pack, gy_sum, gq_sum, gv_sum = call(
            attend_grads_kernel,
            [
                shape((4 * local, width), BF16),
                shape((1, width), F32),
                shape((1, local), F32),
                shape((1, local), F32),
            ],
            (layer, ()),
            o_low,
            g_y,
            a_low,
            g_q,
            g_kv,
            room=16,
            blocks={1: ((slots, share, width), lambda i: (0, 0, 0))},
        )
        smalls = [gy_sum, gm_sum, gq_sum, gv_sum, gf_sum] + smalls
        if layer:
            g_m = swap_all(sent, "tensor").reshape(rows, width)
            end_part = halve(halve(end_pack, CORE, go_all), DEPTH, grad)
            attend_part = halve(halve(attend_pack, CORE), DEPTH, g_m)
            done[layer] = sum_over_x((end_part, attend_part))
    tail = jnp.concatenate([sent, jnp.broadcast_to(jnp.concatenate(sums, 0).astype(BF16), (slots, 8, width))], 1)
    tail_got = got = swap_all(tail, "tensor")
    grad_input = got[:, :share].reshape(rows, width).astype(F32)
    norm_sums = jnp.sum(got[:, share:].astype(F32), 0)
    small = jnp.concatenate([norm_sums.reshape(-1)] + [part.reshape(-1) for part in smalls])
    each = small.size // (8 * ranks)
    wide = 4 * width
    packed = jnp.concatenate(
        (
            attend_pack.reshape(ranks, 4, 8, width).transpose(0, 2, 1, 3).reshape(ranks, 8, wide),
            jnp.pad(small.astype(BF16).reshape(ranks, 8, each), ((0, 0), (0, 0), (0, 128 - each))),
        ),
        2,
    )
    half = halve(packed, CORE)
    arrived = swap_chips(half)
    mine = jnp.sum(arrived.astype(F32), 0).astype(BF16)
    got = rejoin(swap_chips(jnp.broadcast_to(mine, (ranks // 2,) + mine.shape)), CORE)
    attend_pack = got[:, :, :wide].reshape(ranks, 8, 4, width).transpose(0, 2, 1, 3).reshape(attend_pack.shape)
    events = (grad_b, g_o, g_kv, grad, half)
    end_pack = jnp.concatenate(
        [pair_sums(part, turn, events) for turn, part in enumerate((end_pack[:hidden], end_pack[hidden:]))], 0
    )
    ends, attends = [
        [mine, rejoin(rejoin(after(part, grad), DEPTH, None, half), CORE)]
        for mine, part in zip((end_pack, attend_pack), done[1])
    ]

    small = got[:, :, wide : wide + each].reshape(-1).astype(F32)
    norm_grads = small[: 8 * width].reshape(layers, 2, 2, width)
    per_layer = small[8 * width :].reshape(layers, -1)
    cut = 2 * width

    def spread(pack):
        blocks = width // (pack.shape[-2])
        return pack.reshape(pack.shape[:-1] + (blocks, -1)).swapaxes(-3, -2).reshape(pack.shape[:-2] + (width, -1))

    g_w_proj = jnp.stack([pack[:hidden] for pack in ends]).astype(F32)
    g_w_fc = jnp.stack([spread(pack[hidden:]) for pack in ends]).astype(F32)
    g_w_out = jnp.stack([pack[:local] for pack in attends]).astype(F32)
    g_w_qkv = jnp.stack([spread(pack[local:].reshape(3, local, width)) for pack in attends]).astype(F32)

    return (
        out,
        grad_input,
        norm_grads[:, :, 0],
        norm_grads[:, :, 1],
        g_w_qkv.transpose(0, 2, 1, 3),
        per_layer[:, cut : cut + 2 * local].reshape(layers, 2, local),
        g_w_out,
        per_layer[:, :width],
        g_w_fc,
        per_layer[:, cut + 2 * local :],
        g_w_proj,
        per_layer[:, width:cut],
    )


def solution(mesh):
    in_specs = (
        P("dp", None),
        P(),
        P(),
        P(),
        P(None, None, None, "tensor"),
        P(None, None, "tensor"),
        P(None, "tensor", None),
        P(),
        P(None, None, "tensor"),
        P(None, "tensor"),
        P(None, "tensor", None),
        P(),
        P("dp", None),
    )
    out_specs = (
        P("dp", None),
        P("dp", None),
        P(),
        P(),
        P(None, None, None, "tensor"),
        P(None, None, "tensor"),
        P(None, "tensor", None),
        P(),
        P(None, None, "tensor"),
        P(None, "tensor"),
        P(None, "tensor", None),
        P(),
    )
    return jax.shard_map(body, mesh=mesh, in_specs=in_specs, out_specs=out_specs, check_vma=False)
```

```python
import functools

import jax
import jax.numpy as jnp
from jax import lax
from jax.experimental import pallas as pl
from jax.experimental.pallas import tpu as pltpu
from jax.sharding import PartitionSpec as P

HD = 64
F32 = jnp.float32
BF16 = jnp.bfloat16
ROOT = 0.7978845608028654
CUBE = 0.044715


def dot(left, right):
    return jnp.dot(left, right, preferred_element_type=F32)


def dot_t(left, right):
    return lax.dot_general(left, right, (((1,), (1,)), ((), ())), preferred_element_type=F32)


def norm_parts(value):
    mean = jnp.mean(value, -1, keepdims=True)
    centered = value - mean
    spread = jnp.mean(centered * centered, -1, keepdims=True)
    factor = lax.rsqrt(spread + 1e-05)
    return centered * factor, factor


def tanh_part(value):
    return jnp.tanh(ROOT * (value + CUBE * value * value * value))


def gelu(value):
    return 0.5 * value * (1.0 + tanh_part(value))


def gelu_slope(value):
    bend = tanh_part(value)
    inner = ROOT * (1.0 + 3.0 * CUBE * value * value)
    return 0.5 * (1.0 + bend) + 0.5 * value * (1.0 - bend * bend) * inner


def call(kernel, outs, layered, *args, room=12, blocks={}):
    layer, wide = layered
    near = NEAR.get(kernel, ())
    args = [
        arg if index in near or arg.shape == (1,) else pltpu.with_memory_space_constraint(arg, pltpu.HBM)
        for index, arg in enumerate(args)
    ]

    def spec(index, arg):
        if arg.dtype == jnp.int32 and arg.shape == (1,):
            return pl.BlockSpec(memory_space=pltpu.SMEM)
        if index in blocks:
            return pl.BlockSpec(*blocks[index])
        if index in wide:
            rest = arg.shape[1:]
            return pl.BlockSpec((None,) + rest, lambda i: (layer,) + (0,) * len(rest))
        return pl.BlockSpec(arg.shape, lambda i: (0,) * arg.ndim)

    return pl.pallas_call(
        kernel,
        grid=(1,),
        in_specs=[spec(index, arg) for index, arg in enumerate(args)],
        out_specs=[pl.BlockSpec(out.shape, lambda i, n=len(out.shape): (0,) * n) for out in outs],
        out_shape=[pltpu.HBM(out.shape, out.dtype) for out in outs],
        cost_estimate=pl.CostEstimate(flops=1000, bytes_accessed=1000, transcendentals=0),
        compiler_params=pltpu.CompilerParams(vmem_limit_bytes=room * 1024 * 1024),
    )(*args)


def shape(dims, kind):
    return jax.ShapeDtypeStruct(dims, kind)


def project(a_low, w_ref, bias_ref, q_ref, kv_ref, all_ref):
    q_ref[...] = (dot(a_low, w_ref[0]) + bias_ref[0:1].astype(F32)).astype(BF16)
    k_low = dot(a_low, w_ref[1]).astype(BF16)
    v_low = (dot(a_low, w_ref[2]) + bias_ref[1:2].astype(F32)).astype(BF16)
    local = k_low.shape[1]
    kv_ref[:, :local] = k_low
    kv_ref[:, local:] = v_low
    for index in range(all_ref.shape[0]):
        all_ref[index, :, :local] = k_low
        all_ref[index, :, local:] = v_low


def first_kernel(x_ref, gain_ref, shift_ref, w_ref, bias_ref, a_ref, q_ref, kv_ref, all_ref):
    normed, _ = norm_parts(x_ref[...].astype(F32))
    a_low = (normed * gain_ref[...] + shift_ref[...]).astype(BF16)
    a_ref[...] = a_low
    project(a_low, w_ref, bias_ref, q_ref, kv_ref, all_ref)


def project_kernel(a_ref, w_ref, bias_ref, q_ref, kv_ref, all_ref):
    project(a_ref[...], w_ref, bias_ref, q_ref, kv_ref, all_ref)


def head_masks(rows, local):
    column = lax.broadcasted_iota(jnp.int32, (rows, local), 1)
    return [column < HD, column >= HD]


def only(mask, value):
    return jnp.where(mask, value.astype(F32), 0.0).astype(BF16)


def allowed_of(start_ref, own_ref, all_ref, own_is_query):
    own_spot = start_ref[0] + lax.broadcasted_iota(jnp.int32, own_ref.shape, 0)
    spots = lax.broadcasted_iota(jnp.int32, all_ref.shape, 1)
    order = spots <= own_spot if own_is_query else spots >= own_spot
    return (all_ref[...] == own_ref[...]) & order


def attend_kernel(start_ref, own_ref, all_ref, q_ref, kv_ref, w_ref, o_ref, low_ref, log_ref, part_ref):
    rows, local = q_ref.shape
    total = all_ref.shape[1]
    keys = kv_ref[:, :, :local].reshape(total, local)
    values = kv_ref[:, :, local:].reshape(total, local)
    allowed = allowed_of(start_ref, own_ref, all_ref, True)
    queries = q_ref[...].astype(F32) * HD ** (-0.5)
    masks = head_masks(rows, local)
    outs, logs = [], []
    for mask in masks:
        scores = jnp.where(allowed, dot_t(only(mask, queries), keys), -1e30)
        top = jnp.max(scores, -1, keepdims=True)
        expd = jnp.exp(scores - top)
        denom = jnp.sum(expd, -1, keepdims=True)
        outs.append(dot((expd * (1.0 / denom)).astype(BF16), values))
        logs.append(top + jnp.log(denom))
    attended = jnp.where(masks[0], outs[0], outs[1])
    o_low = attended.astype(BF16)
    o_ref[...] = attended
    low_ref[...] = o_low
    log_ref[...] = jnp.where(masks[0], logs[0], logs[1])
    part_ref[...] = dot(o_low, w_ref[...]).astype(BF16).reshape(part_ref.shape)


def sum_parts(ref, start, rows):
    total = ref[0, start : start + rows].astype(F32)
    for index in range(1, ref.shape[0]):
        total = total + ref[index, start : start + rows].astype(F32)
    return total


def row_kernel(parts_ref, state_ref, bias_ref, gain_ref, shift_ref, state_out, normed_ref, factor_ref, sent_ref):
    state = state_ref[...] + (sum_parts(parts_ref, 0, state_ref.shape[0]) + bias_ref[...])
    normed, factor = norm_parts(state)
    low = (normed * gain_ref[...] + shift_ref[...]).astype(BF16)
    state_out[...] = state
    normed_ref[...] = normed
    factor_ref[...] = jnp.broadcast_to(factor, factor_ref.shape)
    for index in range(sent_ref.shape[0]):
        sent_ref[index] = low


def forward_kernel(b_ref, fc_ref, bias_ref, proj_ref, pre_ref, h_ref, part_ref):
    pre = dot(b_ref[...], fc_ref[...]) + bias_ref[...].astype(F32)
    h_low = gelu(pre).astype(BF16)
    pre_ref[...] = pre
    h_ref[...] = h_low
    part_ref[...] = dot(h_low, proj_ref[...]).astype(BF16).reshape(part_ref.shape)


def turn_kernel(b_ref, fc_ref, bias_ref, proj_ref, g_ref, h_ref, gf_ref, part_ref):
    share = part_ref.shape[1] // 2
    pre = dot(b_ref[...], fc_ref[...]) + bias_ref[...].astype(F32)
    h_low = gelu(pre).astype(BF16)
    h_ref[...] = h_low
    parts = dot(h_low, proj_ref[...]).astype(BF16)
    part_ref[:, :share] = parts.reshape(-1, share, parts.shape[1])
    g_f = (dot_t(g_ref[...], proj_ref[...]) * gelu_slope(pre)).astype(BF16)
    gf_ref[...] = g_f
    parts = dot_t(g_f, fc_ref[...]).astype(BF16)
    part_ref[:, share:] = parts.reshape(-1, share, parts.shape[1])


def backward_kernel(g_ref, pre_ref, fc_ref, proj_ref, gf_ref, part_ref):
    g_f = (dot_t(g_ref[...], proj_ref[...]) * gelu_slope(pre_ref[...])).astype(BF16)
    gf_ref[...] = g_f
    part_ref[...] = dot_t(g_f, fc_ref[...]).astype(BF16).reshape(part_ref.shape)


def norm_back(d_value, normed_ref, factor_ref, gain_ref, grad_ref, sums_ref):
    normed = normed_ref[...]
    scaled = d_value * gain_ref[...]
    back = factor_ref[:, 0:1] * (
        scaled
        - jnp.mean(scaled, -1, keepdims=True)
        - normed * jnp.mean(scaled * normed, -1, keepdims=True)
    )
    sums_ref[0:1] = jnp.sum(d_value * normed, 0, keepdims=True)
    sums_ref[1:2] = jnp.sum(d_value, 0, keepdims=True)
    return grad_ref[...] + back


def back_kernel(parts_ref, normed_ref, factor_ref, gain_ref, grad_ref, grad_out, sums_ref, sent_ref):
    share = normed_ref.shape[0]
    grad = norm_back(sum_parts(parts_ref, 0, share), normed_ref, factor_ref, gain_ref, grad_ref, sums_ref)
    grad_out[...] = grad
    low = grad.astype(BF16)
    for index in range(sent_ref.shape[0]):
        sent_ref[index] = low


def turn_back_kernel(
    parts_ref, state_ref, bias_ref, normed_ref, factor_ref, gain_ref, grad_ref, grad_out, sums_ref, sent_ref
):
    share = normed_ref.shape[0]
    out = (state_ref[...] + (sum_parts(parts_ref, 0, share) + bias_ref[...])).astype(BF16)
    grad = norm_back(sum_parts(parts_ref, share, share), normed_ref, factor_ref, gain_ref, grad_ref, sums_ref)
    grad_out[...] = grad
    low = grad.astype(BF16)
    for index in range(sent_ref.shape[0]):
        sent_ref[index, :share] = low
        sent_ref[index, share:] = out


def two_terms(value):
    high = value.astype(BF16).astype(F32)
    return high, value - high


def output_back_kernel(gy_ref, w_ref, o_ref, log_ref, go_ref, delta_ref, sent_ref):
    rows, local = o_ref.shape
    g_o = dot_t(gy_ref[...].reshape(rows, -1), w_ref[...]).astype(BF16)
    go_ref[...] = g_o
    masks = head_masks(rows, local)
    product = g_o.astype(F32) * o_ref[...]
    deltas = [jnp.sum(jnp.where(mask, product, 0.0), -1, keepdims=True) for mask in masks]
    delta = jnp.where(masks[0], deltas[0], deltas[1])
    delta_ref[...] = delta
    rows_of = []
    for value in (log_ref[...], delta):
        turned = value.T
        high, rest = two_terms(jnp.concatenate((turned[0:1], turned[HD : HD + 1]), 0))
        rows_of += [high, rest]
    rows_of.append(jnp.zeros((8, local), F32))
    extra = jnp.concatenate(rows_of, 0).astype(BF16)
    for index in range(sent_ref.shape[0]):
        sent_ref[index, :rows] = g_o
        sent_ref[index, rows:] = extra


def query_back_kernel(start_ref, own_ref, all_ref, q_ref, kv_ref, go_ref, log_ref, delta_ref, gq_ref):
    rows, local = q_ref.shape
    total = all_ref.shape[1]
    keys = kv_ref[:, :, :local].reshape(total, local)
    values = kv_ref[:, :, local:].reshape(total, local)
    allowed = allowed_of(start_ref, own_ref, all_ref, True)
    queries = q_ref[...].astype(F32) * HD ** (-0.5)
    masks = head_masks(rows, local)
    outs = []
    for head, mask in enumerate(masks):
        at = slice(head * HD, head * HD + 1)
        scores = jnp.where(allowed, dot_t(only(mask, queries), keys), -1e30)
        probs = jnp.exp(scores - log_ref[:, at])
        d_probs = dot_t(only(mask, go_ref[...]), values)
        g_s = (probs * (d_probs - delta_ref[:, at])).astype(BF16)
        outs.append(dot(g_s, keys))
    gq_ref[...] = (jnp.where(masks[0], outs[0], outs[1]) * HD ** (-0.5)).astype(BF16)


def key_back_kernel(start_ref, own_ref, all_ref, kv_ref, q_ref, got_ref, gq_ref, w_ref, gkv_ref, part_ref):
    rows, twice = kv_ref.shape
    local = twice // 2
    total = all_ref.shape[1]
    allowed = allowed_of(start_ref, own_ref, all_ref, False)
    queries = q_ref[...]
    g_o = got_ref[:, :rows].reshape(total, local)
    extra = got_ref[:, rows:].astype(F32)
    keys = kv_ref[:, :local].astype(F32) * HD ** (-0.5)
    values = kv_ref[:, local:]
    masks = head_masks(rows, local)
    d_keys, d_values = [], []
    for head, mask in enumerate(masks):

        def row_of(base):
            row = extra[:, base + head : base + head + 1] + extra[:, base + 2 + head : base + 3 + head]
            return jnp.concatenate([row[index] for index in range(row.shape[0])], 1)

        scores = jnp.where(allowed, dot_t(only(mask, keys), queries), -1e30)
        probs = jnp.exp(scores - row_of(0))
        d_probs = dot_t(only(mask, values), g_o)
        g_s = (probs * (d_probs - row_of(4))).astype(BF16)
        d_keys.append(dot(g_s, queries))
        d_values.append(dot(probs.astype(BF16), g_o))
    g_k = (jnp.where(masks[0], d_keys[0], d_keys[1]) * HD ** (-0.5)).astype(BF16)
    g_v = jnp.where(masks[0], d_values[0], d_values[1]).astype(BF16)
    gkv_ref[:, :local] = g_k
    gkv_ref[:, local:] = g_v
    part = dot_t(gq_ref[...], w_ref[0]) + dot_t(g_k, w_ref[1]) + dot_t(g_v, w_ref[2])
    part_ref[...] = part.astype(BF16).reshape(part_ref.shape)


def end_grads_kernel(h_ref, gm_ref, b_ref, gf_ref, pack_ref, gm_sum, gf_sum):
    g_m, g_f = gm_ref[...], gf_ref[...]
    hidden = g_f.shape[1]
    pack_ref[:hidden] = cross(h_ref[...], g_m).astype(BF16)
    g_w_fc = cross(b_ref[...], g_f).astype(BF16)
    for block in range(g_w_fc.shape[0] // hidden):
        at = slice(block * hidden, (block + 1) * hidden)
        pack_ref[hidden:, at] = g_w_fc[at]
    gm_sum[...] = jnp.sum(g_m.astype(F32), 0, keepdims=True)
    gf_sum[...] = jnp.sum(g_f.astype(F32), 0, keepdims=True)


def attend_grads_kernel(o_ref, gy_ref, a_ref, gq_ref, gkv_ref, pack_ref, gy_sum, gq_sum, gv_sum):
    local = gq_ref.shape[1]
    g_y = gy_ref[...].reshape(-1, gy_ref.shape[-1])
    a_low = a_ref[...]
    g_q, g_k, g_v = gq_ref[...], gkv_ref[:, :local], gkv_ref[:, local:]
    pack_ref[:local] = cross(o_ref[...], g_y).astype(BF16)
    for index, grad in enumerate((g_q, g_k, g_v)):
        product = cross(a_low, grad).astype(BF16)
        for block in range(product.shape[0] // local):
            at = slice(block * local, (block + 1) * local)
            pack_ref[(index + 1) * local : (index + 2) * local, at] = product[at]
    gy_sum[...] = jnp.sum(g_y.astype(F32), 0, keepdims=True)
    gq_sum[...] = jnp.sum(g_q.astype(F32), 0, keepdims=True)
    gv_sum[...] = jnp.sum(g_v.astype(F32), 0, keepdims=True)


def finish_end_kernel(side_ref, p_own, p_got, f_own, f_got, own_ref, got_ref, proj_ref, fc_ref):
    side = side_ref[0]
    half = p_own.shape[0]
    hidden = fc_ref.shape[2]

    def pick(own, got, index):
        return jnp.where(side == index, own[...].astype(F32), got[...].astype(F32))

    for index in range(2):
        rows = slice(index * half, (index + 1) * half)
        proj_ref[0, rows] = pick(p_own, p_got, index)
        packed = pick(f_own, f_got, index)
        for block in range(fc_ref.shape[1] // hidden):
            at = block * hidden + index * half
            fc_ref[0, at : at + half] = packed[:, block * hidden : (block + 1) * hidden]
    proj_ref[1] = pick(own_ref, got_ref, 0)
    packed = pick(own_ref, got_ref, 1)
    for block in range(fc_ref.shape[1] // hidden):
        at = slice(block * hidden, (block + 1) * hidden)
        fc_ref[1, at] = packed[:, at]


def finish_attend_kernel(side_ref, late_own, late_got, own_ref, got_ref, out_ref, qkv_ref):
    side = side_ref[0]
    local, width = out_ref.shape[1:]

    def put(layer, row, value):
        count = value.shape[0]
        if row < local:
            out_ref[layer, row : row + count] = value
        else:
            index, at = row // local - 1, row % local
            for block in range(width // local):
                base = block * local + at
                qkv_ref[layer, index, base : base + count] = value[:, block * local : (block + 1) * local]

    half = own_ref.shape[0]
    for index in range(2):
        picked = jnp.where(side == index, own_ref[...].astype(F32), got_ref[...].astype(F32))
        for row in range(0, half, local):
            put(1, index * half + row, picked[row : row + local])
        for chip in range(late_own.shape[0]):
            picked = jnp.where(side == index, late_own[chip].astype(F32), late_got[chip].astype(F32))
            for group in range(4):
                row = index * half + chip * 32 + group * 8
                put(0, row, picked[:, group * width : (group + 1) * width])


NEAR = {
    project_kernel: (0,),
    attend_kernel: (4,),
    row_kernel: (0,),
    forward_kernel: (0,),
    turn_kernel: (0,),
    turn_back_kernel: (0,),
    back_kernel: (0,),
    backward_kernel: (0,),
    output_back_kernel: (0,),
    query_back_kernel: (4,),
    key_back_kernel: (5,),
    end_grads_kernel: (1, 2),
    attend_grads_kernel: (1, 2),
}


def swap_all(value, axis):
    return lax.all_to_all(value, axis, 0, 0)


def cross(left, right):
    return lax.dot_general(left, right, (((0,), (0,)), ((), ())), preferred_element_type=F32)


CORE, DEPTH = 1, 2


def side_of(flip):
    return (lax.axis_index("dp") // flip) % 2


def swap(value, flip):
    return lax.ppermute(value, "dp", [(i, i ^ flip) for i in range(lax.axis_size("dp"))])


def after(value, event):
    return lax.optimization_barrier((value, event))[0]


def halve(value, flip, event=None, side=None):
    halves = value.reshape((2, value.shape[0] // 2) + value.shape[1:])
    side = side_of(flip) if side is None else side
    mine = lax.dynamic_index_in_dim(halves, side, 0, keepdims=False)
    got = swap(lax.dynamic_index_in_dim(halves, 1 - side, 0, keepdims=False), flip)
    got = got if event is None else after(got, event)
    return (mine.astype(F32) + got.astype(F32)).astype(BF16)


def rejoin(value, flip, side=None, event=None):
    got = swap(value, flip)
    got = got if event is None else after(got, event)
    side = side_of(flip) if side is None else side
    return jnp.concatenate((jnp.where(side, got, value), jnp.where(side, value, got)), 0)


def finish_sums(value, turn, events):
    place = lax.axis_index("dp")
    x_low, x_high = (place // 4) % 2, place // 8
    steps = ((4, x_low ^ x_high), (12, x_high)) if turn else ((12, x_high), (4, x_low ^ x_high))
    for (flip, side), event in zip(steps, events):
        value = halve(value, flip, event, side)
    for flip, side in steps[::-1]:
        value = rejoin(value, flip, side)
    value = rejoin(after(value, events[-1]), DEPTH)
    return value, swap(value, CORE)


def sum_over_x(values):
    groups = [[4 * x + rest for x in range(lax.axis_size("dp") // 4)] for rest in range(4)]
    return lax.psum(values, "dp", axis_index_groups=groups)


def swap_chips(value):
    groups = [[2 * chip + core for chip in range(lax.axis_size("dp") // 2)] for core in range(2)]
    return lax.all_to_all(value, "dp", 0, 0, axis_index_groups=groups)


def body(
    tokens,
    segment_ids,
    norm_gain,
    norm_bias,
    w_qkv,
    b_qv,
    w_out,
    b_out,
    w_fc,
    b_fc,
    w_proj,
    b_proj,
    cotangent,
):
    rows, width = tokens.shape
    total = segment_ids.shape[0]
    layers = w_qkv.shape[0]
    local = w_qkv.shape[3]
    hidden = w_fc.shape[2]
    ranks, slots = lax.axis_size("dp"), lax.axis_size("tensor")
    share = rows // slots
    first = (lax.axis_index("dp") * rows).astype(jnp.int32)
    own = lax.axis_index("tensor") * share
    start = first.reshape(1)
    seg_own = lax.dynamic_slice_in_dim(segment_ids, first, rows).reshape(rows, 1)
    seg_all = segment_ids.reshape(1, total)
    spots = (start, seg_own, seg_all)
    gains = norm_gain.astype(F32).reshape(layers, 2, 1, width)
    shifts = norm_bias.astype(F32).reshape(layers, 2, 1, width)
    out_bias = b_out.astype(F32).reshape(layers, 1, width)
    end_bias = b_proj.astype(F32).reshape(layers, 1, width)
    w_three = w_qkv.transpose(0, 2, 1, 3)
    fc_bias = b_fc.reshape(layers, 1, hidden)
    state = lax.dynamic_slice_in_dim(tokens, own, share).astype(F32)
    a_normed, a_factor = norm_parts(state)
    a_factor = jnp.broadcast_to(a_factor, (share, 128))
    row_block = shape((share, width), F32)
    row_stat = shape((share, 128), F32)
    exchange = shape((slots, share, width), BF16)
    saved = []
    qkv_shapes = [
        shape((rows, local), BF16),
        shape((rows, 2 * local), BF16),
        shape((ranks, rows, 2 * local), BF16),
    ]
    a_low = None
    for layer in range(layers):
        if layer:
            q_low, kv_own, kv_sent = call(project_kernel, qkv_shapes, (layer, (1, 2)), a_low, w_three, b_qv)
        else:
            a_low, q_low, kv_own, kv_sent = call(
                first_kernel,
                [shape((rows, width), BF16)] + qkv_shapes,
                (layer, (3, 4)),
                tokens,
                gains[0, 0],
                shifts[0, 0],
                w_three,
                b_qv,
            )
        kv_all = swap_all(kv_sent, "dp")
        o_full, o_low, logs, attn_parts = call(
            attend_kernel,
            [shape((rows, local), F32), shape((rows, local), BF16), shape((rows, local), F32), exchange],
            (layer, (5,)),
            *spots,
            q_low,
            kv_all,
            w_out,
            room=24,
        )
        middle, b_normed, b_factor, b_sent = call(
            row_kernel,
            [row_block, row_block, row_stat, exchange],
            (layer, ()),
            swap_all(attn_parts, "tensor"),
            state,
            out_bias[layer],
            gains[layer, 1],
            shifts[layer, 1],
        )
        b_low = swap_all(b_sent, "tensor").reshape(rows, width)
        kept = [a_normed, a_factor, a_low, q_low, kv_own, kv_all, o_full, o_low, logs, b_normed, b_factor, b_low]
        if layer < layers - 1:
            pre, h_low, parts = call(
                forward_kernel,
                [shape((rows, hidden), F32), shape((rows, hidden), BF16), exchange],
                (layer, (1, 2, 3)),
                b_low,
                w_fc,
                fc_bias,
                w_proj,
            )
            state, a_normed, a_factor, a_sent = call(
                row_kernel,
                [row_block, row_block, row_stat, exchange],
                (layer, ()),
                swap_all(parts, "tensor"),
                middle,
                end_bias[layer],
                gains[layer + 1, 0],
                shifts[layer + 1, 0],
            )
            a_low = swap_all(a_sent, "tensor").reshape(rows, width)
            kept += [pre, h_low]
        saved.append(kept)
    q_every = lax.all_gather(jnp.concatenate([kept[3] for kept in saved], 1), "dp", axis=0, tiled=True)
    g_m = cotangent
    grad = lax.dynamic_slice_in_dim(cotangent, own, share).astype(F32)
    done = [None] * layers
    smalls, sums = [], []
    two_rows = shape((2, width), F32)
    out = None
    def end_grads(layer, h_low, g_m, b_low, g_f):
        return call(
            end_grads_kernel,
            [shape((2 * hidden, width), BF16), shape((1, width), F32), shape((1, hidden), F32)],
            (layer, ()),
            h_low,
            g_m,
            b_low,
            g_f,
            room=16,
        )

    for layer in reversed(range(layers)):
        a_normed, a_factor, a_low, q_low, kv_own, kv_all, o_full, o_low, logs, b_normed, b_factor, b_low = (
            saved[layer][:12]
        )
        if layer == layers - 1:
            double = shape((slots, 2 * share, width), BF16)
            h_low, g_f, parts = call(
                turn_kernel,
                [shape((rows, hidden), BF16), shape((rows, hidden), BF16), double],
                (layer, (1, 2, 3)),
                b_low,
                w_fc,
                fc_bias,
                w_proj,
                g_m,
            )
            grad, sums_b, sent = call(
                turn_back_kernel,
                [row_block, two_rows, double],
                (layer, ()),
                swap_all(parts, "tensor"),
                middle,
                end_bias[layer],
                b_normed,
                b_factor,
                gains[layer, 1],
                grad,
            )
            got = swap_all(sent, "tensor")
            g_y = got
            out = got[:, share:].reshape(rows, width).astype(F32)
        else:
            pre, h_low = saved[layer][12:]
            g_f, parts = call(
                backward_kernel,
                [shape((rows, hidden), BF16), exchange],
                (layer, (2, 3)),
                g_m,
                pre,
                w_fc,
                w_proj,
            )
            end_pack, gm_sum, gf_sum = end_grads(layer, h_low, g_m, b_low, g_f)
            grad, sums_b, sent = call(
                back_kernel,
                [row_block, two_rows, exchange],
                (layer, ()),
                swap_all(parts, "tensor"),
                b_normed,
                b_factor,
                gains[layer, 1],
                grad,
            )
            g_y = swap_all(sent, "tensor")
        grad_b = grad
        g_o, delta, sent = call(
            output_back_kernel,
            [shape((rows, local), BF16), shape((rows, local), F32), shape((ranks, rows + 16, local), BF16)],
            (layer, (1,)),
            g_y,
            w_out,
            o_full,
            logs,
            blocks={0: ((slots, share, width), lambda i: (0, 0, 0))},
        )
        if not layer:
            starts = [
                halve(halve(part, CORE), DEPTH) for part in (end_pack[:hidden], end_pack[hidden:])
            ]
            sent, starts = lax.optimization_barrier((sent, starts))
        go_all = swap_all(sent, "dp")
        (g_q,) = call(
            query_back_kernel,
            [shape((rows, local), BF16)],
            (layer, ()),
            *spots,
            q_low,
            kv_all,
            g_o,
            logs,
            delta,
            room=24,
        )
        g_kv, parts = call(
            key_back_kernel,
            [shape((rows, 2 * local), BF16), exchange],
            (layer, (7,)),
            *spots,
            kv_own,
            q_every,
            go_all,
            g_q,
            w_three,
            room=24,
            blocks={4: ((total, local), lambda i: (0, layer))},
        )
        grad, sums_a, sent = call(
            back_kernel,
            [row_block, two_rows, exchange],
            (layer, ()),
            swap_all(parts, "tensor"),
            a_normed,
            a_factor,
            gains[layer, 0],
            grad,
        )
        sums = [sums_a, sums_b] + sums
        if layer:
            end_pack, gm_sum, gf_sum = end_grads(layer, h_low, g_m, b_low, g_f)
        attend_pack, gy_sum, gq_sum, gv_sum = call(
            attend_grads_kernel,
            [
                shape((4 * local, width), BF16),
                shape((1, width), F32),
                shape((1, local), F32),
                shape((1, local), F32),
            ],
            (layer, ()),
            o_low,
            g_y,
            a_low,
            g_q,
            g_kv,
            room=16,
            blocks={1: ((slots, share, width), lambda i: (0, 0, 0))},
        )
        smalls = [gy_sum, gm_sum, gq_sum, gv_sum, gf_sum] + smalls
        if layer:
            g_m = swap_all(sent, "tensor").reshape(rows, width)
            end_part = halve(halve(end_pack, CORE, go_all), DEPTH, grad)
            attend_part = halve(halve(attend_pack, CORE), DEPTH, g_m)
            done[layer] = sum_over_x((end_part, attend_part))
    tail = jnp.concatenate([sent, jnp.broadcast_to(jnp.concatenate(sums, 0).astype(BF16), (slots, 8, width))], 1)
    tail_got = got = swap_all(tail, "tensor")
    grad_input = got[:, :share].reshape(rows, width).astype(F32)
    norm_sums = jnp.sum(got[:, share:].astype(F32), 0)
    small = jnp.concatenate([norm_sums.reshape(-1)] + [part.reshape(-1) for part in smalls])
    each = small.size // (8 * ranks)
    wide = 4 * width
    packed = jnp.concatenate(
        (
            attend_pack.reshape(ranks, 4, 8, width).transpose(0, 2, 1, 3).reshape(ranks, 8, wide),
            jnp.pad(small.astype(BF16).reshape(ranks, 8, each), ((0, 0), (0, 0), (0, 128 - each))),
        ),
        2,
    )
    half = halve(packed, CORE)
    arrived = swap_chips(half)
    mine = jnp.sum(arrived.astype(F32), 0).astype(BF16)
    late = swap_chips(jnp.broadcast_to(mine, (ranks // 2,) + mine.shape))
    late_got = swap(late, CORE)
    events = (g_kv, grad, half)
    end_parts = [part for turn, value in enumerate(starts) for part in finish_sums(value, turn, events)]
    end_last, attend_last = [rejoin(after(part, grad), DEPTH, None, half) for part in done[1]]
    side = side_of(CORE)
    sides = side.astype(jnp.int32).reshape(1)
    g_w_proj, g_w_fc = call(
        finish_end_kernel,
        [shape((layers, hidden, width), F32), shape((layers, width, hidden), F32)],
        (0, ()),
        sides,
        *end_parts,
        end_last,
        swap(end_last, CORE),
        room=40,
    )
    g_w_out, g_w_qkv = call(
        finish_attend_kernel,
        [shape((layers, local, width), F32), shape((layers, 3, width, local), F32)],
        (0, ()),
        sides,
        late,
        late_got,
        attend_last,
        swap(attend_last, CORE),
        room=24,
    )
    ours, theirs = late[:, :, wide : wide + each], late_got[:, :, wide : wide + each]
    small = jnp.concatenate((jnp.where(side, theirs, ours), jnp.where(side, ours, theirs)), 0)
    small = small.reshape(-1).astype(F32)
    norm_grads = small[: 8 * width].reshape(layers, 2, 2, width)
    per_layer = small[8 * width :].reshape(layers, -1)
    cut = 2 * width

    return (
        out,
        grad_input,
        norm_grads[:, :, 0],
        norm_grads[:, :, 1],
        g_w_qkv.transpose(0, 2, 1, 3),
        per_layer[:, cut : cut + 2 * local].reshape(layers, 2, local),
        g_w_out,
        per_layer[:, :width],
        g_w_fc,
        per_layer[:, cut + 2 * local :],
        g_w_proj,
        per_layer[:, width:cut],
    )


def solution(mesh):
    in_specs = (
        P("dp", None),
        P(),
        P(),
        P(),
        P(None, None, None, "tensor"),
        P(None, None, "tensor"),
        P(None, "tensor", None),
        P(),
        P(None, None, "tensor"),
        P(None, "tensor"),
        P(None, "tensor", None),
        P(),
        P("dp", None),
    )
    out_specs = (
        P("dp", None),
        P("dp", None),
        P(),
        P(),
        P(None, None, None, "tensor"),
        P(None, None, "tensor"),
        P(None, "tensor", None),
        P(),
        P(None, None, "tensor"),
        P(None, "tensor"),
        P(None, "tensor", None),
        P(),
    )
    return jax.shard_map(body, mesh=mesh, in_specs=in_specs, out_specs=out_specs, check_vma=False)
```

```python
import functools

import jax
import jax.numpy as jnp
from jax import lax
from jax.experimental import pallas as pl
from jax.experimental.pallas import tpu as pltpu
from jax.sharding import PartitionSpec as P

HD = 64
F32 = jnp.float32
BF16 = jnp.bfloat16
ROOT = 0.7978845608028654
CUBE = 0.044715


def dot(left, right):
    return jnp.dot(left, right, preferred_element_type=F32)


def dot_t(left, right):
    return lax.dot_general(left, right, (((1,), (1,)), ((), ())), preferred_element_type=F32)


def norm_parts(value):
    mean = jnp.mean(value, -1, keepdims=True)
    centered = value - mean
    spread = jnp.mean(centered * centered, -1, keepdims=True)
    factor = lax.rsqrt(spread + 1e-05)
    return centered * factor, factor


def tanh_part(value):
    return jnp.tanh(ROOT * (value + CUBE * value * value * value))


def gelu(value):
    return 0.5 * value * (1.0 + tanh_part(value))


def gelu_slope(value):
    bend = tanh_part(value)
    inner = ROOT * (1.0 + 3.0 * CUBE * value * value)
    return 0.5 * (1.0 + bend) + 0.5 * value * (1.0 - bend * bend) * inner


def call(kernel, outs, layered, *args, room=12, blocks={}):
    layer, wide = layered
    near = NEAR.get(kernel, ())
    args = [
        arg if index in near or arg.shape == (1,) else pltpu.with_memory_space_constraint(arg, pltpu.HBM)
        for index, arg in enumerate(args)
    ]

    def spec(index, arg):
        if arg.dtype == jnp.int32 and arg.shape == (1,):
            return pl.BlockSpec(memory_space=pltpu.SMEM)
        if index in blocks:
            return pl.BlockSpec(*blocks[index])
        if index in wide:
            rest = arg.shape[1:]
            return pl.BlockSpec((None,) + rest, lambda i: (layer,) + (0,) * len(rest))
        return pl.BlockSpec(arg.shape, lambda i: (0,) * arg.ndim)

    return pl.pallas_call(
        kernel,
        grid=(1,),
        in_specs=[spec(index, arg) for index, arg in enumerate(args)],
        out_specs=[pl.BlockSpec(out.shape, lambda i, n=len(out.shape): (0,) * n) for out in outs],
        out_shape=[pltpu.HBM(out.shape, out.dtype) for out in outs],
        cost_estimate=pl.CostEstimate(flops=1000, bytes_accessed=1000, transcendentals=0),
        compiler_params=pltpu.CompilerParams(vmem_limit_bytes=room * 1024 * 1024),
    )(*args)


def shape(dims, kind):
    return jax.ShapeDtypeStruct(dims, kind)


def project(a_low, w_ref, bias_ref, q_ref, kv_ref, all_ref):
    q_ref[...] = (dot(a_low, w_ref[0]) + bias_ref[0:1].astype(F32)).astype(BF16)
    k_low = dot(a_low, w_ref[1]).astype(BF16)
    v_low = (dot(a_low, w_ref[2]) + bias_ref[1:2].astype(F32)).astype(BF16)
    local = k_low.shape[1]
    kv_ref[:, :local] = k_low
    kv_ref[:, local:] = v_low
    for index in range(all_ref.shape[0]):
        all_ref[index, :, :local] = k_low
        all_ref[index, :, local:] = v_low


def first_kernel(x_ref, gain_ref, shift_ref, w_ref, bias_ref, a_ref, q_ref, kv_ref, all_ref):
    normed, _ = norm_parts(x_ref[...].astype(F32))
    a_low = (normed * gain_ref[...] + shift_ref[...]).astype(BF16)
    a_ref[...] = a_low
    project(a_low, w_ref, bias_ref, q_ref, kv_ref, all_ref)


def project_kernel(a_ref, w_ref, bias_ref, q_ref, kv_ref, all_ref):
    project(a_ref[...], w_ref, bias_ref, q_ref, kv_ref, all_ref)


def head_masks(rows, local):
    column = lax.broadcasted_iota(jnp.int32, (rows, local), 1)
    return [column < HD, column >= HD]


def only(mask, value):
    return jnp.where(mask, value.astype(F32), 0.0).astype(BF16)


def allowed_of(start_ref, own_ref, all_ref, own_is_query):
    own_spot = start_ref[0] + lax.broadcasted_iota(jnp.int32, own_ref.shape, 0)
    spots = lax.broadcasted_iota(jnp.int32, all_ref.shape, 1)
    order = spots <= own_spot if own_is_query else spots >= own_spot
    return (all_ref[...] == own_ref[...]) & order


def attend_kernel(start_ref, own_ref, all_ref, q_ref, kv_ref, w_ref, o_ref, low_ref, log_ref, part_ref):
    rows, local = q_ref.shape
    total = all_ref.shape[1]
    keys = kv_ref[:, :, :local].reshape(total, local)
    values = kv_ref[:, :, local:].reshape(total, local)
    allowed = allowed_of(start_ref, own_ref, all_ref, True)
    queries = q_ref[...].astype(F32) * HD ** (-0.5)
    masks = head_masks(rows, local)
    outs, logs = [], []
    for mask in masks:
        scores = jnp.where(allowed, dot_t(only(mask, queries), keys), -1e30)
        top = jnp.max(scores, -1, keepdims=True)
        expd = jnp.exp(scores - top)
        denom = jnp.sum(expd, -1, keepdims=True)
        outs.append(dot((expd * (1.0 / denom)).astype(BF16), values))
        logs.append(top + jnp.log(denom))
    attended = jnp.where(masks[0], outs[0], outs[1])
    o_low = attended.astype(BF16)
    o_ref[...] = attended
    low_ref[...] = o_low
    log_ref[...] = jnp.where(masks[0], logs[0], logs[1])
    part_ref[...] = dot(o_low, w_ref[...]).astype(BF16).reshape(part_ref.shape)


def sum_parts(ref, start, rows):
    total = ref[0, start : start + rows].astype(F32)
    for index in range(1, ref.shape[0]):
        total = total + ref[index, start : start + rows].astype(F32)
    return total


def row_kernel(parts_ref, state_ref, bias_ref, gain_ref, shift_ref, state_out, normed_ref, factor_ref, sent_ref):
    state = state_ref[...] + (sum_parts(parts_ref, 0, state_ref.shape[0]) + bias_ref[...])
    normed, factor = norm_parts(state)
    low = (normed * gain_ref[...] + shift_ref[...]).astype(BF16)
    state_out[...] = state
    normed_ref[...] = normed
    factor_ref[...] = jnp.broadcast_to(factor, factor_ref.shape)
    for index in range(sent_ref.shape[0]):
        sent_ref[index] = low


def forward_kernel(b_ref, fc_ref, bias_ref, proj_ref, pre_ref, h_ref, part_ref):
    pre = dot(b_ref[...], fc_ref[...]) + bias_ref[...].astype(F32)
    h_low = gelu(pre).astype(BF16)
    pre_ref[...] = pre
    h_ref[...] = h_low
    part_ref[...] = dot(h_low, proj_ref[...]).astype(BF16).reshape(part_ref.shape)


def turn_kernel(b_ref, fc_ref, bias_ref, proj_ref, g_ref, h_ref, gf_ref, part_ref):
    share = part_ref.shape[1] // 2
    pre = dot(b_ref[...], fc_ref[...]) + bias_ref[...].astype(F32)
    h_low = gelu(pre).astype(BF16)
    h_ref[...] = h_low
    parts = dot(h_low, proj_ref[...]).astype(BF16)
    part_ref[:, :share] = parts.reshape(-1, share, parts.shape[1])
    g_f = (dot_t(g_ref[...], proj_ref[...]) * gelu_slope(pre)).astype(BF16)
    gf_ref[...] = g_f
    parts = dot_t(g_f, fc_ref[...]).astype(BF16)
    part_ref[:, share:] = parts.reshape(-1, share, parts.shape[1])


def backward_kernel(g_ref, pre_ref, fc_ref, proj_ref, gf_ref, part_ref):
    g_f = (dot_t(g_ref[...], proj_ref[...]) * gelu_slope(pre_ref[...])).astype(BF16)
    gf_ref[...] = g_f
    part_ref[...] = dot_t(g_f, fc_ref[...]).astype(BF16).reshape(part_ref.shape)


def norm_back(d_value, normed_ref, factor_ref, gain_ref, grad_ref, sums_ref):
    normed = normed_ref[...]
    scaled = d_value * gain_ref[...]
    back = factor_ref[:, 0:1] * (
        scaled
        - jnp.mean(scaled, -1, keepdims=True)
        - normed * jnp.mean(scaled * normed, -1, keepdims=True)
    )
    sums_ref[0:1] = jnp.sum(d_value * normed, 0, keepdims=True)
    sums_ref[1:2] = jnp.sum(d_value, 0, keepdims=True)
    return grad_ref[...] + back


def back_kernel(parts_ref, normed_ref, factor_ref, gain_ref, grad_ref, grad_out, sums_ref, sent_ref):
    share = normed_ref.shape[0]
    grad = norm_back(sum_parts(parts_ref, 0, share), normed_ref, factor_ref, gain_ref, grad_ref, sums_ref)
    grad_out[...] = grad
    low = grad.astype(BF16)
    for index in range(sent_ref.shape[0]):
        sent_ref[index] = low


def turn_back_kernel(
    parts_ref, state_ref, bias_ref, normed_ref, factor_ref, gain_ref, grad_ref, grad_out, sums_ref, sent_ref
):
    share = normed_ref.shape[0]
    out = (state_ref[...] + (sum_parts(parts_ref, 0, share) + bias_ref[...])).astype(BF16)
    grad = norm_back(sum_parts(parts_ref, share, share), normed_ref, factor_ref, gain_ref, grad_ref, sums_ref)
    grad_out[...] = grad
    low = grad.astype(BF16)
    for index in range(sent_ref.shape[0]):
        sent_ref[index, :share] = low
        sent_ref[index, share:] = out


def two_terms(value):
    high = value.astype(BF16).astype(F32)
    return high, value - high


def output_back_kernel(gy_ref, w_ref, o_ref, log_ref, go_ref, delta_ref, sent_ref):
    rows, local = o_ref.shape
    g_o = dot_t(gy_ref[...].reshape(rows, -1), w_ref[...]).astype(BF16)
    go_ref[...] = g_o
    masks = head_masks(rows, local)
    product = g_o.astype(F32) * o_ref[...]
    deltas = [jnp.sum(jnp.where(mask, product, 0.0), -1, keepdims=True) for mask in masks]
    delta = jnp.where(masks[0], deltas[0], deltas[1])
    delta_ref[...] = delta
    rows_of = []
    for value in (log_ref[...], delta):
        turned = value.T
        high, rest = two_terms(jnp.concatenate((turned[0:1], turned[HD : HD + 1]), 0))
        rows_of += [high, rest]
    rows_of.append(jnp.zeros((8, local), F32))
    extra = jnp.concatenate(rows_of, 0).astype(BF16)
    for index in range(sent_ref.shape[0]):
        sent_ref[index, :rows] = g_o
        sent_ref[index, rows:] = extra


def query_back_kernel(start_ref, own_ref, all_ref, q_ref, kv_ref, go_ref, log_ref, delta_ref, gq_ref):
    rows, local = q_ref.shape
    total = all_ref.shape[1]
    keys = kv_ref[:, :, :local].reshape(total, local)
    values = kv_ref[:, :, local:].reshape(total, local)
    allowed = allowed_of(start_ref, own_ref, all_ref, True)
    queries = q_ref[...].astype(F32) * HD ** (-0.5)
    masks = head_masks(rows, local)
    outs = []
    for head, mask in enumerate(masks):
        at = slice(head * HD, head * HD + 1)
        scores = jnp.where(allowed, dot_t(only(mask, queries), keys), -1e30)
        probs = jnp.exp(scores - log_ref[:, at])
        d_probs = dot_t(only(mask, go_ref[...]), values)
        g_s = (probs * (d_probs - delta_ref[:, at])).astype(BF16)
        outs.append(dot(g_s, keys))
    gq_ref[...] = (jnp.where(masks[0], outs[0], outs[1]) * HD ** (-0.5)).astype(BF16)


def key_back_kernel(start_ref, own_ref, all_ref, kv_ref, q_ref, got_ref, gq_ref, w_ref, gkv_ref, part_ref):
    rows, twice = kv_ref.shape
    local = twice // 2
    total = all_ref.shape[1]
    allowed = allowed_of(start_ref, own_ref, all_ref, False)
    queries = q_ref[...]
    g_o = got_ref[:, :rows].reshape(total, local)
    extra = got_ref[:, rows:].astype(F32)
    keys = kv_ref[:, :local].astype(F32) * HD ** (-0.5)
    values = kv_ref[:, local:]
    masks = head_masks(rows, local)
    d_keys, d_values = [], []
    for head, mask in enumerate(masks):

        def row_of(base):
            row = extra[:, base + head : base + head + 1] + extra[:, base + 2 + head : base + 3 + head]
            return jnp.concatenate([row[index] for index in range(row.shape[0])], 1)

        scores = jnp.where(allowed, dot_t(only(mask, keys), queries), -1e30)
        probs = jnp.exp(scores - row_of(0))
        d_probs = dot_t(only(mask, values), g_o)
        g_s = (probs * (d_probs - row_of(4))).astype(BF16)
        d_keys.append(dot(g_s, queries))
        d_values.append(dot(probs.astype(BF16), g_o))
    g_k = (jnp.where(masks[0], d_keys[0], d_keys[1]) * HD ** (-0.5)).astype(BF16)
    g_v = jnp.where(masks[0], d_values[0], d_values[1]).astype(BF16)
    gkv_ref[:, :local] = g_k
    gkv_ref[:, local:] = g_v
    part = dot_t(gq_ref[...], w_ref[0]) + dot_t(g_k, w_ref[1]) + dot_t(g_v, w_ref[2])
    part_ref[...] = part.astype(BF16).reshape(part_ref.shape)


def end_grads_kernel(h_ref, gm_ref, b_ref, gf_ref, pack_ref, gm_sum, gf_sum):
    g_m, g_f = gm_ref[...], gf_ref[...]
    hidden = g_f.shape[1]
    pack_ref[:hidden] = cross(h_ref[...], g_m).astype(BF16)
    g_w_fc = cross(b_ref[...], g_f).astype(BF16)
    for block in range(g_w_fc.shape[0] // hidden):
        at = slice(block * hidden, (block + 1) * hidden)
        pack_ref[hidden:, at] = g_w_fc[at]
    gm_sum[...] = jnp.sum(g_m.astype(F32), 0, keepdims=True)
    gf_sum[...] = jnp.sum(g_f.astype(F32), 0, keepdims=True)


def attend_grads_kernel(o_ref, gy_ref, a_ref, gq_ref, gkv_ref, pack_ref, gy_sum, gq_sum, gv_sum):
    local = gq_ref.shape[1]
    g_y = gy_ref[...].reshape(-1, gy_ref.shape[-1])
    a_low = a_ref[...]
    g_q, g_k, g_v = gq_ref[...], gkv_ref[:, :local], gkv_ref[:, local:]
    pack_ref[:local] = cross(o_ref[...], g_y).astype(BF16)
    for index, grad in enumerate((g_q, g_k, g_v)):
        product = cross(a_low, grad).astype(BF16)
        for block in range(product.shape[0] // local):
            at = slice(block * local, (block + 1) * local)
            pack_ref[(index + 1) * local : (index + 2) * local, at] = product[at]
    gy_sum[...] = jnp.sum(g_y.astype(F32), 0, keepdims=True)
    gq_sum[...] = jnp.sum(g_q.astype(F32), 0, keepdims=True)
    gv_sum[...] = jnp.sum(g_v.astype(F32), 0, keepdims=True)


def finish_end_kernel(side_ref, p_own, p_got, f_own, f_got, own_ref, got_ref, proj_ref, fc_ref):
    side = side_ref[0]
    half = p_own.shape[0]
    hidden = fc_ref.shape[2]

    def pick(own, got, index):
        return jnp.where(side == index, own[...].astype(F32), got[...].astype(F32))

    for index in range(2):
        rows = slice(index * half, (index + 1) * half)
        proj_ref[0, rows] = pick(p_own, p_got, index)
        packed = pick(f_own, f_got, index)
        for block in range(fc_ref.shape[1] // hidden):
            at = block * hidden + index * half
            fc_ref[0, at : at + half] = packed[:, block * hidden : (block + 1) * hidden]
    proj_ref[1] = pick(own_ref, got_ref, 0)
    packed = pick(own_ref, got_ref, 1)
    for block in range(fc_ref.shape[1] // hidden):
        at = slice(block * hidden, (block + 1) * hidden)
        fc_ref[1, at] = packed[:, at]


def finish_attend_kernel(side_ref, late_own, late_got, own_ref, got_ref, out_ref, qkv_ref):
    side = side_ref[0]
    local, width = out_ref.shape[1:]

    def put(layer, row, value):
        count = value.shape[0]
        if row < local:
            out_ref[layer, row : row + count] = value
        else:
            index, at = row // local - 1, row % local
            for block in range(width // local):
                base = block * local + at
                qkv_ref[layer, index, base : base + count] = value[:, block * local : (block + 1) * local]

    half = own_ref.shape[0]
    for index in range(2):
        picked = jnp.where(side == index, own_ref[...].astype(F32), got_ref[...].astype(F32))
        for row in range(0, half, local):
            put(1, index * half + row, picked[row : row + local])
        for chip in range(late_own.shape[0]):
            picked = jnp.where(side == index, late_own[chip].astype(F32), late_got[chip].astype(F32))
            for group in range(4):
                row = index * half + chip * 32 + group * 8
                put(0, row, picked[:, group * width : (group + 1) * width])


NEAR = {
    project_kernel: (0,),
    attend_kernel: (4,),
    row_kernel: (0,),
    forward_kernel: (0,),
    turn_kernel: (0,),
    turn_back_kernel: (0,),
    back_kernel: (0,),
    backward_kernel: (0,),
    output_back_kernel: (0,),
    query_back_kernel: (4,),
    key_back_kernel: (5,),
    end_grads_kernel: (1, 2),
    attend_grads_kernel: (1, 2),
}


def swap_all(value, axis):
    return lax.all_to_all(value, axis, 0, 0)


def cross(left, right):
    return lax.dot_general(left, right, (((0,), (0,)), ((), ())), preferred_element_type=F32)


CORE, DEPTH = 1, 2


def side_of(flip):
    return (lax.axis_index("dp") // flip) % 2


def swap(value, flip):
    return lax.ppermute(value, "dp", [(i, i ^ flip) for i in range(lax.axis_size("dp"))])


def after(value, event):
    return lax.optimization_barrier((value, event))[0]


def halve(value, flip, event=None, side=None):
    halves = value.reshape((2, value.shape[0] // 2) + value.shape[1:])
    side = side_of(flip) if side is None else side
    mine = lax.dynamic_index_in_dim(halves, side, 0, keepdims=False)
    got = swap(lax.dynamic_index_in_dim(halves, 1 - side, 0, keepdims=False), flip)
    got = got if event is None else after(got, event)
    return (mine.astype(F32) + got.astype(F32)).astype(BF16)


def rejoin(value, flip, side=None, event=None):
    got = swap(value, flip)
    got = got if event is None else after(got, event)
    side = side_of(flip) if side is None else side
    return jnp.concatenate((jnp.where(side, got, value), jnp.where(side, value, got)), 0)


def finish_sums(value, turn, events):
    place = lax.axis_index("dp")
    x_low, x_high = (place // 4) % 2, place // 8
    steps = ((4, x_low ^ x_high), (12, x_high)) if turn else ((12, x_high), (4, x_low ^ x_high))
    for (flip, side), event in zip(steps, events):
        value = halve(value, flip, event, side)
    for flip, side in steps[::-1]:
        value = rejoin(value, flip, side)
    value = rejoin(after(value, events[-1]), DEPTH)
    return value, swap(value, CORE)


def sum_over_x(values):
    groups = [[4 * x + rest for x in range(lax.axis_size("dp") // 4)] for rest in range(4)]
    return lax.psum(values, "dp", axis_index_groups=groups)


def swap_chips(value):
    groups = [[2 * chip + core for chip in range(lax.axis_size("dp") // 2)] for core in range(2)]
    return lax.all_to_all(value, "dp", 0, 0, axis_index_groups=groups)


def body(
    tokens,
    segment_ids,
    norm_gain,
    norm_bias,
    w_qkv,
    b_qv,
    w_out,
    b_out,
    w_fc,
    b_fc,
    w_proj,
    b_proj,
    cotangent,
):
    rows, width = tokens.shape
    total = segment_ids.shape[0]
    layers = w_qkv.shape[0]
    local = w_qkv.shape[3]
    hidden = w_fc.shape[2]
    ranks, slots = lax.axis_size("dp"), lax.axis_size("tensor")
    share = rows // slots
    first = (lax.axis_index("dp") * rows).astype(jnp.int32)
    own = lax.axis_index("tensor") * share
    start = first.reshape(1)
    seg_own = lax.dynamic_slice_in_dim(segment_ids, first, rows).reshape(rows, 1)
    seg_all = segment_ids.reshape(1, total)
    spots = (start, seg_own, seg_all)
    gains = norm_gain.astype(F32).reshape(layers, 2, 1, width)
    shifts = norm_bias.astype(F32).reshape(layers, 2, 1, width)
    out_bias = b_out.astype(F32).reshape(layers, 1, width)
    end_bias = b_proj.astype(F32).reshape(layers, 1, width)
    w_three = w_qkv.transpose(0, 2, 1, 3)
    fc_bias = b_fc.reshape(layers, 1, hidden)
    state = lax.dynamic_slice_in_dim(tokens, own, share).astype(F32)
    a_normed, a_factor = norm_parts(state)
    a_factor = jnp.broadcast_to(a_factor, (share, 128))
    row_block = shape((share, width), F32)
    row_stat = shape((share, 128), F32)
    exchange = shape((slots, share, width), BF16)
    saved = []
    qkv_shapes = [
        shape((rows, local), BF16),
        shape((rows, 2 * local), BF16),
        shape((ranks, rows, 2 * local), BF16),
    ]
    a_low = None
    for layer in range(layers):
        if layer:
            q_low, kv_own, kv_sent = call(project_kernel, qkv_shapes, (layer, (1, 2)), a_low, w_three, b_qv)
        else:
            a_low, q_low, kv_own, kv_sent = call(
                first_kernel,
                [shape((rows, width), BF16)] + qkv_shapes,
                (layer, (3, 4)),
                tokens,
                gains[0, 0],
                shifts[0, 0],
                w_three,
                b_qv,
            )
        kv_all = swap_all(kv_sent, "dp")
        o_full, o_low, logs, attn_parts = call(
            attend_kernel,
            [shape((rows, local), F32), shape((rows, local), BF16), shape((rows, local), F32), exchange],
            (layer, (5,)),
            *spots,
            q_low,
            kv_all,
            w_out,
            room=24,
        )
        middle, b_normed, b_factor, b_sent = call(
            row_kernel,
            [row_block, row_block, row_stat, exchange],
            (layer, ()),
            swap_all(attn_parts, "tensor"),
            state,
            out_bias[layer],
            gains[layer, 1],
            shifts[layer, 1],
        )
        b_low = swap_all(b_sent, "tensor").reshape(rows, width)
        kept = [a_normed, a_factor, a_low, q_low, kv_own, kv_all, o_full, o_low, logs, b_normed, b_factor, b_low]
        if layer < layers - 1:
            pre, h_low, parts = call(
                forward_kernel,
                [shape((rows, hidden), F32), shape((rows, hidden), BF16), exchange],
                (layer, (1, 2, 3)),
                b_low,
                w_fc,
                fc_bias,
                w_proj,
            )
            state, a_normed, a_factor, a_sent = call(
                row_kernel,
                [row_block, row_block, row_stat, exchange],
                (layer, ()),
                swap_all(parts, "tensor"),
                middle,
                end_bias[layer],
                gains[layer + 1, 0],
                shifts[layer + 1, 0],
            )
            a_low = swap_all(a_sent, "tensor").reshape(rows, width)
            kept += [pre, h_low]
        saved.append(kept)
    q_every = lax.all_gather(jnp.concatenate([kept[3] for kept in saved], 1), "dp", axis=0, tiled=True)
    g_m = cotangent
    grad = lax.dynamic_slice_in_dim(cotangent, own, share).astype(F32)
    done = [None] * layers
    smalls, sums = [], []
    two_rows = shape((2, width), F32)
    out = None
    def end_grads(layer, h_low, g_m, b_low, g_f):
        return call(
            end_grads_kernel,
            [shape((2 * hidden, width), BF16), shape((1, width), F32), shape((1, hidden), F32)],
            (layer, ()),
            h_low,
            g_m,
            b_low,
            g_f,
            room=16,
        )

    for layer in reversed(range(layers)):
        a_normed, a_factor, a_low, q_low, kv_own, kv_all, o_full, o_low, logs, b_normed, b_factor, b_low = (
            saved[layer][:12]
        )
        if layer == layers - 1:
            double = shape((slots, 2 * share, width), BF16)
            h_low, g_f, parts = call(
                turn_kernel,
                [shape((rows, hidden), BF16), shape((rows, hidden), BF16), double],
                (layer, (1, 2, 3)),
                b_low,
                w_fc,
                fc_bias,
                w_proj,
                g_m,
            )
            grad, sums_b, sent = call(
                turn_back_kernel,
                [row_block, two_rows, double],
                (layer, ()),
                swap_all(parts, "tensor"),
                middle,
                end_bias[layer],
                b_normed,
                b_factor,
                gains[layer, 1],
                grad,
            )
            got = swap_all(sent, "tensor")
            g_y = got
            out = got[:, share:].reshape(rows, width).astype(F32)
        else:
            pre, h_low = saved[layer][12:]
            g_f, parts = call(
                backward_kernel,
                [shape((rows, hidden), BF16), exchange],
                (layer, (2, 3)),
                g_m,
                pre,
                w_fc,
                w_proj,
            )
            end_pack, gm_sum, gf_sum = end_grads(layer, h_low, g_m, b_low, g_f)
            grad, sums_b, sent = call(
                back_kernel,
                [row_block, two_rows, exchange],
                (layer, ()),
                swap_all(parts, "tensor"),
                b_normed,
                b_factor,
                gains[layer, 1],
                grad,
            )
            sent, quarters = lax.optimization_barrier((sent, quarters))
            done[1] = sum_over_x(quarters)
            g_y = swap_all(sent, "tensor")
        grad_b = grad
        g_o, delta, sent = call(
            output_back_kernel,
            [shape((rows, local), BF16), shape((rows, local), F32), shape((ranks, rows + 16, local), BF16)],
            (layer, (1,)),
            g_y,
            w_out,
            o_full,
            logs,
            blocks={0: ((slots, share, width), lambda i: (0, 0, 0))},
        )
        if layer:
            sent, q_every = lax.optimization_barrier((sent, q_every))
        else:
            starts = [
                halve(halve(part, CORE), DEPTH) for part in (end_pack[:hidden], end_pack[hidden:])
            ]
            sent, starts = lax.optimization_barrier((sent, starts))
        go_all = swap_all(sent, "dp")
        (g_q,) = call(
            query_back_kernel,
            [shape((rows, local), BF16)],
            (layer, ()),
            *spots,
            q_low,
            kv_all,
            g_o,
            logs,
            delta,
            room=24,
        )
        g_kv, parts = call(
            key_back_kernel,
            [shape((rows, 2 * local), BF16), exchange],
            (layer, (7,)),
            *spots,
            kv_own,
            q_every,
            go_all,
            g_q,
            w_three,
            room=24,
            blocks={4: ((total, local), lambda i: (0, layer))},
        )
        if not layer:
            parts, done[1] = lax.optimization_barrier((parts, done[1]))
        grad, sums_a, sent = call(
            back_kernel,
            [row_block, two_rows, exchange],
            (layer, ()),
            swap_all(parts, "tensor"),
            a_normed,
            a_factor,
            gains[layer, 0],
            grad,
        )
        sums = [sums_a, sums_b] + sums
        if layer:
            end_pack, gm_sum, gf_sum = end_grads(layer, h_low, g_m, b_low, g_f)
        attend_pack, gy_sum, gq_sum, gv_sum = call(
            attend_grads_kernel,
            [
                shape((4 * local, width), BF16),
                shape((1, width), F32),
                shape((1, local), F32),
                shape((1, local), F32),
            ],
            (layer, ()),
            o_low,
            g_y,
            a_low,
            g_q,
            g_kv,
            room=16,
            blocks={1: ((slots, share, width), lambda i: (0, 0, 0))},
        )
        smalls = [gy_sum, gm_sum, gq_sum, gv_sum, gf_sum] + smalls
        if layer:
            g_m = swap_all(sent, "tensor").reshape(rows, width)
            end_part = halve(halve(end_pack, CORE, go_all), DEPTH, grad)
            attend_part = halve(halve(attend_pack, CORE), DEPTH, g_m)
            quarters = (end_part, attend_part)
    tail = jnp.concatenate([sent, jnp.broadcast_to(jnp.concatenate(sums, 0).astype(BF16), (slots, 8, width))], 1)
    tail_got = got = swap_all(tail, "tensor")
    grad_input = got[:, :share].reshape(rows, width).astype(F32)
    norm_sums = jnp.sum(got[:, share:].astype(F32), 0)
    small = jnp.concatenate([norm_sums.reshape(-1)] + [part.reshape(-1) for part in smalls])
    each = small.size // (8 * ranks)
    wide = 4 * width
    packed = jnp.concatenate(
        (
            attend_pack.reshape(ranks, 4, 8, width).transpose(0, 2, 1, 3).reshape(ranks, 8, wide),
            jnp.pad(small.astype(BF16).reshape(ranks, 8, each), ((0, 0), (0, 0), (0, 128 - each))),
        ),
        2,
    )
    half = halve(packed, CORE)
    arrived = swap_chips(half)
    mine = jnp.sum(arrived.astype(F32), 0).astype(BF16)
    late = swap_chips(jnp.broadcast_to(mine, (ranks // 2,) + mine.shape))
    events = (g_kv, grad, half)
    end_parts = [part for turn, value in enumerate(starts) for part in finish_sums(value, turn, events)]
    end_last, attend_last = [rejoin(part, DEPTH, None, half) for part in done[1]]
    side = side_of(CORE)
    sides = side.astype(jnp.int32).reshape(1)
    g_w_proj, g_w_fc = call(
        finish_end_kernel,
        [shape((layers, hidden, width), F32), shape((layers, width, hidden), F32)],
        (0, ()),
        sides,
        *end_parts,
        end_last,
        swap(end_last, CORE),
        room=40,
    )
    late, g_w_proj, g_w_fc = lax.optimization_barrier((late, g_w_proj, g_w_fc))
    late_got = swap(late, CORE)
    g_w_out, g_w_qkv = call(
        finish_attend_kernel,
        [shape((layers, local, width), F32), shape((layers, 3, width, local), F32)],
        (0, ()),
        sides,
        late,
        late_got,
        attend_last,
        swap(attend_last, CORE),
        room=24,
    )
    ours, theirs = late[:, :, wide : wide + each], late_got[:, :, wide : wide + each]
    small = jnp.concatenate((jnp.where(side, theirs, ours), jnp.where(side, ours, theirs)), 0)
    small = small.reshape(-1).astype(F32)
    norm_grads = small[: 8 * width].reshape(layers, 2, 2, width)
    per_layer = small[8 * width :].reshape(layers, -1)
    cut = 2 * width

    return (
        out,
        grad_input,
        norm_grads[:, :, 0],
        norm_grads[:, :, 1],
        g_w_qkv.transpose(0, 2, 1, 3),
        per_layer[:, cut : cut + 2 * local].reshape(layers, 2, local),
        g_w_out,
        per_layer[:, :width],
        g_w_fc,
        per_layer[:, cut + 2 * local :],
        g_w_proj,
        per_layer[:, width:cut],
    )


def solution(mesh):
    in_specs = (
        P("dp", None),
        P(),
        P(),
        P(),
        P(None, None, None, "tensor"),
        P(None, None, "tensor"),
        P(None, "tensor", None),
        P(),
        P(None, None, "tensor"),
        P(None, "tensor"),
        P(None, "tensor", None),
        P(),
        P("dp", None),
    )
    out_specs = (
        P("dp", None),
        P("dp", None),
        P(),
        P(),
        P(None, None, None, "tensor"),
        P(None, None, "tensor"),
        P(None, "tensor", None),
        P(),
        P(None, None, "tensor"),
        P(None, "tensor"),
        P(None, "tensor", None),
        P(),
    )
    return jax.shard_map(body, mesh=mesh, in_specs=in_specs, out_specs=out_specs, check_vma=False)
```

```python
import functools

import jax
import jax.numpy as jnp
from jax import lax
from jax.experimental import pallas as pl
from jax.experimental.pallas import tpu as pltpu
from jax.sharding import PartitionSpec as P

HD = 64
F32 = jnp.float32
BF16 = jnp.bfloat16
ROOT = 0.7978845608028654
CUBE = 0.044715


def dot(left, right):
    return jnp.dot(left, right, preferred_element_type=F32)


def dot_t(left, right):
    return lax.dot_general(left, right, (((1,), (1,)), ((), ())), preferred_element_type=F32)


def norm_parts(value):
    mean = jnp.mean(value, -1, keepdims=True)
    centered = value - mean
    spread = jnp.mean(centered * centered, -1, keepdims=True)
    factor = lax.rsqrt(spread + 1e-05)
    return centered * factor, factor


def tanh_part(value):
    return jnp.tanh(ROOT * (value + CUBE * value * value * value))


def gelu(value):
    return 0.5 * value * (1.0 + tanh_part(value))


def gelu_slope(value):
    bend = tanh_part(value)
    inner = ROOT * (1.0 + 3.0 * CUBE * value * value)
    return 0.5 * (1.0 + bend) + 0.5 * value * (1.0 - bend * bend) * inner


def call(kernel, outs, layered, *args, room=12, blocks={}):
    layer, wide = layered
    near = NEAR.get(kernel, ())
    args = [
        arg if index in near or arg.shape == (1,) else pltpu.with_memory_space_constraint(arg, pltpu.HBM)
        for index, arg in enumerate(args)
    ]

    def spec(index, arg):
        if arg.dtype == jnp.int32 and arg.shape == (1,):
            return pl.BlockSpec(memory_space=pltpu.SMEM)
        if index in blocks:
            return pl.BlockSpec(*blocks[index])
        if index in wide:
            rest = arg.shape[1:]
            return pl.BlockSpec((None,) + rest, lambda i: (layer,) + (0,) * len(rest))
        return pl.BlockSpec(arg.shape, lambda i: (0,) * arg.ndim)

    return pl.pallas_call(
        kernel,
        grid=(1,),
        in_specs=[spec(index, arg) for index, arg in enumerate(args)],
        out_specs=[pl.BlockSpec(out.shape, lambda i, n=len(out.shape): (0,) * n) for out in outs],
        out_shape=[pltpu.HBM(out.shape, out.dtype) for out in outs],
        cost_estimate=pl.CostEstimate(flops=1000, bytes_accessed=1000, transcendentals=0),
        compiler_params=pltpu.CompilerParams(vmem_limit_bytes=room * 1024 * 1024),
    )(*args)


def shape(dims, kind):
    return jax.ShapeDtypeStruct(dims, kind)


def project(a_low, w_ref, bias_ref, q_ref, kv_ref, all_ref):
    q_ref[...] = (dot(a_low, w_ref[0]) + bias_ref[0:1].astype(F32)).astype(BF16)
    k_low = dot(a_low, w_ref[1]).astype(BF16)
    v_low = (dot(a_low, w_ref[2]) + bias_ref[1:2].astype(F32)).astype(BF16)
    local = k_low.shape[1]
    kv_ref[:, :local] = k_low
    kv_ref[:, local:] = v_low
    for index in range(all_ref.shape[0]):
        all_ref[index, :, :local] = k_low
        all_ref[index, :, local:] = v_low


def first_kernel(x_ref, gain_ref, shift_ref, w_ref, bias_ref, a_ref, q_ref, kv_ref, all_ref):
    normed, _ = norm_parts(x_ref[...].astype(F32))
    a_low = (normed * gain_ref[...] + shift_ref[...]).astype(BF16)
    a_ref[...] = a_low
    project(a_low, w_ref, bias_ref, q_ref, kv_ref, all_ref)


def project_kernel(a_ref, w_ref, bias_ref, q_ref, kv_ref, all_ref):
    project(a_ref[...], w_ref, bias_ref, q_ref, kv_ref, all_ref)


def head_masks(rows, local):
    column = lax.broadcasted_iota(jnp.int32, (rows, local), 1)
    return [column < HD, column >= HD]


def only(mask, value):
    return jnp.where(mask, value.astype(F32), 0.0).astype(BF16)


def allowed_of(start_ref, own_ref, all_ref, own_is_query):
    own_spot = start_ref[0] + lax.broadcasted_iota(jnp.int32, own_ref.shape, 0)
    spots = lax.broadcasted_iota(jnp.int32, all_ref.shape, 1)
    order = spots <= own_spot if own_is_query else spots >= own_spot
    return (all_ref[...] == own_ref[...]) & order


def attend_kernel(start_ref, own_ref, all_ref, q_ref, kv_ref, w_ref, o_ref, low_ref, log_ref, part_ref):
    rows, local = q_ref.shape
    total = all_ref.shape[1]
    keys = kv_ref[:, :, :local].reshape(total, local)
    values = kv_ref[:, :, local:].reshape(total, local)
    allowed = allowed_of(start_ref, own_ref, all_ref, True)
    queries = q_ref[...].astype(F32) * HD ** (-0.5)
    masks = head_masks(rows, local)
    outs, logs = [], []
    for mask in masks:
        scores = jnp.where(allowed, dot_t(only(mask, queries), keys), -1e30)
        top = jnp.max(scores, -1, keepdims=True)
        expd = jnp.exp(scores - top)
        denom = jnp.sum(expd, -1, keepdims=True)
        outs.append(dot((expd * (1.0 / denom)).astype(BF16), values))
        logs.append(top + jnp.log(denom))
    attended = jnp.where(masks[0], outs[0], outs[1])
    o_low = attended.astype(BF16)
    o_ref[...] = attended
    low_ref[...] = o_low
    log_ref[...] = jnp.where(masks[0], logs[0], logs[1])
    part_ref[...] = dot(o_low, w_ref[...]).astype(BF16).reshape(part_ref.shape)


def sum_parts(ref, start, rows):
    total = ref[0, start : start + rows].astype(F32)
    for index in range(1, ref.shape[0]):
        total = total + ref[index, start : start + rows].astype(F32)
    return total


def row_kernel(parts_ref, state_ref, bias_ref, gain_ref, shift_ref, state_out, normed_ref, factor_ref, sent_ref):
    state = state_ref[...] + (sum_parts(parts_ref, 0, state_ref.shape[0]) + bias_ref[...])
    normed, factor = norm_parts(state)
    low = (normed * gain_ref[...] + shift_ref[...]).astype(BF16)
    state_out[...] = state
    normed_ref[...] = normed
    factor_ref[...] = jnp.broadcast_to(factor, factor_ref.shape)
    for index in range(sent_ref.shape[0]):
        sent_ref[index] = low


def forward_kernel(b_ref, fc_ref, bias_ref, proj_ref, pre_ref, h_ref, part_ref):
    pre = dot(b_ref[...], fc_ref[...]) + bias_ref[...].astype(F32)
    h_low = gelu(pre).astype(BF16)
    pre_ref[...] = pre
    h_ref[...] = h_low
    part_ref[...] = dot(h_low, proj_ref[...]).astype(BF16).reshape(part_ref.shape)


def turn_kernel(b_ref, fc_ref, bias_ref, proj_ref, g_ref, h_ref, gf_ref, part_ref):
    share = part_ref.shape[1] // 2
    pre = dot(b_ref[...], fc_ref[...]) + bias_ref[...].astype(F32)
    h_low = gelu(pre).astype(BF16)
    h_ref[...] = h_low
    parts = dot(h_low, proj_ref[...]).astype(BF16)
    part_ref[:, :share] = parts.reshape(-1, share, parts.shape[1])
    g_f = (dot_t(g_ref[...], proj_ref[...]) * gelu_slope(pre)).astype(BF16)
    gf_ref[...] = g_f
    parts = dot_t(g_f, fc_ref[...]).astype(BF16)
    part_ref[:, share:] = parts.reshape(-1, share, parts.shape[1])


def backward_kernel(g_ref, pre_ref, fc_ref, proj_ref, gf_ref, part_ref):
    g_f = (dot_t(g_ref[...], proj_ref[...]) * gelu_slope(pre_ref[...])).astype(BF16)
    gf_ref[...] = g_f
    part_ref[...] = dot_t(g_f, fc_ref[...]).astype(BF16).reshape(part_ref.shape)


def norm_back(d_value, normed_ref, factor_ref, gain_ref, grad_ref, sums_ref):
    normed = normed_ref[...]
    scaled = d_value * gain_ref[...]
    back = factor_ref[:, 0:1] * (
        scaled
        - jnp.mean(scaled, -1, keepdims=True)
        - normed * jnp.mean(scaled * normed, -1, keepdims=True)
    )
    sums_ref[0:1] = jnp.sum(d_value * normed, 0, keepdims=True)
    sums_ref[1:2] = jnp.sum(d_value, 0, keepdims=True)
    return grad_ref[...] + back


def back_kernel(parts_ref, normed_ref, factor_ref, gain_ref, grad_ref, grad_out, sums_ref, sent_ref):
    share = normed_ref.shape[0]
    grad = norm_back(sum_parts(parts_ref, 0, share), normed_ref, factor_ref, gain_ref, grad_ref, sums_ref)
    grad_out[...] = grad
    low = grad.astype(BF16)
    for index in range(sent_ref.shape[0]):
        sent_ref[index] = low


def turn_back_kernel(
    parts_ref, state_ref, bias_ref, normed_ref, factor_ref, gain_ref, grad_ref, grad_out, sums_ref, sent_ref
):
    share = normed_ref.shape[0]
    out = (state_ref[...] + (sum_parts(parts_ref, 0, share) + bias_ref[...])).astype(BF16)
    grad = norm_back(sum_parts(parts_ref, share, share), normed_ref, factor_ref, gain_ref, grad_ref, sums_ref)
    grad_out[...] = grad
    low = grad.astype(BF16)
    for index in range(sent_ref.shape[0]):
        sent_ref[index, :share] = low
        sent_ref[index, share:] = out


def two_terms(value):
    high = value.astype(BF16).astype(F32)
    return high, value - high


def output_back_kernel(gy_ref, w_ref, o_ref, log_ref, go_ref, delta_ref, sent_ref):
    rows, local = o_ref.shape
    g_o = dot_t(gy_ref[...].reshape(rows, -1), w_ref[...]).astype(BF16)
    go_ref[...] = g_o
    masks = head_masks(rows, local)
    product = g_o.astype(F32) * o_ref[...]
    deltas = [jnp.sum(jnp.where(mask, product, 0.0), -1, keepdims=True) for mask in masks]
    delta = jnp.where(masks[0], deltas[0], deltas[1])
    delta_ref[...] = delta
    rows_of = []
    for value in (log_ref[...], delta):
        turned = value.T
        high, rest = two_terms(jnp.concatenate((turned[0:1], turned[HD : HD + 1]), 0))
        rows_of += [high, rest]
    rows_of.append(jnp.zeros((8, local), F32))
    extra = jnp.concatenate(rows_of, 0).astype(BF16)
    for index in range(sent_ref.shape[0]):
        sent_ref[index, :rows] = g_o
        sent_ref[index, rows:] = extra


def query_back_kernel(start_ref, own_ref, all_ref, q_ref, kv_ref, go_ref, log_ref, delta_ref, gq_ref):
    rows, local = q_ref.shape
    total = all_ref.shape[1]
    keys = kv_ref[:, :, :local].reshape(total, local)
    values = kv_ref[:, :, local:].reshape(total, local)
    allowed = allowed_of(start_ref, own_ref, all_ref, True)
    queries = q_ref[...].astype(F32) * HD ** (-0.5)
    masks = head_masks(rows, local)
    outs = []
    for head, mask in enumerate(masks):
        at = slice(head * HD, head * HD + 1)
        scores = jnp.where(allowed, dot_t(only(mask, queries), keys), -1e30)
        probs = jnp.exp(scores - log_ref[:, at])
        d_probs = dot_t(only(mask, go_ref[...]), values)
        g_s = (probs * (d_probs - delta_ref[:, at])).astype(BF16)
        outs.append(dot(g_s, keys))
    gq_ref[...] = (jnp.where(masks[0], outs[0], outs[1]) * HD ** (-0.5)).astype(BF16)


def key_back_kernel(start_ref, own_ref, all_ref, kv_ref, q_ref, got_ref, gq_ref, w_ref, gkv_ref, part_ref):
    rows, twice = kv_ref.shape
    local = twice // 2
    total = all_ref.shape[1]
    allowed = allowed_of(start_ref, own_ref, all_ref, False)
    queries = q_ref[...]
    g_o = got_ref[:, :rows].reshape(total, local)
    extra = got_ref[:, rows:].astype(F32)
    keys = kv_ref[:, :local].astype(F32) * HD ** (-0.5)
    values = kv_ref[:, local:]
    masks = head_masks(rows, local)
    d_keys, d_values = [], []
    for head, mask in enumerate(masks):

        def row_of(base):
            row = extra[:, base + head : base + head + 1] + extra[:, base + 2 + head : base + 3 + head]
            return jnp.concatenate([row[index] for index in range(row.shape[0])], 1)

        scores = jnp.where(allowed, dot_t(only(mask, keys), queries), -1e30)
        probs = jnp.exp(scores - row_of(0))
        d_probs = dot_t(only(mask, values), g_o)
        g_s = (probs * (d_probs - row_of(4))).astype(BF16)
        d_keys.append(dot(g_s, queries))
        d_values.append(dot(probs.astype(BF16), g_o))
    g_k = (jnp.where(masks[0], d_keys[0], d_keys[1]) * HD ** (-0.5)).astype(BF16)
    g_v = jnp.where(masks[0], d_values[0], d_values[1]).astype(BF16)
    gkv_ref[:, :local] = g_k
    gkv_ref[:, local:] = g_v
    part = dot_t(gq_ref[...], w_ref[0]) + dot_t(g_k, w_ref[1]) + dot_t(g_v, w_ref[2])
    part_ref[...] = part.astype(BF16).reshape(part_ref.shape)


def end_grads_kernel(h_ref, gm_ref, b_ref, gf_ref, pack_ref, gm_sum, gf_sum):
    g_m, g_f = gm_ref[...], gf_ref[...]
    hidden = g_f.shape[1]
    pack_ref[:hidden] = cross(h_ref[...], g_m).astype(BF16)
    g_w_fc = cross(b_ref[...], g_f).astype(BF16)
    for block in range(g_w_fc.shape[0] // hidden):
        at = slice(block * hidden, (block + 1) * hidden)
        pack_ref[hidden:, at] = g_w_fc[at]
    gm_sum[...] = jnp.sum(g_m.astype(F32), 0, keepdims=True)
    gf_sum[...] = jnp.sum(g_f.astype(F32), 0, keepdims=True)


def attend_grads_kernel(o_ref, gy_ref, a_ref, gq_ref, gkv_ref, pack_ref, gy_sum, gq_sum, gv_sum):
    local = gq_ref.shape[1]
    g_y = gy_ref[...].reshape(-1, gy_ref.shape[-1])
    a_low = a_ref[...]
    g_q, g_k, g_v = gq_ref[...], gkv_ref[:, :local], gkv_ref[:, local:]
    pack_ref[:local] = cross(o_ref[...], g_y).astype(BF16)
    for index, grad in enumerate((g_q, g_k, g_v)):
        product = cross(a_low, grad).astype(BF16)
        for block in range(product.shape[0] // local):
            at = slice(block * local, (block + 1) * local)
            pack_ref[(index + 1) * local : (index + 2) * local, at] = product[at]
    gy_sum[...] = jnp.sum(g_y.astype(F32), 0, keepdims=True)
    gq_sum[...] = jnp.sum(g_q.astype(F32), 0, keepdims=True)
    gv_sum[...] = jnp.sum(g_v.astype(F32), 0, keepdims=True)


def finish_end_kernel(side_ref, p_own, p_got, f_own, f_got, own_ref, got_ref, proj_ref, fc_ref):
    side = side_ref[0]
    half = p_own.shape[0]
    hidden = fc_ref.shape[2]

    def pick(own, got, index):
        return jnp.where(side == index, own[...].astype(F32), got[...].astype(F32))

    for index in range(2):
        rows = slice(index * half, (index + 1) * half)
        proj_ref[0, rows] = pick(p_own, p_got, index)
        packed = pick(f_own, f_got, index)
        for block in range(fc_ref.shape[1] // hidden):
            at = block * hidden + index * half
            fc_ref[0, at : at + half] = packed[:, block * hidden : (block + 1) * hidden]
    proj_ref[1] = pick(own_ref, got_ref, 0)
    packed = pick(own_ref, got_ref, 1)
    for block in range(fc_ref.shape[1] // hidden):
        at = slice(block * hidden, (block + 1) * hidden)
        fc_ref[1, at] = packed[:, at]


def finish_attend_kernel(side_ref, late_own, late_got, own_ref, got_ref, out_ref, qkv_ref):
    side = side_ref[0]
    local, width = out_ref.shape[1:]

    def put(layer, row, value):
        count = value.shape[0]
        if row < local:
            out_ref[layer, row : row + count] = value
        else:
            index, at = row // local - 1, row % local
            for block in range(width // local):
                base = block * local + at
                qkv_ref[layer, index, base : base + count] = value[:, block * local : (block + 1) * local]

    half = own_ref.shape[0]
    for index in range(2):
        picked = jnp.where(side == index, own_ref[...].astype(F32), got_ref[...].astype(F32))
        for row in range(0, half, local):
            put(1, index * half + row, picked[row : row + local])
        for chip in range(late_own.shape[0]):
            picked = jnp.where(side == index, late_own[chip].astype(F32), late_got[chip].astype(F32))
            for group in range(4):
                row = index * half + chip * 32 + group * 8
                put(0, row, picked[:, group * width : (group + 1) * width])


NEAR = {
    project_kernel: (0,),
    attend_kernel: (4,),
    row_kernel: (0,),
    forward_kernel: (0,),
    turn_kernel: (0,),
    turn_back_kernel: (0,),
    back_kernel: (0,),
    backward_kernel: (0,),
    output_back_kernel: (0,),
    query_back_kernel: (4,),
    key_back_kernel: (5,),
    end_grads_kernel: (1, 2),
    attend_grads_kernel: (1, 2),
}


def swap_all(value, axis):
    return lax.all_to_all(value, axis, 0, 0)


def cross(left, right):
    return lax.dot_general(left, right, (((0,), (0,)), ((), ())), preferred_element_type=F32)


CORE, DEPTH = 1, 2


def side_of(flip):
    return (lax.axis_index("dp") // flip) % 2


def swap(value, flip):
    return lax.ppermute(value, "dp", [(i, i ^ flip) for i in range(lax.axis_size("dp"))])


def after(value, event):
    return lax.optimization_barrier((value, event))[0]


def halve(value, flip, event=None, side=None):
    halves = value.reshape((2, value.shape[0] // 2) + value.shape[1:])
    side = side_of(flip) if side is None else side
    mine = lax.dynamic_index_in_dim(halves, side, 0, keepdims=False)
    got = swap(lax.dynamic_index_in_dim(halves, 1 - side, 0, keepdims=False), flip)
    got = got if event is None else after(got, event)
    return (mine.astype(F32) + got.astype(F32)).astype(BF16)


def rejoin(value, flip, side=None, event=None):
    got = swap(value, flip)
    got = got if event is None else after(got, event)
    side = side_of(flip) if side is None else side
    return jnp.concatenate((jnp.where(side, got, value), jnp.where(side, value, got)), 0)


def finish_sums(value, turn, events):
    place = lax.axis_index("dp")
    x_low, x_high = (place // 4) % 2, place // 8
    steps = ((4, x_low ^ x_high), (12, x_high)) if turn else ((12, x_high), (4, x_low ^ x_high))
    for (flip, side), event in zip(steps, events):
        value = halve(value, flip, event, side)
    for flip, side in steps[::-1]:
        value = rejoin(value, flip, side)
    value = rejoin(after(value, events[-1]), DEPTH)
    return value, swap(value, CORE)


def sum_over_x(values):
    groups = [[4 * x + rest for x in range(lax.axis_size("dp") // 4)] for rest in range(4)]
    return lax.psum(values, "dp", axis_index_groups=groups)


def swap_chips(value):
    groups = [[2 * chip + core for chip in range(lax.axis_size("dp") // 2)] for core in range(2)]
    return lax.all_to_all(value, "dp", 0, 0, axis_index_groups=groups)


def body(
    tokens,
    segment_ids,
    norm_gain,
    norm_bias,
    w_qkv,
    b_qv,
    w_out,
    b_out,
    w_fc,
    b_fc,
    w_proj,
    b_proj,
    cotangent,
):
    rows, width = tokens.shape
    total = segment_ids.shape[0]
    layers = w_qkv.shape[0]
    local = w_qkv.shape[3]
    hidden = w_fc.shape[2]
    ranks, slots = lax.axis_size("dp"), lax.axis_size("tensor")
    share = rows // slots
    first = (lax.axis_index("dp") * rows).astype(jnp.int32)
    own = lax.axis_index("tensor") * share
    start = first.reshape(1)
    seg_own = lax.dynamic_slice_in_dim(segment_ids, first, rows).reshape(rows, 1)
    seg_all = segment_ids.reshape(1, total)
    spots = (start, seg_own, seg_all)
    gains = norm_gain.astype(F32).reshape(layers, 2, 1, width)
    shifts = norm_bias.astype(F32).reshape(layers, 2, 1, width)
    out_bias = b_out.astype(F32).reshape(layers, 1, width)
    end_bias = b_proj.astype(F32).reshape(layers, 1, width)
    w_three = w_qkv.transpose(0, 2, 1, 3)
    fc_bias = b_fc.reshape(layers, 1, hidden)
    state = lax.dynamic_slice_in_dim(tokens, own, share).astype(F32)
    a_normed, a_factor = norm_parts(state)
    a_factor = jnp.broadcast_to(a_factor, (share, 128))
    row_block = shape((share, width), F32)
    row_stat = shape((share, 128), F32)
    exchange = shape((slots, share, width), BF16)
    saved = []
    qkv_shapes = [
        shape((rows, local), BF16),
        shape((rows, 2 * local), BF16),
        shape((ranks, rows, 2 * local), BF16),
    ]
    a_low = None
    for layer in range(layers):
        if layer:
            q_low, kv_own, kv_sent = call(project_kernel, qkv_shapes, (layer, (1, 2)), a_low, w_three, b_qv)
        else:
            a_low, q_low, kv_own, kv_sent = call(
                first_kernel,
                [shape((rows, width), BF16)] + qkv_shapes,
                (layer, (3, 4)),
                tokens,
                gains[0, 0],
                shifts[0, 0],
                w_three,
                b_qv,
            )
        kv_all = swap_all(kv_sent, "dp")
        o_full, o_low, logs, attn_parts = call(
            attend_kernel,
            [shape((rows, local), F32), shape((rows, local), BF16), shape((rows, local), F32), exchange],
            (layer, (5,)),
            *spots,
            q_low,
            kv_all,
            w_out,
            room=24,
        )
        middle, b_normed, b_factor, b_sent = call(
            row_kernel,
            [row_block, row_block, row_stat, exchange],
            (layer, ()),
            swap_all(attn_parts, "tensor"),
            state,
            out_bias[layer],
            gains[layer, 1],
            shifts[layer, 1],
        )
        b_low = swap_all(b_sent, "tensor").reshape(rows, width)
        kept = [a_normed, a_factor, a_low, q_low, kv_own, kv_all, o_full, o_low, logs, b_normed, b_factor, b_low]
        if layer < layers - 1:
            pre, h_low, parts = call(
                forward_kernel,
                [shape((rows, hidden), F32), shape((rows, hidden), BF16), exchange],
                (layer, (1, 2, 3)),
                b_low,
                w_fc,
                fc_bias,
                w_proj,
            )
            state, a_normed, a_factor, a_sent = call(
                row_kernel,
                [row_block, row_block, row_stat, exchange],
                (layer, ()),
                swap_all(parts, "tensor"),
                middle,
                end_bias[layer],
                gains[layer + 1, 0],
                shifts[layer + 1, 0],
            )
            a_low = swap_all(a_sent, "tensor").reshape(rows, width)
            kept += [pre, h_low]
        saved.append(kept)
    q_every = lax.all_gather(jnp.concatenate([kept[3] for kept in saved], 1), "dp", axis=0, tiled=True)
    g_m = cotangent
    grad = lax.dynamic_slice_in_dim(cotangent, own, share).astype(F32)
    done = [None] * layers
    smalls, sums = [], []
    two_rows = shape((2, width), F32)
    out = None
    def end_grads(layer, h_low, g_m, b_low, g_f):
        return call(
            end_grads_kernel,
            [shape((2 * hidden, width), BF16), shape((1, width), F32), shape((1, hidden), F32)],
            (layer, ()),
            h_low,
            g_m,
            b_low,
            g_f,
            room=16,
        )

    for layer in reversed(range(layers)):
        a_normed, a_factor, a_low, q_low, kv_own, kv_all, o_full, o_low, logs, b_normed, b_factor, b_low = (
            saved[layer][:12]
        )
        if layer == layers - 1:
            double = shape((slots, 2 * share, width), BF16)
            h_low, g_f, parts = call(
                turn_kernel,
                [shape((rows, hidden), BF16), shape((rows, hidden), BF16), double],
                (layer, (1, 2, 3)),
                b_low,
                w_fc,
                fc_bias,
                w_proj,
                g_m,
            )
            grad, sums_b, sent = call(
                turn_back_kernel,
                [row_block, two_rows, double],
                (layer, ()),
                swap_all(parts, "tensor"),
                middle,
                end_bias[layer],
                b_normed,
                b_factor,
                gains[layer, 1],
                grad,
            )
            got = swap_all(sent, "tensor")
            g_y = got
            out = got[:, share:].reshape(rows, width).astype(F32)
        else:
            pre, h_low = saved[layer][12:]
            g_f, parts = call(
                backward_kernel,
                [shape((rows, hidden), BF16), exchange],
                (layer, (2, 3)),
                g_m,
                pre,
                w_fc,
                w_proj,
            )
            end_pack, gm_sum, gf_sum = end_grads(layer, h_low, g_m, b_low, g_f)
            grad, sums_b, sent = call(
                back_kernel,
                [row_block, two_rows, exchange],
                (layer, ()),
                swap_all(parts, "tensor"),
                b_normed,
                b_factor,
                gains[layer, 1],
                grad,
            )
            g_y = swap_all(sent, "tensor")
        grad_b = grad
        g_o, delta, sent = call(
            output_back_kernel,
            [shape((rows, local), BF16), shape((rows, local), F32), shape((ranks, rows + 16, local), BF16)],
            (layer, (1,)),
            g_y,
            w_out,
            o_full,
            logs,
            blocks={0: ((slots, share, width), lambda i: (0, 0, 0))},
        )
        if layer:
            sent, q_every = lax.optimization_barrier((sent, q_every))
        go_all = swap_all(sent, "dp")
        (g_q,) = call(
            query_back_kernel,
            [shape((rows, local), BF16)],
            (layer, ()),
            *spots,
            q_low,
            kv_all,
            g_o,
            logs,
            delta,
            room=24,
        )
        g_kv, parts = call(
            key_back_kernel,
            [shape((rows, 2 * local), BF16), exchange],
            (layer, (7,)),
            *spots,
            kv_own,
            q_every,
            go_all,
            g_q,
            w_three,
            room=24,
            blocks={4: ((total, local), lambda i: (0, layer))},
        )
        grad, sums_a, sent = call(
            back_kernel,
            [row_block, two_rows, exchange],
            (layer, ()),
            swap_all(parts, "tensor"),
            a_normed,
            a_factor,
            gains[layer, 0],
            grad,
        )
        sums = [sums_a, sums_b] + sums
        if layer:
            end_pack, gm_sum, gf_sum = end_grads(layer, h_low, g_m, b_low, g_f)
        attend_pack, gy_sum, gq_sum, gv_sum = call(
            attend_grads_kernel,
            [
                shape((4 * local, width), BF16),
                shape((1, width), F32),
                shape((1, local), F32),
                shape((1, local), F32),
            ],
            (layer, ()),
            o_low,
            g_y,
            a_low,
            g_q,
            g_kv,
            room=16,
            blocks={1: ((slots, share, width), lambda i: (0, 0, 0))},
        )
        smalls = [gy_sum, gm_sum, gq_sum, gv_sum, gf_sum] + smalls
        if layer:
            g_m = swap_all(sent, "tensor").reshape(rows, width)
            end_part = halve(halve(end_pack, CORE, go_all), DEPTH, grad)
            attend_part = halve(halve(attend_pack, CORE), DEPTH, g_m)
            done[layer] = sum_over_x((end_part, attend_part))
    tail = jnp.concatenate([sent, jnp.broadcast_to(jnp.concatenate(sums, 0).astype(BF16), (slots, 8, width))], 1)
    tail_got = got = swap_all(tail, "tensor")
    grad_input = got[:, :share].reshape(rows, width).astype(F32)
    norm_sums = jnp.sum(got[:, share:].astype(F32), 0)
    small = jnp.concatenate([norm_sums.reshape(-1)] + [part.reshape(-1) for part in smalls])
    each = small.size // (8 * ranks)
    wide = 4 * width
    packed = jnp.concatenate(
        (
            attend_pack.reshape(ranks, 4, 8, width).transpose(0, 2, 1, 3).reshape(ranks, 8, wide),
            jnp.pad(small.astype(BF16).reshape(ranks, 8, each), ((0, 0), (0, 0), (0, 128 - each))),
        ),
        2,
    )
    half = halve(packed, CORE)
    arrived = swap_chips(half)
    mine = jnp.sum(arrived.astype(F32), 0).astype(BF16)
    late = swap_chips(jnp.broadcast_to(mine, (ranks // 2,) + mine.shape))
    starts = [halve(halve(part, CORE, grad_b), DEPTH, g_o) for part in (end_pack[:hidden], end_pack[hidden:])]
    events = (g_kv, grad, half)
    end_parts = [part for turn, value in enumerate(starts) for part in finish_sums(value, turn, events)]
    end_last, attend_last = [rejoin(after(part, grad), DEPTH, None, half) for part in done[1]]
    side = side_of(CORE)
    sides = side.astype(jnp.int32).reshape(1)
    g_w_proj, g_w_fc = call(
        finish_end_kernel,
        [shape((layers, hidden, width), F32), shape((layers, width, hidden), F32)],
        (0, ()),
        sides,
        *end_parts,
        end_last,
        swap(end_last, CORE),
        room=40,
    )
    attend_got = swap(attend_last, CORE)
    late, attend_got, g_w_proj, g_w_fc = lax.optimization_barrier((late, attend_got, g_w_proj, g_w_fc))
    late_got = swap(late, CORE)
    g_w_out, g_w_qkv = call(
        finish_attend_kernel,
        [shape((layers, local, width), F32), shape((layers, 3, width, local), F32)],
        (0, ()),
        sides,
        late,
        late_got,
        attend_last,
        attend_got,
        room=24,
    )
    ours, theirs = late[:, :, wide : wide + each], late_got[:, :, wide : wide + each]
    small = jnp.concatenate((jnp.where(side, theirs, ours), jnp.where(side, ours, theirs)), 0)
    small = small.reshape(-1).astype(F32)
    norm_grads = small[: 8 * width].reshape(layers, 2, 2, width)
    per_layer = small[8 * width :].reshape(layers, -1)
    cut = 2 * width

    return (
        out,
        grad_input,
        norm_grads[:, :, 0],
        norm_grads[:, :, 1],
        g_w_qkv.transpose(0, 2, 1, 3),
        per_layer[:, cut : cut + 2 * local].reshape(layers, 2, local),
        g_w_out,
        per_layer[:, :width],
        g_w_fc,
        per_layer[:, cut + 2 * local :],
        g_w_proj,
        per_layer[:, width:cut],
    )


def solution(mesh):
    in_specs = (
        P("dp", None),
        P(),
        P(),
        P(),
        P(None, None, None, "tensor"),
        P(None, None, "tensor"),
        P(None, "tensor", None),
        P(),
        P(None, None, "tensor"),
        P(None, "tensor"),
        P(None, "tensor", None),
        P(),
        P("dp", None),
    )
    out_specs = (
        P("dp", None),
        P("dp", None),
        P(),
        P(),
        P(None, None, None, "tensor"),
        P(None, None, "tensor"),
        P(None, "tensor", None),
        P(),
        P(None, None, "tensor"),
        P(None, "tensor"),
        P(None, "tensor", None),
        P(),
    )
    return jax.shard_map(body, mesh=mesh, in_specs=in_specs, out_specs=out_specs, check_vma=False)
```

```python
import functools

import jax
import jax.numpy as jnp
from jax import lax
from jax.experimental import pallas as pl
from jax.experimental.pallas import tpu as pltpu
from jax.sharding import PartitionSpec as P

HD = 64
F32 = jnp.float32
BF16 = jnp.bfloat16
ROOT = 0.7978845608028654
CUBE = 0.044715


def dot(left, right):
    return jnp.dot(left, right, preferred_element_type=F32)


def dot_t(left, right):
    return lax.dot_general(left, right, (((1,), (1,)), ((), ())), preferred_element_type=F32)


def norm_parts(value):
    mean = jnp.mean(value, -1, keepdims=True)
    centered = value - mean
    spread = jnp.mean(centered * centered, -1, keepdims=True)
    factor = lax.rsqrt(spread + 1e-05)
    return centered * factor, factor


def tanh_part(value):
    return jnp.tanh(ROOT * (value + CUBE * value * value * value))


def gelu(value):
    return 0.5 * value * (1.0 + tanh_part(value))


def gelu_slope(value):
    bend = tanh_part(value)
    inner = ROOT * (1.0 + 3.0 * CUBE * value * value)
    return 0.5 * (1.0 + bend) + 0.5 * value * (1.0 - bend * bend) * inner


def call(kernel, outs, layered, *args, room=12, blocks={}):
    layer, wide = layered
    near = NEAR.get(kernel, ())
    args = [
        arg if index in near or arg.shape == (1,) else pltpu.with_memory_space_constraint(arg, pltpu.HBM)
        for index, arg in enumerate(args)
    ]

    def spec(index, arg):
        if arg.dtype == jnp.int32 and arg.shape == (1,):
            return pl.BlockSpec(memory_space=pltpu.SMEM)
        if index in blocks:
            return pl.BlockSpec(*blocks[index])
        if index in wide:
            rest = arg.shape[1:]
            return pl.BlockSpec((None,) + rest, lambda i: (layer,) + (0,) * len(rest))
        return pl.BlockSpec(arg.shape, lambda i: (0,) * arg.ndim)

    return pl.pallas_call(
        kernel,
        grid=(1,),
        in_specs=[spec(index, arg) for index, arg in enumerate(args)],
        out_specs=[pl.BlockSpec(out.shape, lambda i, n=len(out.shape): (0,) * n) for out in outs],
        out_shape=[pltpu.HBM(out.shape, out.dtype) for out in outs],
        cost_estimate=pl.CostEstimate(flops=1000, bytes_accessed=1000, transcendentals=0),
        compiler_params=pltpu.CompilerParams(vmem_limit_bytes=room * 1024 * 1024),
    )(*args)


def shape(dims, kind):
    return jax.ShapeDtypeStruct(dims, kind)


def project(a_low, w_ref, bias_ref, q_ref, kv_ref, all_ref):
    q_ref[...] = (dot(a_low, w_ref[0]) + bias_ref[0:1].astype(F32)).astype(BF16)
    k_low = dot(a_low, w_ref[1]).astype(BF16)
    v_low = (dot(a_low, w_ref[2]) + bias_ref[1:2].astype(F32)).astype(BF16)
    local = k_low.shape[1]
    kv_ref[:, :local] = k_low
    kv_ref[:, local:] = v_low
    for index in range(all_ref.shape[0]):
        all_ref[index, :, :local] = k_low
        all_ref[index, :, local:] = v_low


def first_kernel(x_ref, gain_ref, shift_ref, w_ref, bias_ref, a_ref, q_ref, kv_ref, all_ref):
    normed, _ = norm_parts(x_ref[...].astype(F32))
    a_low = (normed * gain_ref[...] + shift_ref[...]).astype(BF16)
    a_ref[...] = a_low
    project(a_low, w_ref, bias_ref, q_ref, kv_ref, all_ref)


def project_kernel(a_ref, w_ref, bias_ref, q_ref, kv_ref, all_ref):
    project(a_ref[...], w_ref, bias_ref, q_ref, kv_ref, all_ref)


def head_masks(rows, local):
    column = lax.broadcasted_iota(jnp.int32, (rows, local), 1)
    return [column < HD, column >= HD]


def only(mask, value):
    return jnp.where(mask, value.astype(F32), 0.0).astype(BF16)


def allowed_of(start_ref, own_ref, all_ref, own_is_query):
    own_spot = start_ref[0] + lax.broadcasted_iota(jnp.int32, own_ref.shape, 0)
    spots = lax.broadcasted_iota(jnp.int32, all_ref.shape, 1)
    order = spots <= own_spot if own_is_query else spots >= own_spot
    return (all_ref[...] == own_ref[...]) & order


def attend_kernel(start_ref, own_ref, all_ref, q_ref, kv_ref, w_ref, o_ref, low_ref, log_ref, part_ref):
    rows, local = q_ref.shape
    total = all_ref.shape[1]
    keys = kv_ref[:, :, :local].reshape(total, local)
    values = kv_ref[:, :, local:].reshape(total, local)
    allowed = allowed_of(start_ref, own_ref, all_ref, True)
    queries = q_ref[...].astype(F32) * HD ** (-0.5)
    masks = head_masks(rows, local)
    outs, logs = [], []
    for mask in masks:
        scores = jnp.where(allowed, dot_t(only(mask, queries), keys), -1e30)
        top = jnp.max(scores, -1, keepdims=True)
        expd = jnp.exp(scores - top)
        denom = jnp.sum(expd, -1, keepdims=True)
        outs.append(dot((expd * (1.0 / denom)).astype(BF16), values))
        logs.append(top + jnp.log(denom))
    attended = jnp.where(masks[0], outs[0], outs[1])
    o_low = attended.astype(BF16)
    o_ref[...] = attended
    low_ref[...] = o_low
    log_ref[...] = jnp.where(masks[0], logs[0], logs[1])
    part_ref[...] = dot(o_low, w_ref[...]).astype(BF16).reshape(part_ref.shape)


def sum_parts(ref, start, rows):
    total = ref[0, start : start + rows].astype(F32)
    for index in range(1, ref.shape[0]):
        total = total + ref[index, start : start + rows].astype(F32)
    return total


def row_kernel(parts_ref, state_ref, bias_ref, gain_ref, shift_ref, state_out, normed_ref, factor_ref, sent_ref):
    state = state_ref[...] + (sum_parts(parts_ref, 0, state_ref.shape[0]) + bias_ref[...])
    normed, factor = norm_parts(state)
    low = (normed * gain_ref[...] + shift_ref[...]).astype(BF16)
    state_out[...] = state
    normed_ref[...] = normed
    factor_ref[...] = jnp.broadcast_to(factor, factor_ref.shape)
    for index in range(sent_ref.shape[0]):
        sent_ref[index] = low


def forward_kernel(b_ref, fc_ref, bias_ref, proj_ref, pre_ref, h_ref, part_ref):
    pre = dot(b_ref[...], fc_ref[...]) + bias_ref[...].astype(F32)
    h_low = gelu(pre).astype(BF16)
    pre_ref[...] = pre
    h_ref[...] = h_low
    part_ref[...] = dot(h_low, proj_ref[...]).astype(BF16).reshape(part_ref.shape)


def turn_kernel(b_ref, fc_ref, bias_ref, proj_ref, g_ref, h_ref, gf_ref, part_ref):
    share = part_ref.shape[1] // 2
    pre = dot(b_ref[...], fc_ref[...]) + bias_ref[...].astype(F32)
    h_low = gelu(pre).astype(BF16)
    h_ref[...] = h_low
    parts = dot(h_low, proj_ref[...]).astype(BF16)
    part_ref[:, :share] = parts.reshape(-1, share, parts.shape[1])
    g_f = (dot_t(g_ref[...], proj_ref[...]) * gelu_slope(pre)).astype(BF16)
    gf_ref[...] = g_f
    parts = dot_t(g_f, fc_ref[...]).astype(BF16)
    part_ref[:, share:] = parts.reshape(-1, share, parts.shape[1])


def backward_kernel(g_ref, pre_ref, fc_ref, proj_ref, gf_ref, part_ref):
    g_f = (dot_t(g_ref[...], proj_ref[...]) * gelu_slope(pre_ref[...])).astype(BF16)
    gf_ref[...] = g_f
    part_ref[...] = dot_t(g_f, fc_ref[...]).astype(BF16).reshape(part_ref.shape)


def norm_back(d_value, normed_ref, factor_ref, gain_ref, grad_ref, sums_ref):
    normed = normed_ref[...]
    scaled = d_value * gain_ref[...]
    back = factor_ref[:, 0:1] * (
        scaled
        - jnp.mean(scaled, -1, keepdims=True)
        - normed * jnp.mean(scaled * normed, -1, keepdims=True)
    )
    sums_ref[0:1] = jnp.sum(d_value * normed, 0, keepdims=True)
    sums_ref[1:2] = jnp.sum(d_value, 0, keepdims=True)
    return grad_ref[...] + back


def back_kernel(parts_ref, normed_ref, factor_ref, gain_ref, grad_ref, grad_out, sums_ref, sent_ref):
    share = normed_ref.shape[0]
    grad = norm_back(sum_parts(parts_ref, 0, share), normed_ref, factor_ref, gain_ref, grad_ref, sums_ref)
    grad_out[...] = grad
    low = grad.astype(BF16)
    for index in range(sent_ref.shape[0]):
        sent_ref[index] = low


def turn_back_kernel(
    parts_ref, state_ref, bias_ref, normed_ref, factor_ref, gain_ref, grad_ref, grad_out, sums_ref, sent_ref
):
    share = normed_ref.shape[0]
    out = (state_ref[...] + (sum_parts(parts_ref, 0, share) + bias_ref[...])).astype(BF16)
    grad = norm_back(sum_parts(parts_ref, share, share), normed_ref, factor_ref, gain_ref, grad_ref, sums_ref)
    grad_out[...] = grad
    low = grad.astype(BF16)
    for index in range(sent_ref.shape[0]):
        sent_ref[index, :share] = low
        sent_ref[index, share:] = out


def two_terms(value):
    high = value.astype(BF16).astype(F32)
    return high, value - high


def output_back_kernel(gy_ref, w_ref, o_ref, log_ref, go_ref, delta_ref, sent_ref):
    rows, local = o_ref.shape
    g_o = dot_t(gy_ref[...].reshape(rows, -1), w_ref[...]).astype(BF16)
    go_ref[...] = g_o
    masks = head_masks(rows, local)
    product = g_o.astype(F32) * o_ref[...]
    deltas = [jnp.sum(jnp.where(mask, product, 0.0), -1, keepdims=True) for mask in masks]
    delta = jnp.where(masks[0], deltas[0], deltas[1])
    delta_ref[...] = delta
    rows_of = []
    for value in (log_ref[...], delta):
        turned = value.T
        high, rest = two_terms(jnp.concatenate((turned[0:1], turned[HD : HD + 1]), 0))
        rows_of += [high, rest]
    rows_of.append(jnp.zeros((8, local), F32))
    extra = jnp.concatenate(rows_of, 0).astype(BF16)
    for index in range(sent_ref.shape[0]):
        sent_ref[index, :rows] = g_o
        sent_ref[index, rows:] = extra


def query_back_kernel(start_ref, own_ref, all_ref, q_ref, kv_ref, go_ref, log_ref, delta_ref, gq_ref):
    rows, local = q_ref.shape
    total = all_ref.shape[1]
    keys = kv_ref[:, :, :local].reshape(total, local)
    values = kv_ref[:, :, local:].reshape(total, local)
    allowed = allowed_of(start_ref, own_ref, all_ref, True)
    queries = q_ref[...].astype(F32) * HD ** (-0.5)
    masks = head_masks(rows, local)
    outs = []
    for head, mask in enumerate(masks):
        at = slice(head * HD, head * HD + 1)
        scores = jnp.where(allowed, dot_t(only(mask, queries), keys), -1e30)
        probs = jnp.exp(scores - log_ref[:, at])
        d_probs = dot_t(only(mask, go_ref[...]), values)
        g_s = (probs * (d_probs - delta_ref[:, at])).astype(BF16)
        outs.append(dot(g_s, keys))
    gq_ref[...] = (jnp.where(masks[0], outs[0], outs[1]) * HD ** (-0.5)).astype(BF16)


def key_back_kernel(start_ref, own_ref, all_ref, kv_ref, q_ref, got_ref, gq_ref, w_ref, gkv_ref, part_ref):
    rows, twice = kv_ref.shape
    local = twice // 2
    total = all_ref.shape[1]
    allowed = allowed_of(start_ref, own_ref, all_ref, False)
    queries = q_ref[...]
    g_o = got_ref[:, :rows].reshape(total, local)
    extra = got_ref[:, rows:].astype(F32)
    keys = kv_ref[:, :local].astype(F32) * HD ** (-0.5)
    values = kv_ref[:, local:]
    masks = head_masks(rows, local)
    d_keys, d_values = [], []
    for head, mask in enumerate(masks):

        def row_of(base):
            row = extra[:, base + head : base + head + 1] + extra[:, base + 2 + head : base + 3 + head]
            return jnp.concatenate([row[index] for index in range(row.shape[0])], 1)

        scores = jnp.where(allowed, dot_t(only(mask, keys), queries), -1e30)
        probs = jnp.exp(scores - row_of(0))
        d_probs = dot_t(only(mask, values), g_o)
        g_s = (probs * (d_probs - row_of(4))).astype(BF16)
        d_keys.append(dot(g_s, queries))
        d_values.append(dot(probs.astype(BF16), g_o))
    g_k = (jnp.where(masks[0], d_keys[0], d_keys[1]) * HD ** (-0.5)).astype(BF16)
    g_v = jnp.where(masks[0], d_values[0], d_values[1]).astype(BF16)
    gkv_ref[:, :local] = g_k
    gkv_ref[:, local:] = g_v
    part = dot_t(gq_ref[...], w_ref[0]) + dot_t(g_k, w_ref[1]) + dot_t(g_v, w_ref[2])
    part_ref[...] = part.astype(BF16).reshape(part_ref.shape)


def end_grads_kernel(h_ref, gm_ref, b_ref, gf_ref, pack_ref, gm_sum, gf_sum):
    g_m, g_f = gm_ref[...], gf_ref[...]
    hidden = g_f.shape[1]
    pack_ref[:hidden] = cross(h_ref[...], g_m).astype(BF16)
    g_w_fc = cross(b_ref[...], g_f).astype(BF16)
    for block in range(g_w_fc.shape[0] // hidden):
        at = slice(block * hidden, (block + 1) * hidden)
        pack_ref[hidden:, at] = g_w_fc[at]
    gm_sum[...] = jnp.sum(g_m.astype(F32), 0, keepdims=True)
    gf_sum[...] = jnp.sum(g_f.astype(F32), 0, keepdims=True)


def attend_grads_kernel(o_ref, gy_ref, a_ref, gq_ref, gkv_ref, pack_ref, gy_sum, gq_sum, gv_sum):
    local = gq_ref.shape[1]
    g_y = gy_ref[...].reshape(-1, gy_ref.shape[-1])
    a_low = a_ref[...]
    g_q, g_k, g_v = gq_ref[...], gkv_ref[:, :local], gkv_ref[:, local:]
    pack_ref[:local] = cross(o_ref[...], g_y).astype(BF16)
    for index, grad in enumerate((g_q, g_k, g_v)):
        product = cross(a_low, grad).astype(BF16)
        for block in range(product.shape[0] // local):
            at = slice(block * local, (block + 1) * local)
            pack_ref[(index + 1) * local : (index + 2) * local, at] = product[at]
    gy_sum[...] = jnp.sum(g_y.astype(F32), 0, keepdims=True)
    gq_sum[...] = jnp.sum(g_q.astype(F32), 0, keepdims=True)
    gv_sum[...] = jnp.sum(g_v.astype(F32), 0, keepdims=True)


def finish_end_kernel(side_ref, p_own, p_got, f_own, f_got, own_ref, got_ref, proj_ref, fc_ref):
    side = side_ref[0]
    half = p_own.shape[0]
    hidden = fc_ref.shape[2]

    def pick(own, got, index):
        return jnp.where(side == index, own[...].astype(F32), got[...].astype(F32))

    for index in range(2):
        rows = slice(index * half, (index + 1) * half)
        proj_ref[0, rows] = pick(p_own, p_got, index)
        packed = pick(f_own, f_got, index)
        for block in range(fc_ref.shape[1] // hidden):
            at = block * hidden + index * half
            fc_ref[0, at : at + half] = packed[:, block * hidden : (block + 1) * hidden]
    proj_ref[1] = pick(own_ref, got_ref, 0)
    packed = pick(own_ref, got_ref, 1)
    for block in range(fc_ref.shape[1] // hidden):
        at = slice(block * hidden, (block + 1) * hidden)
        fc_ref[1, at] = packed[:, at]


def finish_attend_kernel(side_ref, late_own, late_got, own_ref, got_ref, out_ref, qkv_ref):
    side = side_ref[0]
    local, width = out_ref.shape[1:]

    def put(layer, row, value):
        count = value.shape[0]
        if row < local:
            out_ref[layer, row : row + count] = value
        else:
            index, at = row // local - 1, row % local
            for block in range(width // local):
                base = block * local + at
                qkv_ref[layer, index, base : base + count] = value[:, block * local : (block + 1) * local]

    half = own_ref.shape[0]
    for index in range(2):
        picked = jnp.where(side == index, own_ref[...].astype(F32), got_ref[...].astype(F32))
        for row in range(0, half, local):
            put(1, index * half + row, picked[row : row + local])
        for chip in range(late_own.shape[0]):
            picked = jnp.where(side == index, late_own[chip].astype(F32), late_got[chip].astype(F32))
            for group in range(4):
                row = index * half + chip * 32 + group * 8
                put(0, row, picked[:, group * width : (group + 1) * width])


NEAR = {
    project_kernel: (0,),
    attend_kernel: (4,),
    row_kernel: (0,),
    forward_kernel: (0,),
    turn_kernel: (0,),
    turn_back_kernel: (0,),
    back_kernel: (0,),
    backward_kernel: (0,),
    output_back_kernel: (0,),
    query_back_kernel: (4,),
    key_back_kernel: (5,),
    end_grads_kernel: (1, 2),
    attend_grads_kernel: (1, 2),
}


def swap_all(value, axis):
    return lax.all_to_all(value, axis, 0, 0)


def cross(left, right):
    return lax.dot_general(left, right, (((0,), (0,)), ((), ())), preferred_element_type=F32)


CORE, DEPTH = 1, 2


def side_of(flip):
    return (lax.axis_index("dp") // flip) % 2


def swap(value, flip):
    return lax.ppermute(value, "dp", [(i, i ^ flip) for i in range(lax.axis_size("dp"))])


def after(value, event):
    return lax.optimization_barrier((value, event))[0]


def halve(value, flip, event=None, side=None):
    halves = value.reshape((2, value.shape[0] // 2) + value.shape[1:])
    side = side_of(flip) if side is None else side
    mine = lax.dynamic_index_in_dim(halves, side, 0, keepdims=False)
    got = swap(lax.dynamic_index_in_dim(halves, 1 - side, 0, keepdims=False), flip)
    got = got if event is None else after(got, event)
    return (mine.astype(F32) + got.astype(F32)).astype(BF16)


def rejoin(value, flip, side=None, event=None):
    got = swap(value, flip)
    got = got if event is None else after(got, event)
    side = side_of(flip) if side is None else side
    return jnp.concatenate((jnp.where(side, got, value), jnp.where(side, value, got)), 0)


def finish_sums(value, turn, events):
    place = lax.axis_index("dp")
    x_low, x_high = (place // 4) % 2, place // 8
    steps = ((4, x_low ^ x_high), (12, x_high)) if turn else ((12, x_high), (4, x_low ^ x_high))
    for (flip, side), event in zip(steps, events):
        value = halve(value, flip, event, side)
    for flip, side in steps[::-1]:
        value = rejoin(value, flip, side)
    value = rejoin(value, DEPTH, None, events[-1])
    return value, swap(value, CORE)


def sum_over_x(values):
    groups = [[4 * x + rest for x in range(lax.axis_size("dp") // 4)] for rest in range(4)]
    return lax.psum(values, "dp", axis_index_groups=groups)


def swap_chips(value):
    groups = [[2 * chip + core for chip in range(lax.axis_size("dp") // 2)] for core in range(2)]
    return lax.all_to_all(value, "dp", 0, 0, axis_index_groups=groups)


def body(
    tokens,
    segment_ids,
    norm_gain,
    norm_bias,
    w_qkv,
    b_qv,
    w_out,
    b_out,
    w_fc,
    b_fc,
    w_proj,
    b_proj,
    cotangent,
):
    rows, width = tokens.shape
    total = segment_ids.shape[0]
    layers = w_qkv.shape[0]
    local = w_qkv.shape[3]
    hidden = w_fc.shape[2]
    ranks, slots = lax.axis_size("dp"), lax.axis_size("tensor")
    share = rows // slots
    first = (lax.axis_index("dp") * rows).astype(jnp.int32)
    own = lax.axis_index("tensor") * share
    start = first.reshape(1)
    seg_own = lax.dynamic_slice_in_dim(segment_ids, first, rows).reshape(rows, 1)
    seg_all = segment_ids.reshape(1, total)
    spots = (start, seg_own, seg_all)
    gains = norm_gain.astype(F32).reshape(layers, 2, 1, width)
    shifts = norm_bias.astype(F32).reshape(layers, 2, 1, width)
    out_bias = b_out.astype(F32).reshape(layers, 1, width)
    end_bias = b_proj.astype(F32).reshape(layers, 1, width)
    w_three = w_qkv.transpose(0, 2, 1, 3)
    fc_bias = b_fc.reshape(layers, 1, hidden)
    state = lax.dynamic_slice_in_dim(tokens, own, share).astype(F32)
    a_normed, a_factor = norm_parts(state)
    a_factor = jnp.broadcast_to(a_factor, (share, 128))
    row_block = shape((share, width), F32)
    row_stat = shape((share, 128), F32)
    exchange = shape((slots, share, width), BF16)
    saved = []
    qkv_shapes = [
        shape((rows, local), BF16),
        shape((rows, 2 * local), BF16),
        shape((ranks, rows, 2 * local), BF16),
    ]
    a_low = None
    for layer in range(layers):
        if layer:
            q_low, kv_own, kv_sent = call(project_kernel, qkv_shapes, (layer, (1, 2)), a_low, w_three, b_qv)
        else:
            a_low, q_low, kv_own, kv_sent = call(
                first_kernel,
                [shape((rows, width), BF16)] + qkv_shapes,
                (layer, (3, 4)),
                tokens,
                gains[0, 0],
                shifts[0, 0],
                w_three,
                b_qv,
            )
        kv_all = swap_all(kv_sent, "dp")
        o_full, o_low, logs, attn_parts = call(
            attend_kernel,
            [shape((rows, local), F32), shape((rows, local), BF16), shape((rows, local), F32), exchange],
            (layer, (5,)),
            *spots,
            q_low,
            kv_all,
            w_out,
            room=24,
        )
        middle, b_normed, b_factor, b_sent = call(
            row_kernel,
            [row_block, row_block, row_stat, exchange],
            (layer, ()),
            swap_all(attn_parts, "tensor"),
            state,
            out_bias[layer],
            gains[layer, 1],
            shifts[layer, 1],
        )
        b_low = swap_all(b_sent, "tensor").reshape(rows, width)
        kept = [a_normed, a_factor, a_low, q_low, kv_own, kv_all, o_full, o_low, logs, b_normed, b_factor, b_low]
        if layer < layers - 1:
            pre, h_low, parts = call(
                forward_kernel,
                [shape((rows, hidden), F32), shape((rows, hidden), BF16), exchange],
                (layer, (1, 2, 3)),
                b_low,
                w_fc,
                fc_bias,
                w_proj,
            )
            state, a_normed, a_factor, a_sent = call(
                row_kernel,
                [row_block, row_block, row_stat, exchange],
                (layer, ()),
                swap_all(parts, "tensor"),
                middle,
                end_bias[layer],
                gains[layer + 1, 0],
                shifts[layer + 1, 0],
            )
            a_low = swap_all(a_sent, "tensor").reshape(rows, width)
            kept += [pre, h_low]
        saved.append(kept)
    q_every = lax.all_gather(jnp.concatenate([kept[3] for kept in saved], 1), "dp", axis=0, tiled=True)
    g_m = cotangent
    grad = lax.dynamic_slice_in_dim(cotangent, own, share).astype(F32)
    done = [None] * layers
    smalls, sums = [], []
    two_rows = shape((2, width), F32)
    out = None
    def end_grads(layer, h_low, g_m, b_low, g_f):
        return call(
            end_grads_kernel,
            [shape((2 * hidden, width), BF16), shape((1, width), F32), shape((1, hidden), F32)],
            (layer, ()),
            h_low,
            g_m,
            b_low,
            g_f,
            room=16,
        )

    for layer in reversed(range(layers)):
        a_normed, a_factor, a_low, q_low, kv_own, kv_all, o_full, o_low, logs, b_normed, b_factor, b_low = (
            saved[layer][:12]
        )
        if layer == layers - 1:
            double = shape((slots, 2 * share, width), BF16)
            h_low, g_f, parts = call(
                turn_kernel,
                [shape((rows, hidden), BF16), shape((rows, hidden), BF16), double],
                (layer, (1, 2, 3)),
                b_low,
                w_fc,
                fc_bias,
                w_proj,
                g_m,
            )
            grad, sums_b, sent = call(
                turn_back_kernel,
                [row_block, two_rows, double],
                (layer, ()),
                swap_all(parts, "tensor"),
                middle,
                end_bias[layer],
                b_normed,
                b_factor,
                gains[layer, 1],
                grad,
            )
            got = swap_all(sent, "tensor")
            g_y = got
            out = got[:, share:].reshape(rows, width).astype(F32)
        else:
            pre, h_low = saved[layer][12:]
            g_f, parts = call(
                backward_kernel,
                [shape((rows, hidden), BF16), exchange],
                (layer, (2, 3)),
                g_m,
                pre,
                w_fc,
                w_proj,
            )
            end_pack, gm_sum, gf_sum = end_grads(layer, h_low, g_m, b_low, g_f)
            grad, sums_b, sent = call(
                back_kernel,
                [row_block, two_rows, exchange],
                (layer, ()),
                swap_all(parts, "tensor"),
                b_normed,
                b_factor,
                gains[layer, 1],
                grad,
            )
            g_y = swap_all(sent, "tensor")
        grad_b = grad
        g_o, delta, sent = call(
            output_back_kernel,
            [shape((rows, local), BF16), shape((rows, local), F32), shape((ranks, rows + 16, local), BF16)],
            (layer, (1,)),
            g_y,
            w_out,
            o_full,
            logs,
            blocks={0: ((slots, share, width), lambda i: (0, 0, 0))},
        )
        if layer:
            sent, q_every = lax.optimization_barrier((sent, q_every))
        go_all = swap_all(sent, "dp")
        (g_q,) = call(
            query_back_kernel,
            [shape((rows, local), BF16)],
            (layer, ()),
            *spots,
            q_low,
            kv_all,
            g_o,
            logs,
            delta,
            room=24,
        )
        g_kv, parts = call(
            key_back_kernel,
            [shape((rows, 2 * local), BF16), exchange],
            (layer, (7,)),
            *spots,
            kv_own,
            q_every,
            go_all,
            g_q,
            w_three,
            room=24,
            blocks={4: ((total, local), lambda i: (0, layer))},
        )
        grad, sums_a, sent = call(
            back_kernel,
            [row_block, two_rows, exchange],
            (layer, ()),
            swap_all(parts, "tensor"),
            a_normed,
            a_factor,
            gains[layer, 0],
            grad,
        )
        sums = [sums_a, sums_b] + sums
        if layer:
            end_pack, gm_sum, gf_sum = end_grads(layer, h_low, g_m, b_low, g_f)
        attend_pack, gy_sum, gq_sum, gv_sum = call(
            attend_grads_kernel,
            [
                shape((4 * local, width), BF16),
                shape((1, width), F32),
                shape((1, local), F32),
                shape((1, local), F32),
            ],
            (layer, ()),
            o_low,
            g_y,
            a_low,
            g_q,
            g_kv,
            room=16,
            blocks={1: ((slots, share, width), lambda i: (0, 0, 0))},
        )
        smalls = [gy_sum, gm_sum, gq_sum, gv_sum, gf_sum] + smalls
        if layer:
            g_m = swap_all(sent, "tensor").reshape(rows, width)
            end_part = halve(halve(end_pack, CORE, go_all), DEPTH, grad)
            attend_part = halve(halve(attend_pack, CORE), DEPTH, g_m)
            done[layer] = sum_over_x((end_part, attend_part))
    tail = jnp.concatenate([sent, jnp.broadcast_to(jnp.concatenate(sums, 0).astype(BF16), (slots, 8, width))], 1)
    tail_got = got = swap_all(tail, "tensor")
    grad_input = got[:, :share].reshape(rows, width).astype(F32)
    norm_sums = jnp.sum(got[:, share:].astype(F32), 0)
    small = jnp.concatenate([norm_sums.reshape(-1)] + [part.reshape(-1) for part in smalls])
    each = small.size // (8 * ranks)
    wide = 4 * width
    packed = jnp.concatenate(
        (
            attend_pack.reshape(ranks, 4, 8, width).transpose(0, 2, 1, 3).reshape(ranks, 8, wide),
            jnp.pad(small.astype(BF16).reshape(ranks, 8, each), ((0, 0), (0, 0), (0, 128 - each))),
        ),
        2,
    )
    half = halve(packed, CORE)
    arrived = swap_chips(half)
    mine = jnp.sum(arrived.astype(F32), 0).astype(BF16)
    late = swap_chips(jnp.broadcast_to(mine, (ranks // 2,) + mine.shape))
    starts = [halve(halve(part, CORE, grad_b), DEPTH, g_kv) for part in (end_pack[:hidden], end_pack[hidden:])]
    events = (grad, half, mine)
    end_parts = [part for turn, value in enumerate(starts) for part in finish_sums(value, turn, events)]
    end_last, attend_last = [rejoin(after(part, grad), DEPTH, None, half) for part in done[1]]
    side = side_of(CORE)
    sides = side.astype(jnp.int32).reshape(1)
    g_w_proj, g_w_fc = call(
        finish_end_kernel,
        [shape((layers, hidden, width), F32), shape((layers, width, hidden), F32)],
        (0, ()),
        sides,
        *end_parts,
        end_last,
        swap(end_last, CORE),
        room=40,
    )
    attend_got = swap(attend_last, CORE)
    late, attend_got = lax.optimization_barrier((late, attend_got))
    late_got = swap(late, CORE)
    g_w_out, g_w_qkv = call(
        finish_attend_kernel,
        [shape((layers, local, width), F32), shape((layers, 3, width, local), F32)],
        (0, ()),
        sides,
        late,
        late_got,
        attend_last,
        attend_got,
        room=24,
    )
    ours, theirs = late[:, :, wide : wide + each], late_got[:, :, wide : wide + each]
    small = jnp.concatenate((jnp.where(side, theirs, ours), jnp.where(side, ours, theirs)), 0)
    small = small.reshape(-1).astype(F32)
    norm_grads = small[: 8 * width].reshape(layers, 2, 2, width)
    per_layer = small[8 * width :].reshape(layers, -1)
    cut = 2 * width

    return (
        out,
        grad_input,
        norm_grads[:, :, 0],
        norm_grads[:, :, 1],
        g_w_qkv.transpose(0, 2, 1, 3),
        per_layer[:, cut : cut + 2 * local].reshape(layers, 2, local),
        g_w_out,
        per_layer[:, :width],
        g_w_fc,
        per_layer[:, cut + 2 * local :],
        g_w_proj,
        per_layer[:, width:cut],
    )


def solution(mesh):
    in_specs = (
        P("dp", None),
        P(),
        P(),
        P(),
        P(None, None, None, "tensor"),
        P(None, None, "tensor"),
        P(None, "tensor", None),
        P(),
        P(None, None, "tensor"),
        P(None, "tensor"),
        P(None, "tensor", None),
        P(),
        P("dp", None),
    )
    out_specs = (
        P("dp", None),
        P("dp", None),
        P(),
        P(),
        P(None, None, None, "tensor"),
        P(None, None, "tensor"),
        P(None, "tensor", None),
        P(),
        P(None, None, "tensor"),
        P(None, "tensor"),
        P(None, "tensor", None),
        P(),
    )
    return jax.shard_map(body, mesh=mesh, in_specs=in_specs, out_specs=out_specs, check_vma=False)
```

```python
import functools

import jax
import jax.numpy as jnp
from jax import lax
from jax.experimental import pallas as pl
from jax.experimental.pallas import tpu as pltpu
from jax.sharding import PartitionSpec as P

HD = 64
F32 = jnp.float32
BF16 = jnp.bfloat16
ROOT = 0.7978845608028654
CUBE = 0.044715


def dot(left, right):
    return jnp.dot(left, right, preferred_element_type=F32)


def dot_t(left, right):
    return lax.dot_general(left, right, (((1,), (1,)), ((), ())), preferred_element_type=F32)


def norm_parts(value):
    mean = jnp.mean(value, -1, keepdims=True)
    centered = value - mean
    spread = jnp.mean(centered * centered, -1, keepdims=True)
    factor = lax.rsqrt(spread + 1e-05)
    return centered * factor, factor


def tanh_part(value):
    return jnp.tanh(ROOT * (value + CUBE * value * value * value))


def gelu(value):
    return 0.5 * value * (1.0 + tanh_part(value))


def gelu_slope(value):
    bend = tanh_part(value)
    inner = ROOT * (1.0 + 3.0 * CUBE * value * value)
    return 0.5 * (1.0 + bend) + 0.5 * value * (1.0 - bend * bend) * inner


def call(kernel, outs, layered, *args, room=12, blocks={}):
    layer, wide = layered
    near = NEAR.get(kernel, ())
    args = [
        arg if index in near or arg.shape == (1,) else pltpu.with_memory_space_constraint(arg, pltpu.HBM)
        for index, arg in enumerate(args)
    ]

    def spec(index, arg):
        if arg.dtype == jnp.int32 and arg.shape == (1,):
            return pl.BlockSpec(memory_space=pltpu.SMEM)
        if index in blocks:
            return pl.BlockSpec(*blocks[index])
        if index in wide:
            rest = arg.shape[1:]
            return pl.BlockSpec((None,) + rest, lambda i: (layer,) + (0,) * len(rest))
        return pl.BlockSpec(arg.shape, lambda i: (0,) * arg.ndim)

    return pl.pallas_call(
        kernel,
        grid=(1,),
        in_specs=[spec(index, arg) for index, arg in enumerate(args)],
        out_specs=[pl.BlockSpec(out.shape, lambda i, n=len(out.shape): (0,) * n) for out in outs],
        out_shape=[pltpu.HBM(out.shape, out.dtype) for out in outs],
        cost_estimate=pl.CostEstimate(flops=1000, bytes_accessed=1000, transcendentals=0),
        compiler_params=pltpu.CompilerParams(vmem_limit_bytes=room * 1024 * 1024),
    )(*args)


def shape(dims, kind):
    return jax.ShapeDtypeStruct(dims, kind)


def project(a_low, w_ref, bias_ref, q_ref, kv_ref, all_ref):
    q_ref[...] = (dot(a_low, w_ref[0]) + bias_ref[0:1].astype(F32)).astype(BF16)
    k_low = dot(a_low, w_ref[1]).astype(BF16)
    v_low = (dot(a_low, w_ref[2]) + bias_ref[1:2].astype(F32)).astype(BF16)
    local = k_low.shape[1]
    kv_ref[:, :local] = k_low
    kv_ref[:, local:] = v_low
    for index in range(all_ref.shape[0]):
        all_ref[index, :, :local] = k_low
        all_ref[index, :, local:] = v_low


def first_kernel(x_ref, gain_ref, shift_ref, w_ref, bias_ref, a_ref, q_ref, kv_ref, all_ref):
    normed, _ = norm_parts(x_ref[...].astype(F32))
    a_low = (normed * gain_ref[...] + shift_ref[...]).astype(BF16)
    a_ref[...] = a_low
    project(a_low, w_ref, bias_ref, q_ref, kv_ref, all_ref)


def project_kernel(a_ref, w_ref, bias_ref, q_ref, kv_ref, all_ref):
    project(a_ref[...], w_ref, bias_ref, q_ref, kv_ref, all_ref)


def head_masks(rows, local):
    column = lax.broadcasted_iota(jnp.int32, (rows, local), 1)
    return [column < HD, column >= HD]


def only(mask, value):
    return jnp.where(mask, value.astype(F32), 0.0).astype(BF16)


def allowed_of(start_ref, own_ref, all_ref, own_is_query):
    own_spot = start_ref[0] + lax.broadcasted_iota(jnp.int32, own_ref.shape, 0)
    spots = lax.broadcasted_iota(jnp.int32, all_ref.shape, 1)
    order = spots <= own_spot if own_is_query else spots >= own_spot
    return (all_ref[...] == own_ref[...]) & order


def attend_kernel(start_ref, own_ref, all_ref, q_ref, kv_ref, w_ref, o_ref, low_ref, log_ref, part_ref):
    rows, local = q_ref.shape
    total = all_ref.shape[1]
    keys = kv_ref[:, :, :local].reshape(total, local)
    values = kv_ref[:, :, local:].reshape(total, local)
    allowed = allowed_of(start_ref, own_ref, all_ref, True)
    queries = q_ref[...].astype(F32) * HD ** (-0.5)
    masks = head_masks(rows, local)
    outs, logs = [], []
    for mask in masks:
        scores = jnp.where(allowed, dot_t(only(mask, queries), keys), -1e30)
        top = jnp.max(scores, -1, keepdims=True)
        expd = jnp.exp(scores - top)
        denom = jnp.sum(expd, -1, keepdims=True)
        outs.append(dot((expd * (1.0 / denom)).astype(BF16), values))
        logs.append(top + jnp.log(denom))
    attended = jnp.where(masks[0], outs[0], outs[1])
    o_low = attended.astype(BF16)
    o_ref[...] = attended
    low_ref[...] = o_low
    log_ref[...] = jnp.where(masks[0], logs[0], logs[1])
    part_ref[...] = dot(o_low, w_ref[...]).astype(BF16).reshape(part_ref.shape)


def sum_parts(ref, start, rows):
    total = ref[0, start : start + rows].astype(F32)
    for index in range(1, ref.shape[0]):
        total = total + ref[index, start : start + rows].astype(F32)
    return total


def row_kernel(parts_ref, state_ref, bias_ref, gain_ref, shift_ref, state_out, normed_ref, factor_ref, sent_ref):
    state = state_ref[...] + (sum_parts(parts_ref, 0, state_ref.shape[0]) + bias_ref[...])
    normed, factor = norm_parts(state)
    low = (normed * gain_ref[...] + shift_ref[...]).astype(BF16)
    state_out[...] = state
    normed_ref[...] = normed
    factor_ref[...] = jnp.broadcast_to(factor, factor_ref.shape)
    for index in range(sent_ref.shape[0]):
        sent_ref[index] = low


def forward_kernel(b_ref, fc_ref, bias_ref, proj_ref, pre_ref, h_ref, part_ref):
    pre = dot(b_ref[...], fc_ref[...]) + bias_ref[...].astype(F32)
    h_low = gelu(pre).astype(BF16)
    pre_ref[...] = pre
    h_ref[...] = h_low
    part_ref[...] = dot(h_low, proj_ref[...]).astype(BF16).reshape(part_ref.shape)


def turn_kernel(b_ref, fc_ref, bias_ref, proj_ref, g_ref, h_ref, gf_ref, part_ref):
    share = part_ref.shape[1] // 2
    pre = dot(b_ref[...], fc_ref[...]) + bias_ref[...].astype(F32)
    h_low = gelu(pre).astype(BF16)
    h_ref[...] = h_low
    parts = dot(h_low, proj_ref[...]).astype(BF16)
    part_ref[:, :share] = parts.reshape(-1, share, parts.shape[1])
    g_f = (dot_t(g_ref[...], proj_ref[...]) * gelu_slope(pre)).astype(BF16)
    gf_ref[...] = g_f
    parts = dot_t(g_f, fc_ref[...]).astype(BF16)
    part_ref[:, share:] = parts.reshape(-1, share, parts.shape[1])


def backward_kernel(g_ref, pre_ref, fc_ref, proj_ref, gf_ref, part_ref):
    g_f = (dot_t(g_ref[...], proj_ref[...]) * gelu_slope(pre_ref[...])).astype(BF16)
    gf_ref[...] = g_f
    part_ref[...] = dot_t(g_f, fc_ref[...]).astype(BF16).reshape(part_ref.shape)


def norm_back(d_value, normed_ref, factor_ref, gain_ref, grad_ref, sums_ref):
    normed = normed_ref[...]
    scaled = d_value * gain_ref[...]
    back = factor_ref[:, 0:1] * (
        scaled
        - jnp.mean(scaled, -1, keepdims=True)
        - normed * jnp.mean(scaled * normed, -1, keepdims=True)
    )
    sums_ref[0:1] = jnp.sum(d_value * normed, 0, keepdims=True)
    sums_ref[1:2] = jnp.sum(d_value, 0, keepdims=True)
    return grad_ref[...] + back


def back_kernel(parts_ref, normed_ref, factor_ref, gain_ref, grad_ref, grad_out, sums_ref, sent_ref):
    share = normed_ref.shape[0]
    grad = norm_back(sum_parts(parts_ref, 0, share), normed_ref, factor_ref, gain_ref, grad_ref, sums_ref)
    grad_out[...] = grad
    low = grad.astype(BF16)
    for index in range(sent_ref.shape[0]):
        sent_ref[index] = low


def turn_back_kernel(
    parts_ref, state_ref, bias_ref, normed_ref, factor_ref, gain_ref, grad_ref, grad_out, sums_ref, sent_ref
):
    share = normed_ref.shape[0]
    out = (state_ref[...] + (sum_parts(parts_ref, 0, share) + bias_ref[...])).astype(BF16)
    grad = norm_back(sum_parts(parts_ref, share, share), normed_ref, factor_ref, gain_ref, grad_ref, sums_ref)
    grad_out[...] = grad
    low = grad.astype(BF16)
    for index in range(sent_ref.shape[0]):
        sent_ref[index, :share] = low
        sent_ref[index, share:] = out


def two_terms(value):
    high = value.astype(BF16).astype(F32)
    return high, value - high


def output_back_kernel(gy_ref, w_ref, o_ref, log_ref, go_ref, delta_ref, sent_ref):
    rows, local = o_ref.shape
    g_o = dot_t(gy_ref[...].reshape(rows, -1), w_ref[...]).astype(BF16)
    go_ref[...] = g_o
    masks = head_masks(rows, local)
    product = g_o.astype(F32) * o_ref[...]
    deltas = [jnp.sum(jnp.where(mask, product, 0.0), -1, keepdims=True) for mask in masks]
    delta = jnp.where(masks[0], deltas[0], deltas[1])
    delta_ref[...] = delta
    rows_of = []
    for value in (log_ref[...], delta):
        turned = value.T
        high, rest = two_terms(jnp.concatenate((turned[0:1], turned[HD : HD + 1]), 0))
        rows_of += [high, rest]
    rows_of.append(jnp.zeros((8, local), F32))
    extra = jnp.concatenate(rows_of, 0).astype(BF16)
    for index in range(sent_ref.shape[0]):
        sent_ref[index, :rows] = g_o
        sent_ref[index, rows:] = extra


def query_back_kernel(start_ref, own_ref, all_ref, q_ref, kv_ref, go_ref, log_ref, delta_ref, gq_ref):
    rows, local = q_ref.shape
    total = all_ref.shape[1]
    keys = kv_ref[:, :, :local].reshape(total, local)
    values = kv_ref[:, :, local:].reshape(total, local)
    allowed = allowed_of(start_ref, own_ref, all_ref, True)
    queries = q_ref[...].astype(F32) * HD ** (-0.5)
    masks = head_masks(rows, local)
    outs = []
    for head, mask in enumerate(masks):
        at = slice(head * HD, head * HD + 1)
        scores = jnp.where(allowed, dot_t(only(mask, queries), keys), -1e30)
        probs = jnp.exp(scores - log_ref[:, at])
        d_probs = dot_t(only(mask, go_ref[...]), values)
        g_s = (probs * (d_probs - delta_ref[:, at])).astype(BF16)
        outs.append(dot(g_s, keys))
    gq_ref[...] = (jnp.where(masks[0], outs[0], outs[1]) * HD ** (-0.5)).astype(BF16)


def key_back_kernel(start_ref, own_ref, all_ref, kv_ref, q_ref, got_ref, gq_ref, w_ref, gkv_ref, part_ref):
    rows, twice = kv_ref.shape
    local = twice // 2
    total = all_ref.shape[1]
    allowed = allowed_of(start_ref, own_ref, all_ref, False)
    queries = q_ref[...]
    g_o = got_ref[:, :rows].reshape(total, local)
    extra = got_ref[:, rows:].astype(F32)
    keys = kv_ref[:, :local].astype(F32) * HD ** (-0.5)
    values = kv_ref[:, local:]
    masks = head_masks(rows, local)
    d_keys, d_values = [], []
    for head, mask in enumerate(masks):

        def row_of(base):
            row = extra[:, base + head : base + head + 1] + extra[:, base + 2 + head : base + 3 + head]
            return jnp.concatenate([row[index] for index in range(row.shape[0])], 1)

        scores = jnp.where(allowed, dot_t(only(mask, keys), queries), -1e30)
        probs = jnp.exp(scores - row_of(0))
        d_probs = dot_t(only(mask, values), g_o)
        g_s = (probs * (d_probs - row_of(4))).astype(BF16)
        d_keys.append(dot(g_s, queries))
        d_values.append(dot(probs.astype(BF16), g_o))
    g_k = (jnp.where(masks[0], d_keys[0], d_keys[1]) * HD ** (-0.5)).astype(BF16)
    g_v = jnp.where(masks[0], d_values[0], d_values[1]).astype(BF16)
    gkv_ref[:, :local] = g_k
    gkv_ref[:, local:] = g_v
    part = dot_t(gq_ref[...], w_ref[0]) + dot_t(g_k, w_ref[1]) + dot_t(g_v, w_ref[2])
    part_ref[...] = part.astype(BF16).reshape(part_ref.shape)


def end_grads_kernel(h_ref, gm_ref, b_ref, gf_ref, pack_ref, gm_sum, gf_sum):
    g_m, g_f = gm_ref[...], gf_ref[...]
    hidden = g_f.shape[1]
    pack_ref[:hidden] = cross(h_ref[...], g_m).astype(BF16)
    g_w_fc = cross(b_ref[...], g_f).astype(BF16)
    for block in range(g_w_fc.shape[0] // hidden):
        at = slice(block * hidden, (block + 1) * hidden)
        pack_ref[hidden:, at] = g_w_fc[at]
    gm_sum[...] = jnp.sum(g_m.astype(F32), 0, keepdims=True)
    gf_sum[...] = jnp.sum(g_f.astype(F32), 0, keepdims=True)


def attend_grads_kernel(o_ref, gy_ref, a_ref, gq_ref, gkv_ref, pack_ref, gy_sum, gq_sum, gv_sum):
    local = gq_ref.shape[1]
    g_y = gy_ref[...].reshape(-1, gy_ref.shape[-1])
    a_low = a_ref[...]
    g_q, g_k, g_v = gq_ref[...], gkv_ref[:, :local], gkv_ref[:, local:]
    pack_ref[:local] = cross(o_ref[...], g_y).astype(BF16)
    for index, grad in enumerate((g_q, g_k, g_v)):
        product = cross(a_low, grad).astype(BF16)
        for block in range(product.shape[0] // local):
            at = slice(block * local, (block + 1) * local)
            pack_ref[(index + 1) * local : (index + 2) * local, at] = product[at]
    gy_sum[...] = jnp.sum(g_y.astype(F32), 0, keepdims=True)
    gq_sum[...] = jnp.sum(g_q.astype(F32), 0, keepdims=True)
    gv_sum[...] = jnp.sum(g_v.astype(F32), 0, keepdims=True)


def finish_end_kernel(side_ref, p_own, p_got, f_own, f_got, own_ref, got_ref, proj_ref, fc_ref):
    side = side_ref[0]
    half = p_own.shape[0]
    hidden = fc_ref.shape[2]

    def pick(own, got, index):
        return jnp.where(side == index, own[...].astype(F32), got[...].astype(F32))

    for index in range(2):
        rows = slice(index * half, (index + 1) * half)
        proj_ref[0, rows] = pick(p_own, p_got, index)
        packed = pick(f_own, f_got, index)
        for block in range(fc_ref.shape[1] // hidden):
            at = block * hidden + index * half
            fc_ref[0, at : at + half] = packed[:, block * hidden : (block + 1) * hidden]
    proj_ref[1] = pick(own_ref, got_ref, 0)
    packed = pick(own_ref, got_ref, 1)
    for block in range(fc_ref.shape[1] // hidden):
        at = slice(block * hidden, (block + 1) * hidden)
        fc_ref[1, at] = packed[:, at]


def finish_attend_kernel(side_ref, late_own, late_got, own_ref, got_ref, out_ref, qkv_ref):
    side = side_ref[0]
    local, width = out_ref.shape[1:]

    def put(layer, row, value):
        count = value.shape[0]
        if row < local:
            out_ref[layer, row : row + count] = value
        else:
            index, at = row // local - 1, row % local
            for block in range(width // local):
                base = block * local + at
                qkv_ref[layer, index, base : base + count] = value[:, block * local : (block + 1) * local]

    half = own_ref.shape[0]
    for index in range(2):
        picked = jnp.where(side == index, own_ref[...].astype(F32), got_ref[...].astype(F32))
        for row in range(0, half, local):
            put(1, index * half + row, picked[row : row + local])
        for chip in range(late_own.shape[0]):
            picked = jnp.where(side == index, late_own[chip].astype(F32), late_got[chip].astype(F32))
            for group in range(4):
                row = index * half + chip * 32 + group * 8
                put(0, row, picked[:, group * width : (group + 1) * width])


NEAR = {
    project_kernel: (0,),
    attend_kernel: (4,),
    row_kernel: (0,),
    forward_kernel: (0,),
    turn_kernel: (0,),
    turn_back_kernel: (0,),
    back_kernel: (0,),
    backward_kernel: (0,),
    output_back_kernel: (0,),
    query_back_kernel: (4,),
    key_back_kernel: (5,),
    end_grads_kernel: (1, 2),
    attend_grads_kernel: (1, 2),
}


def swap_all(value, axis):
    return lax.all_to_all(value, axis, 0, 0)


def cross(left, right):
    return lax.dot_general(left, right, (((0,), (0,)), ((), ())), preferred_element_type=F32)


CORE, DEPTH = 1, 2


def side_of(flip):
    return (lax.axis_index("dp") // flip) % 2


def swap(value, flip):
    return lax.ppermute(value, "dp", [(i, i ^ flip) for i in range(lax.axis_size("dp"))])


def after(value, event):
    return lax.optimization_barrier((value, event))[0]


def halve(value, flip, event=None, side=None):
    halves = value.reshape((2, value.shape[0] // 2) + value.shape[1:])
    side = side_of(flip) if side is None else side
    mine = lax.dynamic_index_in_dim(halves, side, 0, keepdims=False)
    got = swap(lax.dynamic_index_in_dim(halves, 1 - side, 0, keepdims=False), flip)
    got = got if event is None else after(got, event)
    return (mine.astype(F32) + got.astype(F32)).astype(BF16)


def rejoin(value, flip, side=None, event=None):
    got = swap(value, flip)
    got = got if event is None else after(got, event)
    side = side_of(flip) if side is None else side
    return jnp.concatenate((jnp.where(side, got, value), jnp.where(side, value, got)), 0)


def finish_sums(value, turn, events):
    place = lax.axis_index("dp")
    x_low, x_high = (place // 4) % 2, place // 8
    steps = ((4, x_low ^ x_high), (12, x_high)) if turn else ((12, x_high), (4, x_low ^ x_high))
    for (flip, side), event in zip(steps, events):
        value = halve(value, flip, event, side)
    for (flip, side), event in zip(steps[::-1], (None, events[-1])):
        value = rejoin(value, flip, side, event)
    value = rejoin(value, DEPTH)
    return value, swap(value, CORE)


def sum_over_x(values):
    groups = [[4 * x + rest for x in range(lax.axis_size("dp") // 4)] for rest in range(4)]
    return lax.psum(values, "dp", axis_index_groups=groups)


def swap_chips(value):
    groups = [[2 * chip + core for chip in range(lax.axis_size("dp") // 2)] for core in range(2)]
    return lax.all_to_all(value, "dp", 0, 0, axis_index_groups=groups)


def body(
    tokens,
    segment_ids,
    norm_gain,
    norm_bias,
    w_qkv,
    b_qv,
    w_out,
    b_out,
    w_fc,
    b_fc,
    w_proj,
    b_proj,
    cotangent,
):
    rows, width = tokens.shape
    total = segment_ids.shape[0]
    layers = w_qkv.shape[0]
    local = w_qkv.shape[3]
    hidden = w_fc.shape[2]
    ranks, slots = lax.axis_size("dp"), lax.axis_size("tensor")
    share = rows // slots
    first = (lax.axis_index("dp") * rows).astype(jnp.int32)
    own = lax.axis_index("tensor") * share
    start = first.reshape(1)
    seg_own = lax.dynamic_slice_in_dim(segment_ids, first, rows).reshape(rows, 1)
    seg_all = segment_ids.reshape(1, total)
    spots = (start, seg_own, seg_all)
    gains = norm_gain.astype(F32).reshape(layers, 2, 1, width)
    shifts = norm_bias.astype(F32).reshape(layers, 2, 1, width)
    out_bias = b_out.astype(F32).reshape(layers, 1, width)
    end_bias = b_proj.astype(F32).reshape(layers, 1, width)
    w_three = w_qkv.transpose(0, 2, 1, 3)
    fc_bias = b_fc.reshape(layers, 1, hidden)
    state = lax.dynamic_slice_in_dim(tokens, own, share).astype(F32)
    a_normed, a_factor = norm_parts(state)
    a_factor = jnp.broadcast_to(a_factor, (share, 128))
    row_block = shape((share, width), F32)
    row_stat = shape((share, 128), F32)
    exchange = shape((slots, share, width), BF16)
    saved = []
    qkv_shapes = [
        shape((rows, local), BF16),
        shape((rows, 2 * local), BF16),
        shape((ranks, rows, 2 * local), BF16),
    ]
    a_low = None
    for layer in range(layers):
        if layer:
            q_low, kv_own, kv_sent = call(project_kernel, qkv_shapes, (layer, (1, 2)), a_low, w_three, b_qv)
        else:
            a_low, q_low, kv_own, kv_sent = call(
                first_kernel,
                [shape((rows, width), BF16)] + qkv_shapes,
                (layer, (3, 4)),
                tokens,
                gains[0, 0],
                shifts[0, 0],
                w_three,
                b_qv,
            )
        kv_all = swap_all(kv_sent, "dp")
        o_full, o_low, logs, attn_parts = call(
            attend_kernel,
            [shape((rows, local), F32), shape((rows, local), BF16), shape((rows, local), F32), exchange],
            (layer, (5,)),
            *spots,
            q_low,
            kv_all,
            w_out,
            room=24,
        )
        middle, b_normed, b_factor, b_sent = call(
            row_kernel,
            [row_block, row_block, row_stat, exchange],
            (layer, ()),
            swap_all(attn_parts, "tensor"),
            state,
            out_bias[layer],
            gains[layer, 1],
            shifts[layer, 1],
        )
        b_low = swap_all(b_sent, "tensor").reshape(rows, width)
        kept = [a_normed, a_factor, a_low, q_low, kv_own, kv_all, o_full, o_low, logs, b_normed, b_factor, b_low]
        if layer < layers - 1:
            pre, h_low, parts = call(
                forward_kernel,
                [shape((rows, hidden), F32), shape((rows, hidden), BF16), exchange],
                (layer, (1, 2, 3)),
                b_low,
                w_fc,
                fc_bias,
                w_proj,
            )
            state, a_normed, a_factor, a_sent = call(
                row_kernel,
                [row_block, row_block, row_stat, exchange],
                (layer, ()),
                swap_all(parts, "tensor"),
                middle,
                end_bias[layer],
                gains[layer + 1, 0],
                shifts[layer + 1, 0],
            )
            a_low = swap_all(a_sent, "tensor").reshape(rows, width)
            kept += [pre, h_low]
        saved.append(kept)
    q_every = lax.all_gather(jnp.concatenate([kept[3] for kept in saved], 1), "dp", axis=0, tiled=True)
    g_m = cotangent
    grad = lax.dynamic_slice_in_dim(cotangent, own, share).astype(F32)
    done = [None] * layers
    smalls, sums = [], []
    two_rows = shape((2, width), F32)
    out = None
    def end_grads(layer, h_low, g_m, b_low, g_f):
        return call(
            end_grads_kernel,
            [shape((2 * hidden, width), BF16), shape((1, width), F32), shape((1, hidden), F32)],
            (layer, ()),
            h_low,
            g_m,
            b_low,
            g_f,
            room=16,
        )

    for layer in reversed(range(layers)):
        a_normed, a_factor, a_low, q_low, kv_own, kv_all, o_full, o_low, logs, b_normed, b_factor, b_low = (
            saved[layer][:12]
        )
        if layer == layers - 1:
            double = shape((slots, 2 * share, width), BF16)
            h_low, g_f, parts = call(
                turn_kernel,
                [shape((rows, hidden), BF16), shape((rows, hidden), BF16), double],
                (layer, (1, 2, 3)),
                b_low,
                w_fc,
                fc_bias,
                w_proj,
                g_m,
            )
            grad, sums_b, sent = call(
                turn_back_kernel,
                [row_block, two_rows, double],
                (layer, ()),
                swap_all(parts, "tensor"),
                middle,
                end_bias[layer],
                b_normed,
                b_factor,
                gains[layer, 1],
                grad,
            )
            got = swap_all(sent, "tensor")
            g_y = got
            out = got[:, share:].reshape(rows, width).astype(F32)
        else:
            pre, h_low = saved[layer][12:]
            g_f, parts = call(
                backward_kernel,
                [shape((rows, hidden), BF16), exchange],
                (layer, (2, 3)),
                g_m,
                pre,
                w_fc,
                w_proj,
            )
            end_pack, gm_sum, gf_sum = end_grads(layer, h_low, g_m, b_low, g_f)
            grad, sums_b, sent = call(
                back_kernel,
                [row_block, two_rows, exchange],
                (layer, ()),
                swap_all(parts, "tensor"),
                b_normed,
                b_factor,
                gains[layer, 1],
                grad,
            )
            g_y = swap_all(sent, "tensor")
        grad_b = grad
        g_o, delta, sent = call(
            output_back_kernel,
            [shape((rows, local), BF16), shape((rows, local), F32), shape((ranks, rows + 16, local), BF16)],
            (layer, (1,)),
            g_y,
            w_out,
            o_full,
            logs,
            blocks={0: ((slots, share, width), lambda i: (0, 0, 0))},
        )
        if layer:
            sent, q_every = lax.optimization_barrier((sent, q_every))
        go_all = swap_all(sent, "dp")
        (g_q,) = call(
            query_back_kernel,
            [shape((rows, local), BF16)],
            (layer, ()),
            *spots,
            q_low,
            kv_all,
            g_o,
            logs,
            delta,
            room=24,
        )
        g_kv, parts = call(
            key_back_kernel,
            [shape((rows, 2 * local), BF16), exchange],
            (layer, (7,)),
            *spots,
            kv_own,
            q_every,
            go_all,
            g_q,
            w_three,
            room=24,
            blocks={4: ((total, local), lambda i: (0, layer))},
        )
        grad, sums_a, sent = call(
            back_kernel,
            [row_block, two_rows, exchange],
            (layer, ()),
            swap_all(parts, "tensor"),
            a_normed,
            a_factor,
            gains[layer, 0],
            grad,
        )
        sums = [sums_a, sums_b] + sums
        if layer:
            end_pack, gm_sum, gf_sum = end_grads(layer, h_low, g_m, b_low, g_f)
        attend_pack, gy_sum, gq_sum, gv_sum = call(
            attend_grads_kernel,
            [
                shape((4 * local, width), BF16),
                shape((1, width), F32),
                shape((1, local), F32),
                shape((1, local), F32),
            ],
            (layer, ()),
            o_low,
            g_y,
            a_low,
            g_q,
            g_kv,
            room=16,
            blocks={1: ((slots, share, width), lambda i: (0, 0, 0))},
        )
        smalls = [gy_sum, gm_sum, gq_sum, gv_sum, gf_sum] + smalls
        if layer:
            g_m = swap_all(sent, "tensor").reshape(rows, width)
            end_part = halve(halve(end_pack, CORE, go_all), DEPTH, grad)
            attend_part = halve(halve(attend_pack, CORE), DEPTH, g_m)
            done[layer] = sum_over_x((end_part, attend_part))
    tail = jnp.concatenate([sent, jnp.broadcast_to(jnp.concatenate(sums, 0).astype(BF16), (slots, 8, width))], 1)
    tail_got = got = swap_all(tail, "tensor")
    grad_input = got[:, :share].reshape(rows, width).astype(F32)
    norm_sums = jnp.sum(got[:, share:].astype(F32), 0)
    small = jnp.concatenate([norm_sums.reshape(-1)] + [part.reshape(-1) for part in smalls])
    each = small.size // (8 * ranks)
    wide = 4 * width
    packed = jnp.concatenate(
        (
            attend_pack.reshape(ranks, 4, 8, width).transpose(0, 2, 1, 3).reshape(ranks, 8, wide),
            jnp.pad(small.astype(BF16).reshape(ranks, 8, each), ((0, 0), (0, 0), (0, 128 - each))),
        ),
        2,
    )
    half = halve(packed, CORE)
    arrived = swap_chips(half)
    mine = jnp.sum(arrived.astype(F32), 0).astype(BF16)
    late = swap_chips(jnp.broadcast_to(mine, (ranks // 2,) + mine.shape))
    starts = [halve(halve(part, CORE, grad_b), DEPTH, g_kv) for part in (end_pack[:hidden], end_pack[hidden:])]
    events = (grad, half, mine)
    end_parts = [part for turn, value in enumerate(starts) for part in finish_sums(value, turn, events)]
    end_last, attend_last = [rejoin(after(part, grad), DEPTH, None, half) for part in done[1]]
    side = side_of(CORE)
    sides = side.astype(jnp.int32).reshape(1)
    g_w_proj, g_w_fc = call(
        finish_end_kernel,
        [shape((layers, hidden, width), F32), shape((layers, width, hidden), F32)],
        (0, ()),
        sides,
        *end_parts,
        end_last,
        swap(end_last, CORE),
        room=40,
    )
    attend_got = swap(attend_last, CORE)
    late, attend_got = lax.optimization_barrier((late, attend_got))
    late_got = swap(late, CORE)
    g_w_out, g_w_qkv = call(
        finish_attend_kernel,
        [shape((layers, local, width), F32), shape((layers, 3, width, local), F32)],
        (0, ()),
        sides,
        late,
        late_got,
        attend_last,
        attend_got,
        room=24,
    )
    ours, theirs = late[:, :, wide : wide + each], late_got[:, :, wide : wide + each]
    small = jnp.concatenate((jnp.where(side, theirs, ours), jnp.where(side, ours, theirs)), 0)
    small = small.reshape(-1).astype(F32)
    norm_grads = small[: 8 * width].reshape(layers, 2, 2, width)
    per_layer = small[8 * width :].reshape(layers, -1)
    cut = 2 * width

    return (
        out,
        grad_input,
        norm_grads[:, :, 0],
        norm_grads[:, :, 1],
        g_w_qkv.transpose(0, 2, 1, 3),
        per_layer[:, cut : cut + 2 * local].reshape(layers, 2, local),
        g_w_out,
        per_layer[:, :width],
        g_w_fc,
        per_layer[:, cut + 2 * local :],
        g_w_proj,
        per_layer[:, width:cut],
    )


def solution(mesh):
    in_specs = (
        P("dp", None),
        P(),
        P(),
        P(),
        P(None, None, None, "tensor"),
        P(None, None, "tensor"),
        P(None, "tensor", None),
        P(),
        P(None, None, "tensor"),
        P(None, "tensor"),
        P(None, "tensor", None),
        P(),
        P("dp", None),
    )
    out_specs = (
        P("dp", None),
        P("dp", None),
        P(),
        P(),
        P(None, None, None, "tensor"),
        P(None, None, "tensor"),
        P(None, "tensor", None),
        P(),
        P(None, None, "tensor"),
        P(None, "tensor"),
        P(None, "tensor", None),
        P(),
    )
    return jax.shard_map(body, mesh=mesh, in_specs=in_specs, out_specs=out_specs, check_vma=False)
```

```python
import functools

import jax
import jax.numpy as jnp
from jax import lax
from jax.experimental import pallas as pl
from jax.experimental.pallas import tpu as pltpu
from jax.sharding import PartitionSpec as P

HD = 64
F32 = jnp.float32
BF16 = jnp.bfloat16
ROOT = 0.7978845608028654
CUBE = 0.044715


def dot(left, right):
    return jnp.dot(left, right, preferred_element_type=F32)


def dot_t(left, right):
    return lax.dot_general(left, right, (((1,), (1,)), ((), ())), preferred_element_type=F32)


def norm_parts(value):
    mean = jnp.mean(value, -1, keepdims=True)
    centered = value - mean
    spread = jnp.mean(centered * centered, -1, keepdims=True)
    factor = lax.rsqrt(spread + 1e-05)
    return centered * factor, factor


def tanh_part(value):
    return jnp.tanh(ROOT * (value + CUBE * value * value * value))


def gelu(value):
    return 0.5 * value * (1.0 + tanh_part(value))


def gelu_slope(value):
    bend = tanh_part(value)
    inner = ROOT * (1.0 + 3.0 * CUBE * value * value)
    return 0.5 * (1.0 + bend) + 0.5 * value * (1.0 - bend * bend) * inner


def call(kernel, outs, layered, *args, room=12, blocks={}):
    layer, wide = layered
    near = NEAR.get(kernel, ())
    args = [
        arg if index in near or arg.shape == (1,) else pltpu.with_memory_space_constraint(arg, pltpu.HBM)
        for index, arg in enumerate(args)
    ]

    def spec(index, arg):
        if arg.dtype == jnp.int32 and arg.shape == (1,):
            return pl.BlockSpec(memory_space=pltpu.SMEM)
        if index in blocks:
            return pl.BlockSpec(*blocks[index])
        if index in wide:
            rest = arg.shape[1:]
            return pl.BlockSpec((None,) + rest, lambda i: (layer,) + (0,) * len(rest))
        return pl.BlockSpec(arg.shape, lambda i: (0,) * arg.ndim)

    return pl.pallas_call(
        kernel,
        grid=(1,),
        in_specs=[spec(index, arg) for index, arg in enumerate(args)],
        out_specs=[pl.BlockSpec(out.shape, lambda i, n=len(out.shape): (0,) * n) for out in outs],
        out_shape=[pltpu.HBM(out.shape, out.dtype) for out in outs],
        cost_estimate=pl.CostEstimate(flops=1000, bytes_accessed=1000, transcendentals=0),
        compiler_params=pltpu.CompilerParams(vmem_limit_bytes=room * 1024 * 1024),
    )(*args)


def shape(dims, kind):
    return jax.ShapeDtypeStruct(dims, kind)


def project(a_low, w_ref, bias_ref, q_ref, kv_ref, all_ref):
    q_ref[...] = (dot(a_low, w_ref[0]) + bias_ref[0:1].astype(F32)).astype(BF16)
    k_low = dot(a_low, w_ref[1]).astype(BF16)
    v_low = (dot(a_low, w_ref[2]) + bias_ref[1:2].astype(F32)).astype(BF16)
    local = k_low.shape[1]
    kv_ref[:, :local] = k_low
    kv_ref[:, local:] = v_low
    for index in range(all_ref.shape[0]):
        all_ref[index, :, :local] = k_low
        all_ref[index, :, local:] = v_low


def first_kernel(x_ref, gain_ref, shift_ref, w_ref, bias_ref, a_ref, q_ref, kv_ref, all_ref):
    normed, _ = norm_parts(x_ref[...].astype(F32))
    a_low = (normed * gain_ref[...] + shift_ref[...]).astype(BF16)
    a_ref[...] = a_low
    project(a_low, w_ref, bias_ref, q_ref, kv_ref, all_ref)


def project_kernel(a_ref, w_ref, bias_ref, q_ref, kv_ref, all_ref):
    project(a_ref[...], w_ref, bias_ref, q_ref, kv_ref, all_ref)


def head_masks(rows, local):
    column = lax.broadcasted_iota(jnp.int32, (rows, local), 1)
    return [column < HD, column >= HD]


def only(mask, value):
    return jnp.where(mask, value.astype(F32), 0.0).astype(BF16)


def allowed_of(start_ref, own_ref, all_ref, own_is_query):
    own_spot = start_ref[0] + lax.broadcasted_iota(jnp.int32, own_ref.shape, 0)
    spots = lax.broadcasted_iota(jnp.int32, all_ref.shape, 1)
    order = spots <= own_spot if own_is_query else spots >= own_spot
    return (all_ref[...] == own_ref[...]) & order


def attend_kernel(start_ref, own_ref, all_ref, q_ref, kv_ref, w_ref, o_ref, low_ref, log_ref, part_ref):
    rows, local = q_ref.shape
    total = all_ref.shape[1]
    keys = kv_ref[:, :, :local].reshape(total, local)
    values = kv_ref[:, :, local:].reshape(total, local)
    allowed = allowed_of(start_ref, own_ref, all_ref, True)
    queries = q_ref[...].astype(F32) * HD ** (-0.5)
    masks = head_masks(rows, local)
    outs, logs = [], []
    for mask in masks:
        scores = jnp.where(allowed, dot_t(only(mask, queries), keys), -1e30)
        top = jnp.max(scores, -1, keepdims=True)
        expd = jnp.exp(scores - top)
        denom = jnp.sum(expd, -1, keepdims=True)
        outs.append(dot((expd * (1.0 / denom)).astype(BF16), values))
        logs.append(top + jnp.log(denom))
    attended = jnp.where(masks[0], outs[0], outs[1])
    o_low = attended.astype(BF16)
    o_ref[...] = attended
    low_ref[...] = o_low
    log_ref[...] = jnp.where(masks[0], logs[0], logs[1])
    part_ref[...] = dot(o_low, w_ref[...]).astype(BF16).reshape(part_ref.shape)


def sum_parts(ref, start, rows):
    total = ref[0, start : start + rows].astype(F32)
    for index in range(1, ref.shape[0]):
        total = total + ref[index, start : start + rows].astype(F32)
    return total


def row_kernel(parts_ref, state_ref, bias_ref, gain_ref, shift_ref, state_out, normed_ref, factor_ref, sent_ref):
    state = state_ref[...] + (sum_parts(parts_ref, 0, state_ref.shape[0]) + bias_ref[...])
    normed, factor = norm_parts(state)
    low = (normed * gain_ref[...] + shift_ref[...]).astype(BF16)
    state_out[...] = state
    normed_ref[...] = normed
    factor_ref[...] = jnp.broadcast_to(factor, factor_ref.shape)
    for index in range(sent_ref.shape[0]):
        sent_ref[index] = low


def forward_kernel(b_ref, fc_ref, bias_ref, proj_ref, pre_ref, h_ref, part_ref):
    pre = dot(b_ref[...], fc_ref[...]) + bias_ref[...].astype(F32)
    h_low = gelu(pre).astype(BF16)
    pre_ref[...] = pre
    h_ref[...] = h_low
    part_ref[...] = dot(h_low, proj_ref[...]).astype(BF16).reshape(part_ref.shape)


def turn_kernel(b_ref, fc_ref, bias_ref, proj_ref, g_ref, h_ref, gf_ref, part_ref):
    share = part_ref.shape[1] // 2
    pre = dot(b_ref[...], fc_ref[...]) + bias_ref[...].astype(F32)
    h_low = gelu(pre).astype(BF16)
    h_ref[...] = h_low
    parts = dot(h_low, proj_ref[...]).astype(BF16)
    part_ref[:, :share] = parts.reshape(-1, share, parts.shape[1])
    g_f = (dot_t(g_ref[...], proj_ref[...]) * gelu_slope(pre)).astype(BF16)
    gf_ref[...] = g_f
    parts = dot_t(g_f, fc_ref[...]).astype(BF16)
    part_ref[:, share:] = parts.reshape(-1, share, parts.shape[1])


def backward_kernel(g_ref, pre_ref, fc_ref, proj_ref, gf_ref, part_ref):
    g_f = (dot_t(g_ref[...], proj_ref[...]) * gelu_slope(pre_ref[...])).astype(BF16)
    gf_ref[...] = g_f
    part_ref[...] = dot_t(g_f, fc_ref[...]).astype(BF16).reshape(part_ref.shape)


def norm_back(d_value, normed_ref, factor_ref, gain_ref, grad_ref, sums_ref):
    normed = normed_ref[...]
    scaled = d_value * gain_ref[...]
    back = factor_ref[:, 0:1] * (
        scaled
        - jnp.mean(scaled, -1, keepdims=True)
        - normed * jnp.mean(scaled * normed, -1, keepdims=True)
    )
    sums_ref[0:1] = jnp.sum(d_value * normed, 0, keepdims=True)
    sums_ref[1:2] = jnp.sum(d_value, 0, keepdims=True)
    return grad_ref[...] + back


def back_kernel(parts_ref, normed_ref, factor_ref, gain_ref, grad_ref, grad_out, sums_ref, sent_ref):
    share = normed_ref.shape[0]
    grad = norm_back(sum_parts(parts_ref, 0, share), normed_ref, factor_ref, gain_ref, grad_ref, sums_ref)
    grad_out[...] = grad
    low = grad.astype(BF16)
    for index in range(sent_ref.shape[0]):
        sent_ref[index] = low


def turn_back_kernel(
    parts_ref, state_ref, bias_ref, normed_ref, factor_ref, gain_ref, grad_ref, grad_out, sums_ref, sent_ref
):
    share = normed_ref.shape[0]
    out = (state_ref[...] + (sum_parts(parts_ref, 0, share) + bias_ref[...])).astype(BF16)
    grad = norm_back(sum_parts(parts_ref, share, share), normed_ref, factor_ref, gain_ref, grad_ref, sums_ref)
    grad_out[...] = grad
    low = grad.astype(BF16)
    for index in range(sent_ref.shape[0]):
        sent_ref[index, :share] = low
        sent_ref[index, share:] = out


def two_terms(value):
    high = value.astype(BF16).astype(F32)
    return high, value - high


def output_back_kernel(gy_ref, w_ref, o_ref, log_ref, go_ref, delta_ref, sent_ref):
    rows, local = o_ref.shape
    g_o = dot_t(gy_ref[...].reshape(rows, -1), w_ref[...]).astype(BF16)
    go_ref[...] = g_o
    masks = head_masks(rows, local)
    product = g_o.astype(F32) * o_ref[...]
    deltas = [jnp.sum(jnp.where(mask, product, 0.0), -1, keepdims=True) for mask in masks]
    delta = jnp.where(masks[0], deltas[0], deltas[1])
    delta_ref[...] = delta
    rows_of = []
    for value in (log_ref[...], delta):
        turned = value.T
        high, rest = two_terms(jnp.concatenate((turned[0:1], turned[HD : HD + 1]), 0))
        rows_of += [high, rest]
    rows_of.append(jnp.zeros((8, local), F32))
    extra = jnp.concatenate(rows_of, 0).astype(BF16)
    for index in range(sent_ref.shape[0]):
        sent_ref[index, :rows] = g_o
        sent_ref[index, rows:] = extra


def query_back_kernel(start_ref, own_ref, all_ref, q_ref, kv_ref, go_ref, log_ref, delta_ref, gq_ref):
    rows, local = q_ref.shape
    total = all_ref.shape[1]
    keys = kv_ref[:, :, :local].reshape(total, local)
    values = kv_ref[:, :, local:].reshape(total, local)
    allowed = allowed_of(start_ref, own_ref, all_ref, True)
    queries = q_ref[...].astype(F32) * HD ** (-0.5)
    masks = head_masks(rows, local)
    outs = []
    for head, mask in enumerate(masks):
        at = slice(head * HD, head * HD + 1)
        scores = jnp.where(allowed, dot_t(only(mask, queries), keys), -1e30)
        probs = jnp.exp(scores - log_ref[:, at])
        d_probs = dot_t(only(mask, go_ref[...]), values)
        g_s = (probs * (d_probs - delta_ref[:, at])).astype(BF16)
        outs.append(dot(g_s, keys))
    gq_ref[...] = (jnp.where(masks[0], outs[0], outs[1]) * HD ** (-0.5)).astype(BF16)


def key_back_kernel(start_ref, own_ref, all_ref, kv_ref, q_ref, got_ref, gq_ref, w_ref, gkv_ref, part_ref):
    rows, twice = kv_ref.shape
    local = twice // 2
    total = all_ref.shape[1]
    allowed = allowed_of(start_ref, own_ref, all_ref, False)
    queries = q_ref[...]
    g_o = got_ref[:, :rows].reshape(total, local)
    extra = got_ref[:, rows:].astype(F32)
    keys = kv_ref[:, :local].astype(F32) * HD ** (-0.5)
    values = kv_ref[:, local:]
    masks = head_masks(rows, local)
    d_keys, d_values = [], []
    for head, mask in enumerate(masks):

        def row_of(base):
            row = extra[:, base + head : base + head + 1] + extra[:, base + 2 + head : base + 3 + head]
            return jnp.concatenate([row[index] for index in range(row.shape[0])], 1)

        scores = jnp.where(allowed, dot_t(only(mask, keys), queries), -1e30)
        probs = jnp.exp(scores - row_of(0))
        d_probs = dot_t(only(mask, values), g_o)
        g_s = (probs * (d_probs - row_of(4))).astype(BF16)
        d_keys.append(dot(g_s, queries))
        d_values.append(dot(probs.astype(BF16), g_o))
    g_k = (jnp.where(masks[0], d_keys[0], d_keys[1]) * HD ** (-0.5)).astype(BF16)
    g_v = jnp.where(masks[0], d_values[0], d_values[1]).astype(BF16)
    gkv_ref[:, :local] = g_k
    gkv_ref[:, local:] = g_v
    part = dot_t(gq_ref[...], w_ref[0]) + dot_t(g_k, w_ref[1]) + dot_t(g_v, w_ref[2])
    part_ref[...] = part.astype(BF16).reshape(part_ref.shape)


def end_grads_kernel(h_ref, gm_ref, b_ref, gf_ref, pack_ref, gm_sum, gf_sum):
    g_m, g_f = gm_ref[...], gf_ref[...]
    hidden = g_f.shape[1]
    pack_ref[:hidden] = cross(h_ref[...], g_m).astype(BF16)
    g_w_fc = cross(b_ref[...], g_f).astype(BF16)
    for block in range(g_w_fc.shape[0] // hidden):
        at = slice(block * hidden, (block + 1) * hidden)
        pack_ref[hidden:, at] = g_w_fc[at]
    gm_sum[...] = jnp.sum(g_m.astype(F32), 0, keepdims=True)
    gf_sum[...] = jnp.sum(g_f.astype(F32), 0, keepdims=True)


def attend_grads_kernel(o_ref, gy_ref, a_ref, gq_ref, gkv_ref, pack_ref, gy_sum, gq_sum, gv_sum):
    local = gq_ref.shape[1]
    g_y = gy_ref[...].reshape(-1, gy_ref.shape[-1])
    a_low = a_ref[...]
    g_q, g_k, g_v = gq_ref[...], gkv_ref[:, :local], gkv_ref[:, local:]
    pack_ref[:local] = cross(o_ref[...], g_y).astype(BF16)
    for index, grad in enumerate((g_q, g_k, g_v)):
        product = cross(a_low, grad).astype(BF16)
        for block in range(product.shape[0] // local):
            at = slice(block * local, (block + 1) * local)
            pack_ref[(index + 1) * local : (index + 2) * local, at] = product[at]
    gy_sum[...] = jnp.sum(g_y.astype(F32), 0, keepdims=True)
    gq_sum[...] = jnp.sum(g_q.astype(F32), 0, keepdims=True)
    gv_sum[...] = jnp.sum(g_v.astype(F32), 0, keepdims=True)


def finish_end_kernel(side_ref, p_own, p_got, f_own, f_got, own_ref, got_ref, proj_ref, fc_ref):
    side = side_ref[0]
    half = p_own.shape[0]
    hidden = fc_ref.shape[2]

    def pick(own, got, index):
        return jnp.where(side == index, own[...].astype(F32), got[...].astype(F32))

    for index in range(2):
        rows = slice(index * half, (index + 1) * half)
        proj_ref[0, rows] = pick(p_own, p_got, index)
        packed = pick(f_own, f_got, index)
        for block in range(fc_ref.shape[1] // hidden):
            at = block * hidden + index * half
            fc_ref[0, at : at + half] = packed[:, block * hidden : (block + 1) * hidden]
    proj_ref[1] = pick(own_ref, got_ref, 0)
    packed = pick(own_ref, got_ref, 1)
    for block in range(fc_ref.shape[1] // hidden):
        at = slice(block * hidden, (block + 1) * hidden)
        fc_ref[1, at] = packed[:, at]


def finish_attend_kernel(side_ref, late_own, late_got, own_ref, got_ref, out_ref, qkv_ref):
    side = side_ref[0]
    local, width = out_ref.shape[1:]

    def put(layer, row, value):
        count = value.shape[0]
        if row < local:
            out_ref[layer, row : row + count] = value
        else:
            index, at = row // local - 1, row % local
            for block in range(width // local):
                base = block * local + at
                qkv_ref[layer, index, base : base + count] = value[:, block * local : (block + 1) * local]

    half = own_ref.shape[0]
    for index in range(2):
        picked = jnp.where(side == index, own_ref[...].astype(F32), got_ref[...].astype(F32))
        for row in range(0, half, local):
            put(1, index * half + row, picked[row : row + local])
        for chip in range(late_own.shape[0]):
            picked = jnp.where(side == index, late_own[chip].astype(F32), late_got[chip].astype(F32))
            for group in range(4):
                row = index * half + chip * 32 + group * 8
                put(0, row, picked[:, group * width : (group + 1) * width])


NEAR = {
    project_kernel: (0,),
    attend_kernel: (4,),
    row_kernel: (0,),
    forward_kernel: (0,),
    turn_kernel: (0,),
    turn_back_kernel: (0,),
    back_kernel: (0,),
    backward_kernel: (0,),
    output_back_kernel: (0,),
    query_back_kernel: (4,),
    key_back_kernel: (5,),
    end_grads_kernel: (1, 2),
    attend_grads_kernel: (1, 2),
}


def swap_all(value, axis):
    return lax.all_to_all(value, axis, 0, 0)


def cross(left, right):
    return lax.dot_general(left, right, (((0,), (0,)), ((), ())), preferred_element_type=F32)


CORE, DEPTH = 1, 2


def side_of(flip):
    return (lax.axis_index("dp") // flip) % 2


def swap(value, flip):
    return lax.ppermute(value, "dp", [(i, i ^ flip) for i in range(lax.axis_size("dp"))])


def after(value, event):
    return lax.optimization_barrier((value, event))[0]


def halve(value, flip, event=None, side=None):
    halves = value.reshape((2, value.shape[0] // 2) + value.shape[1:])
    side = side_of(flip) if side is None else side
    mine = lax.dynamic_index_in_dim(halves, side, 0, keepdims=False)
    got = swap(lax.dynamic_index_in_dim(halves, 1 - side, 0, keepdims=False), flip)
    got = got if event is None else after(got, event)
    return (mine.astype(F32) + got.astype(F32)).astype(BF16)


def rejoin(value, flip, side=None, event=None):
    got = swap(value, flip)
    got = got if event is None else after(got, event)
    side = side_of(flip) if side is None else side
    return jnp.concatenate((jnp.where(side, got, value), jnp.where(side, value, got)), 0)


def finish_sums(value, turn, events):
    place = lax.axis_index("dp")
    x_low, x_high = (place // 4) % 2, place // 8
    steps = ((4, x_low ^ x_high), (12, x_high)) if turn else ((12, x_high), (4, x_low ^ x_high))
    for (flip, side), event in zip(steps, events):
        value = halve(value, flip, event, side)
    for (flip, side), event in zip(steps[::-1], (None, events[-1])):
        value = rejoin(value, flip, side, event)
    value = rejoin(value, DEPTH)
    return value, swap(value, CORE)


def sum_over_x(values):
    groups = [[4 * x + rest for x in range(lax.axis_size("dp") // 4)] for rest in range(4)]
    return lax.psum(values, "dp", axis_index_groups=groups)


def swap_chips(value):
    groups = [[2 * chip + core for chip in range(lax.axis_size("dp") // 2)] for core in range(2)]
    return lax.all_to_all(value, "dp", 0, 0, axis_index_groups=groups)


def body(
    tokens,
    segment_ids,
    norm_gain,
    norm_bias,
    w_qkv,
    b_qv,
    w_out,
    b_out,
    w_fc,
    b_fc,
    w_proj,
    b_proj,
    cotangent,
):
    rows, width = tokens.shape
    total = segment_ids.shape[0]
    layers = w_qkv.shape[0]
    local = w_qkv.shape[3]
    hidden = w_fc.shape[2]
    ranks, slots = lax.axis_size("dp"), lax.axis_size("tensor")
    share = rows // slots
    first = (lax.axis_index("dp") * rows).astype(jnp.int32)
    own = lax.axis_index("tensor") * share
    start = first.reshape(1)
    seg_own = lax.dynamic_slice_in_dim(segment_ids, first, rows).reshape(rows, 1)
    seg_all = segment_ids.reshape(1, total)
    spots = (start, seg_own, seg_all)
    gains = norm_gain.astype(F32).reshape(layers, 2, 1, width)
    shifts = norm_bias.astype(F32).reshape(layers, 2, 1, width)
    out_bias = b_out.astype(F32).reshape(layers, 1, width)
    end_bias = b_proj.astype(F32).reshape(layers, 1, width)
    w_three = w_qkv.transpose(0, 2, 1, 3)
    fc_bias = b_fc.reshape(layers, 1, hidden)
    state = lax.dynamic_slice_in_dim(tokens, own, share).astype(F32)
    a_normed, a_factor = norm_parts(state)
    a_factor = jnp.broadcast_to(a_factor, (share, 128))
    row_block = shape((share, width), F32)
    row_stat = shape((share, 128), F32)
    exchange = shape((slots, share, width), BF16)
    saved = []
    qkv_shapes = [
        shape((rows, local), BF16),
        shape((rows, 2 * local), BF16),
        shape((ranks, rows, 2 * local), BF16),
    ]
    a_low = None
    for layer in range(layers):
        if layer:
            q_low, kv_own, kv_sent = call(project_kernel, qkv_shapes, (layer, (1, 2)), a_low, w_three, b_qv)
        else:
            a_low, q_low, kv_own, kv_sent = call(
                first_kernel,
                [shape((rows, width), BF16)] + qkv_shapes,
                (layer, (3, 4)),
                tokens,
                gains[0, 0],
                shifts[0, 0],
                w_three,
                b_qv,
            )
        kv_all = swap_all(kv_sent, "dp")
        o_full, o_low, logs, attn_parts = call(
            attend_kernel,
            [shape((rows, local), F32), shape((rows, local), BF16), shape((rows, local), F32), exchange],
            (layer, (5,)),
            *spots,
            q_low,
            kv_all,
            w_out,
            room=24,
        )
        middle, b_normed, b_factor, b_sent = call(
            row_kernel,
            [row_block, row_block, row_stat, exchange],
            (layer, ()),
            swap_all(attn_parts, "tensor"),
            state,
            out_bias[layer],
            gains[layer, 1],
            shifts[layer, 1],
        )
        b_low = swap_all(b_sent, "tensor").reshape(rows, width)
        kept = [a_normed, a_factor, a_low, q_low, kv_own, kv_all, o_full, o_low, logs, b_normed, b_factor, b_low]
        if layer < layers - 1:
            pre, h_low, parts = call(
                forward_kernel,
                [shape((rows, hidden), F32), shape((rows, hidden), BF16), exchange],
                (layer, (1, 2, 3)),
                b_low,
                w_fc,
                fc_bias,
                w_proj,
            )
            state, a_normed, a_factor, a_sent = call(
                row_kernel,
                [row_block, row_block, row_stat, exchange],
                (layer, ()),
                swap_all(parts, "tensor"),
                middle,
                end_bias[layer],
                gains[layer + 1, 0],
                shifts[layer + 1, 0],
            )
            a_low = swap_all(a_sent, "tensor").reshape(rows, width)
            kept += [pre, h_low]
        saved.append(kept)
    q_every = lax.all_gather(jnp.concatenate([kept[3] for kept in saved], 1), "dp", axis=0, tiled=True)
    g_m = cotangent
    grad = lax.dynamic_slice_in_dim(cotangent, own, share).astype(F32)
    done = [None] * layers
    smalls, sums = [], []
    two_rows = shape((2, width), F32)
    out = None
    def end_grads(layer, h_low, g_m, b_low, g_f):
        return call(
            end_grads_kernel,
            [shape((2 * hidden, width), BF16), shape((1, width), F32), shape((1, hidden), F32)],
            (layer, ()),
            h_low,
            g_m,
            b_low,
            g_f,
            room=16,
        )

    for layer in reversed(range(layers)):
        a_normed, a_factor, a_low, q_low, kv_own, kv_all, o_full, o_low, logs, b_normed, b_factor, b_low = (
            saved[layer][:12]
        )
        if layer == layers - 1:
            double = shape((slots, 2 * share, width), BF16)
            h_low, g_f, parts = call(
                turn_kernel,
                [shape((rows, hidden), BF16), shape((rows, hidden), BF16), double],
                (layer, (1, 2, 3)),
                b_low,
                w_fc,
                fc_bias,
                w_proj,
                g_m,
            )
            grad, sums_b, sent = call(
                turn_back_kernel,
                [row_block, two_rows, double],
                (layer, ()),
                swap_all(parts, "tensor"),
                middle,
                end_bias[layer],
                b_normed,
                b_factor,
                gains[layer, 1],
                grad,
            )
            got = swap_all(sent, "tensor")
            g_y = got
            out = got[:, share:].reshape(rows, width).astype(F32)
        else:
            pre, h_low = saved[layer][12:]
            g_f, parts = call(
                backward_kernel,
                [shape((rows, hidden), BF16), exchange],
                (layer, (2, 3)),
                g_m,
                pre,
                w_fc,
                w_proj,
            )
            end_pack, gm_sum, gf_sum = end_grads(layer, h_low, g_m, b_low, g_f)
            grad, sums_b, sent = call(
                back_kernel,
                [row_block, two_rows, exchange],
                (layer, ()),
                swap_all(parts, "tensor"),
                b_normed,
                b_factor,
                gains[layer, 1],
                grad,
            )
            g_y = swap_all(sent, "tensor")
        grad_b = grad
        g_o, delta, sent = call(
            output_back_kernel,
            [shape((rows, local), BF16), shape((rows, local), F32), shape((ranks, rows + 16, local), BF16)],
            (layer, (1,)),
            g_y,
            w_out,
            o_full,
            logs,
            blocks={0: ((slots, share, width), lambda i: (0, 0, 0))},
        )
        if layer:
            sent, q_every = lax.optimization_barrier((sent, q_every))
        go_all = swap_all(sent, "dp")
        (g_q,) = call(
            query_back_kernel,
            [shape((rows, local), BF16)],
            (layer, ()),
            *spots,
            q_low,
            kv_all,
            g_o,
            logs,
            delta,
            room=24,
        )
        g_kv, parts = call(
            key_back_kernel,
            [shape((rows, 2 * local), BF16), exchange],
            (layer, (7,)),
            *spots,
            kv_own,
            q_every,
            go_all,
            g_q,
            w_three,
            room=24,
            blocks={4: ((total, local), lambda i: (0, layer))},
        )
        grad, sums_a, sent = call(
            back_kernel,
            [row_block, two_rows, exchange],
            (layer, ()),
            swap_all(parts, "tensor"),
            a_normed,
            a_factor,
            gains[layer, 0],
            grad,
        )
        sums = [sums_a, sums_b] + sums
        if layer:
            end_pack, gm_sum, gf_sum = end_grads(layer, h_low, g_m, b_low, g_f)
        attend_pack, gy_sum, gq_sum, gv_sum = call(
            attend_grads_kernel,
            [
                shape((4 * local, width), BF16),
                shape((1, width), F32),
                shape((1, local), F32),
                shape((1, local), F32),
            ],
            (layer, ()),
            o_low,
            g_y,
            a_low,
            g_q,
            g_kv,
            room=16,
            blocks={1: ((slots, share, width), lambda i: (0, 0, 0))},
        )
        smalls = [gy_sum, gm_sum, gq_sum, gv_sum, gf_sum] + smalls
        if layer:
            g_m = swap_all(sent, "tensor").reshape(rows, width)
            end_part = halve(halve(end_pack, CORE, go_all), DEPTH, grad)
            attend_part = halve(halve(attend_pack, CORE), DEPTH, g_m)
            done[layer] = sum_over_x((end_part, attend_part))
    tail = jnp.concatenate([sent, jnp.broadcast_to(jnp.concatenate(sums, 0).astype(BF16), (slots, 8, width))], 1)
    tail_got = got = swap_all(tail, "tensor")
    grad_input = got[:, :share].reshape(rows, width).astype(F32)
    norm_sums = jnp.sum(got[:, share:].astype(F32), 0)
    small = jnp.concatenate([norm_sums.reshape(-1)] + [part.reshape(-1) for part in smalls])
    each = small.size // (8 * ranks)
    wide = 4 * width
    packed = jnp.concatenate(
        (
            attend_pack.reshape(ranks, 4, 8, width).transpose(0, 2, 1, 3).reshape(ranks, 8, wide),
            jnp.pad(small.astype(BF16).reshape(ranks, 8, each), ((0, 0), (0, 0), (0, 128 - each))),
        ),
        2,
    )
    half = halve(packed, CORE)
    arrived = swap_chips(half)
    mine = jnp.sum(arrived.astype(F32), 0).astype(BF16)
    late = swap_chips(jnp.broadcast_to(mine, (ranks // 2,) + mine.shape))
    starts = [halve(halve(part, CORE, grad_b), DEPTH, g_kv) for part in (end_pack[:hidden], end_pack[hidden:])]
    events = (grad, half, mine)
    end_parts = [part for turn, value in enumerate(starts) for part in finish_sums(value, turn, events)]
    end_last = rejoin(after(done[1][0], grad), DEPTH, None, half)
    attend_last = rejoin(after(done[1][1], half), DEPTH)
    side = side_of(CORE)
    sides = side.astype(jnp.int32).reshape(1)
    g_w_proj, g_w_fc = call(
        finish_end_kernel,
        [shape((layers, hidden, width), F32), shape((layers, width, hidden), F32)],
        (0, ()),
        sides,
        *end_parts,
        end_last,
        swap(end_last, CORE),
        room=40,
    )
    attend_got = swap(attend_last, CORE)
    late, attend_got = lax.optimization_barrier((late, attend_got))
    late_got = swap(late, CORE)
    g_w_out, g_w_qkv = call(
        finish_attend_kernel,
        [shape((layers, local, width), F32), shape((layers, 3, width, local), F32)],
        (0, ()),
        sides,
        late,
        late_got,
        attend_last,
        attend_got,
        room=24,
    )
    ours, theirs = late[:, :, wide : wide + each], late_got[:, :, wide : wide + each]
    small = jnp.concatenate((jnp.where(side, theirs, ours), jnp.where(side, ours, theirs)), 0)
    small = small.reshape(-1).astype(F32)
    norm_grads = small[: 8 * width].reshape(layers, 2, 2, width)
    per_layer = small[8 * width :].reshape(layers, -1)
    cut = 2 * width

    return (
        out,
        grad_input,
        norm_grads[:, :, 0],
        norm_grads[:, :, 1],
        g_w_qkv.transpose(0, 2, 1, 3),
        per_layer[:, cut : cut + 2 * local].reshape(layers, 2, local),
        g_w_out,
        per_layer[:, :width],
        g_w_fc,
        per_layer[:, cut + 2 * local :],
        g_w_proj,
        per_layer[:, width:cut],
    )


def solution(mesh):
    in_specs = (
        P("dp", None),
        P(),
        P(),
        P(),
        P(None, None, None, "tensor"),
        P(None, None, "tensor"),
        P(None, "tensor", None),
        P(),
        P(None, None, "tensor"),
        P(None, "tensor"),
        P(None, "tensor", None),
        P(),
        P("dp", None),
    )
    out_specs = (
        P("dp", None),
        P("dp", None),
        P(),
        P(),
        P(None, None, None, "tensor"),
        P(None, None, "tensor"),
        P(None, "tensor", None),
        P(),
        P(None, None, "tensor"),
        P(None, "tensor"),
        P(None, "tensor", None),
        P(),
    )
    return jax.shard_map(body, mesh=mesh, in_specs=in_specs, out_specs=out_specs, check_vma=False)
```
